256 devices in a mesh: dp: 16 (over x, z_lo, core), ctx: 16 (over y, z_hi).
Axes of the slice: x: 4, y: 4, z: 8 (z_hi: 4, z_lo: 2; z = z_hi * 2 + z_lo), core: 2. Of those that a mesh axis runs over, the one named last changes fastest.
Arguments:
- tokens: bfloat16 [16, 16, 2, 96, 1024], P('dp', 'ctx'), may hold values from -48 to 48
- sweep_tiles: int32 [16, 4], P('dp'), may hold values from 1 to 16, 32 in all within a row
- weights: bfloat16 [4, 1024, 512], replicated
- cotangent: bfloat16 [16, 16, 2, 96, 1024], P('dp', 'ctx'), may hold values from -6 to 6
Outputs:
- attn_out: bfloat16 [16, 16, 2, 96, 1024], P('dp', 'ctx')
- input_grad: bfloat16 [16, 16, 2, 96, 1024], P('dp', 'ctx')
- weight_grads: bfloat16 [4, 1024, 512], P(None, 'ctx')
The draws below stay inside these ranges and needn't reach their ends.
Inputs may be any that keep to these rules, and one draw needn't show every extreme that they name: `sweep_tiles`: each row sums to 32 tiles and its largest entry is exactly 16.
All inputs are finite; a program needn't handle non-finite values.
Results may differ from the reference program's by a relative error of at most 0.035.
The reference program's roundings to bfloat16 on the way (of `queries`, `context`, `context_grad`, `score_grad`, `query_grad` and `key_grad`) count: a program that leaves them out, or rounds other values in their place, can miss the bound.
Values may be sent and summed in bfloat16 or wider, within the bound.
No kernel may reach another device: no remote copies, remote signals or barrier semaphores. Data moves between devices by JAX's collectives and lax.ppermute only.
A program may use at most 64 MiB of HBM per device.

```python
import math
import jax
import jax.numpy as jnp
import numpy as np
from jax import lax

D = 1024
HEADS = 8
HEAD = 64
SWEEPS = 4
SPAN = 96
HQ = 512
RANKS = 16
SEQS = 16


def draw_tokens(key, part):
    key = jax.random.fold_in(key, 11)
    first, second = jax.random.split(key, 2)
    shape = (SEQS, RANKS, 2, SPAN, D)
    base = jax.random.normal(first, shape, jnp.float32)
    scales = jnp.exp(jax.random.uniform(second, (SEQS, RANKS, 2, SPAN, 1), jnp.float32, 0.0, math.log(3.0)))
    base = base * scales
    return jnp.clip(base, -48.0, 48.0).astype(jnp.bfloat16)


def draw_weights(key, part):
    key = jax.random.fold_in(key, 23)
    first, second, third, fourth = jax.random.split(key, 4)
    w_query = jax.random.normal(first, (D, HQ), jnp.float32) * D ** (-0.5)
    w_key = jax.random.normal(second, (D, HQ), jnp.float32) * D ** (-0.5)
    w_value = jax.random.normal(third, (D, HQ), jnp.float32) * D ** (-0.5)
    w_output = jax.random.normal(fourth, (D, HQ), jnp.float32) * HQ ** (-0.5)
    return jnp.stack([w_query, w_key, w_value, w_output]).astype(jnp.bfloat16)


def raised(drawn, rng, source, target, parts, factor):
    def block_of(position):
        return (jnp.arange(drawn.shape[position]) // (drawn.shape[position] // parts)).reshape((-1,) + (1,) * (drawn.ndim - 1 - position))

    one_side = jax.random.permutation(rng, parts)[block_of(target)]
    second = (block_of(target) + parts // 2) % parts
    return jnp.where((block_of(source) == one_side) | (block_of(source) == second), factor * drawn, drawn)


def level_of(own_key, dims, shards, least, high):
    level, own = 1.0, jax.random.fold_in(own_key, 6)
    for position, blocks in shards:
        draws = jnp.exp(jax.random.uniform(jax.random.fold_in(own, position), (blocks,), jnp.float32, least / len(shards), high / len(shards)))
        level = level * jnp.repeat(draws, dims[position] // blocks).reshape([-1 if axis == position else 1 for axis in range(len(dims))])
    return level


def profile(number_of, total, reach, skew):
    portions = [(1 << 20) // math.isqrt(standing ** skew) + 1 for standing in range(2, number_of + 1)]
    rest, given = total - reach - (number_of - 1), [1] * (number_of - 1)
    while rest > 0:
        movable = [i for i in range(number_of - 1) if given[i] < reach]
        mass, remaining = sum([portions[i] for i in movable]), rest
        for i in movable:
            extra = min(reach - given[i], max(1, remaining * portions[i] // mass), rest)
            given[i] = given[i] + extra
            rest = rest - extra
    return np.array([reach] + given)


def ragged_sizes(stream_key, amount, total, limit, lean):
    if amount == 2:
        one = jax.random.randint(stream_key, (), max(1, total - limit), min(limit, total - 1) + 1)
        return jnp.stack([one, total - one])
    sizes = jnp.asarray(profile(amount, total, limit, lean), jnp.int32)
    twos = (amount - 1) // 2
    source_of, receiver = sizes[1:1 + 2 * twos:2], sizes[2:2 + 2 * twos:2]
    slack = jnp.minimum(source_of - 1, limit - receiver)
    shifted = jax.random.randint(jax.random.fold_in(stream_key, 1), (twos,), 0, 1 << 20) % (slack + 1)
    sizes = sizes.at[1:1 + 2 * twos:2].set(source_of - shifted).at[2:2 + 2 * twos:2].set(receiver + shifted)
    return sizes[jax.random.permutation(jax.random.fold_in(stream_key, 2), amount)]


def noise_with(own_key, extent, scale, bound, cuts, heavy, held_as=jnp.bfloat16):
    entries = scale * jax.random.normal(own_key, extent, jnp.float32)
    if cuts:
        entries = entries * level_of(own_key, extent, cuts, -0.22, 0.18)
    return jnp.clip(raised(entries, jax.random.fold_in(own_key, 3), *heavy), -bound, bound).astype(held_as)


def setup_inputs(seed: int = 0) -> dict:
    streams_of = jax.random.split(jax.random.key(seed), 5)
    return {
        "tokens": draw_tokens(jax.random.fold_in(streams_of[4], 71), 0),
        "sweep_tiles": jax.vmap(lambda own: ragged_sizes(own, SWEEPS, 2 * RANKS, RANKS, 2))(jax.random.split(streams_of[1], SEQS)).reshape((SEQS, SWEEPS)).astype(jnp.int32),
        "weights": draw_weights(jax.random.fold_in(streams_of[4], 71), 0),
        "cotangent": noise_with(streams_of[3], (SEQS, RANKS, 2, SPAN, D), 1.0, 6.0, ((0, 16), (1, 16)), (1, 4, 16, 2.0)),
    }


def rounded(values):
    return lax.optimization_barrier(values.astype(jnp.bfloat16)).astype(jnp.float32)


def token_positions(storage):
    owner = storage // (2 * SPAN)
    second = (storage // SPAN) % 2
    within = storage % SPAN
    segment = jnp.where(second == 0, owner, 2 * RANKS - 1 - owner)
    return (segment * SPAN + within).astype(jnp.int32)


def one_sequence(items, weights):
    block_tokens, tiles, block_upstream = items
    total_rows = 2 * RANKS * SPAN
    scale = HEAD ** -0.5
    inputs = block_tokens.reshape(total_rows, D)
    upstream = block_upstream.reshape(total_rows, D)
    bounds = (jnp.cumsum(tiles) * SPAN).astype(jnp.int32)
    places = token_positions(jnp.arange(total_rows, dtype=jnp.int32))
    sweeps = jnp.sum((places[:, None] >= bounds[None, :]).astype(jnp.int32), axis=1)
    allowed = (sweeps[:, None] == sweeps[None, :]) & (places[None, :] <= places[:, None])
    w_query, w_key, w_value, w_output = weights[0], weights[1], weights[2], weights[3]
    queries = jnp.dot(inputs, w_query, preferred_element_type=jnp.float32).astype(jnp.bfloat16)
    keys_all = jnp.dot(inputs, w_key, preferred_element_type=jnp.float32).astype(jnp.bfloat16)
    values_all = jnp.dot(inputs, w_value, preferred_element_type=jnp.float32).astype(jnp.bfloat16)
    query_heads = queries.reshape(total_rows, HEADS, HEAD).astype(jnp.float32)
    key_heads = keys_all.reshape(total_rows, HEADS, HEAD).astype(jnp.float32)
    value_heads = values_all.reshape(total_rows, HEADS, HEAD).astype(jnp.float32)
    scores = jnp.einsum("qhe,khe->hqk", query_heads, key_heads) * scale
    scores = jnp.where(allowed[None], scores, -jnp.inf)
    row_max = jnp.max(scores, axis=-1)
    expo = jnp.exp(scores - row_max[..., None])
    row_sum = jnp.sum(expo, axis=-1)
    log_total = row_max + jnp.log(row_sum)
    accum = jnp.einsum("hqk,khe->qhe", rounded(expo), value_heads)
    context = (accum / row_sum.T[:, :, None]).astype(jnp.bfloat16).reshape(total_rows, HEADS * HEAD)
    attn_out = jnp.dot(context, w_output.T, preferred_element_type=jnp.float32).astype(jnp.bfloat16)
    context_grad = jnp.dot(upstream, w_output, preferred_element_type=jnp.float32).astype(jnp.bfloat16)
    grad_heads = context_grad.reshape(total_rows, HEADS, HEAD).astype(jnp.float32)
    context_heads = context.reshape(total_rows, HEADS, HEAD).astype(jnp.float32)
    delta = jnp.einsum("qhe,qhe->hq", grad_heads, context_heads)
    probs = jnp.where(allowed[None], jnp.exp(scores - log_total[..., None]), 0.0)
    probs_low = rounded(probs)
    prob_grad = jnp.einsum("qhe,khe->hqk", grad_heads, value_heads)
    score_grad = rounded(probs * (prob_grad - delta[..., None]) * scale)
    query_grad = jnp.einsum("hqk,khe->qhe", score_grad, key_heads).astype(jnp.bfloat16).reshape(total_rows, HEADS * HEAD)
    grad_split = score_grad.reshape(HEADS, RANKS, 2 * SPAN, total_rows)
    prob_split = probs_low.reshape(HEADS, RANKS, 2 * SPAN, total_rows)
    query_split = query_heads.reshape(RANKS, 2 * SPAN, HEADS, HEAD)
    upstream_split = grad_heads.reshape(RANKS, 2 * SPAN, HEADS, HEAD)
    key_terms = rounded(jnp.einsum("hrqk,rqhe->rkhe", grad_split, query_split))
    key_grad = jnp.sum(key_terms, axis=0).astype(jnp.bfloat16).reshape(total_rows, HEADS * HEAD)
    value_terms = rounded(jnp.einsum("hrqk,rqhe->rkhe", prob_split, upstream_split))
    value_grad = jnp.sum(value_terms, axis=0).astype(jnp.bfloat16).reshape(total_rows, HEADS * HEAD)
    input_grad = jnp.dot(query_grad, w_query.T, preferred_element_type=jnp.float32)
    input_grad = input_grad + jnp.dot(key_grad, w_key.T, preferred_element_type=jnp.float32)
    input_grad = input_grad + jnp.dot(value_grad, w_value.T, preferred_element_type=jnp.float32)
    input_grad = input_grad.astype(jnp.bfloat16)
    grads = jnp.stack([
        jnp.dot(inputs.T, query_grad, preferred_element_type=jnp.float32),
        jnp.dot(inputs.T, key_grad, preferred_element_type=jnp.float32),
        jnp.dot(inputs.T, value_grad, preferred_element_type=jnp.float32),
        jnp.dot(upstream.T, context, preferred_element_type=jnp.float32)])
    return attn_out.reshape(block_tokens.shape), input_grad.reshape(block_tokens.shape), grads


def reference(tokens, sweep_tiles, weights, cotangent):
    attn_out, input_grad, grads = lax.map(lambda items: one_sequence(items, weights), (tokens, sweep_tiles, cotangent))
    factor = (2.0 * SEQS * RANKS * SPAN) ** -0.5
    weight_grads = (jnp.sum(grads, axis=0) * factor).astype(jnp.bfloat16)
    return attn_out, input_grad, weight_grads
```

```python
import functools

import jax
import jax.numpy as jnp
from jax import lax
from jax.experimental import pallas as pl
from jax.experimental.pallas import tpu as pltpu
from jax.sharding import PartitionSpec as P

D = 1024
HEADS = 8
HEAD = 64
HQ = HEADS * HEAD
SPAN = 96
RANKS = 16
TILES = 2 * RANKS
CHUNK = 256
KEY_ROWS = TILES * SPAN + CHUNK
NEGATIVE = -1e30
VMEM_LIMIT = 48 * 1024 * 1024

CORE_PAIRS = [[2 * i, 2 * i + 1] for i in range(8)]
CORE_SWAP = [(i, i ^ 1) for i in range(16)]
SAME_CORE = [[core + 2 * i for i in range(8)] for core in range(2)]
Y_LINES = [[z + 4 * y for y in range(4)] for z in range(4)]
Z_LINES = [[4 * y + z for z in range(4)] for y in range(4)]


def low_lanes(rows):
    return lax.broadcasted_iota(jnp.int32, (rows, 128), 1) < HEAD


def project_kernel(block_ref, tokens_ref, upstream_ref, weights_ref, out_ref):
    inputs = tokens_ref[...].reshape(2 * SPAN, D)
    upstream = upstream_ref[...].reshape(2 * SPAN, D)

    def product(rows, number):
        return jnp.dot(rows, weights_ref[number], preferred_element_type=jnp.float32)

    queries, keys, values = (product(inputs, number) for number in range(3))
    grads = product(upstream, 3)
    low = low_lanes(2 * SPAN)
    for half, (first, second) in enumerate(((queries, grads), (keys, values))):
        for pair in range(2):
            one = first[:, 128 * pair : 128 * pair + 128]
            two = second[:, 128 * pair : 128 * pair + 128]
            even = jnp.where(low, one, pltpu.roll(two, HEAD, 1)).astype(jnp.bfloat16)
            odd = jnp.where(low, pltpu.roll(one, HEAD, 1), two).astype(jnp.bfloat16)
            for sequence in range(2):
                rows = slice(SPAN * sequence, SPAN * sequence + SPAN)
                place = slice(SPAN * half, SPAN * half + SPAN)
                out_ref[sequence, 2 * pair, place, :] = even[rows]
                out_ref[sequence, 2 * pair + 1, place, :] = odd[rows]


def project(block, tokens_pair, upstream_pair, weights):
    tokens_spec = pl.BlockSpec((2, 1, SPAN, D), lambda j, block: (0, block[0], 0, 0))
    return pl.pallas_call(
        project_kernel,
        out_shape=jax.ShapeDtypeStruct((2, HEADS, 2 * SPAN, 128), jnp.bfloat16),
        grid_spec=pltpu.PrefetchScalarGridSpec(
            num_scalar_prefetch=1,
            grid=(2,),
            in_specs=[
                tokens_spec,
                tokens_spec,
                pl.BlockSpec((4, D, HQ // 2), lambda j, block: (0, 0, j)),
            ],
            out_specs=pl.BlockSpec((2, HEADS // 2, 2 * SPAN, 128), lambda j, block: (0, j, 0, 0)),
        ),
        compiler_params=pltpu.CompilerParams(vmem_limit_bytes=VMEM_LIMIT),
        name="project",
    )(block, tokens_pair, upstream_pair, weights)


def attend_kernel(
    core_ref, tiles_ref, own_ref, other_ref, out_ref, own_grad_ref, other_grad_ref,
    key_ref, grad_ref, score_ref, prob_grad_ref,
):
    core = core_ref[0]
    first = tiles_ref[0]
    second = first + tiles_ref[1]
    third = second + tiles_ref[2]
    grad_ref[...] = jnp.zeros_like(grad_ref)
    key_ref[TILES * SPAN :, :] = jnp.zeros((CHUNK, 128), jnp.bfloat16)

    def own_tile(rank):
        return jnp.where(rank % 2 == core, rank, TILES - 1 - rank)

    def tile_rows(tile):
        return pl.ds(pl.multiple_of(tile * SPAN, SPAN), SPAN)

    for rank in range(RANKS):
        tile = own_tile(rank)
        key_ref[tile_rows(tile), :] = own_ref[rank, SPAN:, :]
        key_ref[tile_rows(TILES - 1 - tile), :] = other_ref[rank]

    low = low_lanes(SPAN)
    scale = HEAD ** -0.5

    def attend(rank, tile, start, chunks):
        base = pl.multiple_of(start * SPAN, SPAN)
        packed = own_ref[rank, :SPAN, :]
        query_only = jnp.where(low, packed, jnp.zeros_like(packed))
        grad_only = jnp.where(low, jnp.zeros_like(packed), packed)
        left = jnp.concatenate([query_only, grad_only], axis=0)
        right = jnp.concatenate([grad_only, query_only], axis=0)

        def rows(j):
            return pl.ds(pl.multiple_of(base + CHUNK * j, 32), CHUNK)

        top = jnp.full((SPAN, 1), NEGATIVE, jnp.float32)
        for j in range(chunks):
            both = lax.dot_general(
                left, key_ref[rows(j), :], (((1,), (1,)), ((), ())),
                preferred_element_type=jnp.float32,
            )
            scores = both[:SPAN] * scale
            if j >= chunks - 2:
                gap = (tile - start) * SPAN - CHUNK * j
                ahead = lax.broadcasted_iota(jnp.int32, (SPAN, CHUNK), 1) - lax.broadcasted_iota(
                    jnp.int32, (SPAN, CHUNK), 0
                )
                scores = jnp.where(ahead <= gap, scores, NEGATIVE)
            place = slice(CHUNK * j, CHUNK * j + CHUNK)
            score_ref[:, place] = scores
            prob_grad_ref[:, place] = both[SPAN:]
            top = jnp.maximum(top, jnp.max(scores, axis=1, keepdims=True))
        total = jnp.zeros((SPAN, 1), jnp.float32)
        accum = jnp.zeros((SPAN, 128), jnp.float32)
        for j in range(chunks):
            place = slice(CHUNK * j, CHUNK * j + CHUNK)
            expo = jnp.exp(score_ref[:, place] - top)
            score_ref[:, place] = expo
            total = total + jnp.sum(expo, axis=1, keepdims=True)
            accum = accum + jnp.dot(
                expo.astype(jnp.bfloat16), key_ref[rows(j), :], preferred_element_type=jnp.float32
            )
        inverse = 1.0 / total
        context = (accum / total).astype(jnp.bfloat16)
        delta = jnp.sum(
            grad_only.astype(jnp.float32) * context.astype(jnp.float32), axis=1, keepdims=True
        )
        query_grad = jnp.zeros((SPAN, 128), jnp.float32)
        for j in range(chunks):
            place = slice(CHUNK * j, CHUNK * j + CHUNK)
            probs = score_ref[:, place] * inverse
            score_grad = (probs * (prob_grad_ref[:, place] - delta) * scale).astype(jnp.bfloat16)
            query_grad = query_grad + jnp.dot(
                score_grad, key_ref[rows(j), :], preferred_element_type=jnp.float32
            )
            stacked = jnp.concatenate([probs.astype(jnp.bfloat16), score_grad], axis=0)
            grad_ref[rows(j), :] += lax.dot_general(
                stacked, right, (((0,), (0,)), ((), ())), preferred_element_type=jnp.float32
            )
        out_ref[rank] = jnp.where(low, query_grad, context.astype(jnp.float32)).astype(jnp.bfloat16)

    def one_tile(rank, carry):
        tile = own_tile(rank)
        start = jnp.where(
            tile >= third, third, jnp.where(tile >= second, second, jnp.where(tile >= first, first, 0))
        )
        chunks = ((tile - start + 1) * SPAN + CHUNK - 1) // CHUNK
        for count in range(1, 7):
            @pl.when(chunks == count)
            def _():
                attend(rank, tile, start, count)
        return carry

    lax.fori_loop(0, RANKS, one_tile, 0)
    for rank in range(RANKS):
        tile = own_tile(rank)
        own_grad_ref[rank] = grad_ref[tile_rows(tile), :]
        other_grad_ref[rank] = grad_ref[tile_rows(TILES - 1 - tile), :].astype(jnp.bfloat16)


def attend(core, tiles, own, other):
    smem = pl.BlockSpec(memory_space=pltpu.SMEM)
    vmem = pl.BlockSpec(memory_space=pltpu.VMEM)
    block = (RANKS, SPAN, 128)
    return pl.pallas_call(
        attend_kernel,
        out_shape=(
            jax.ShapeDtypeStruct(block, jnp.bfloat16),
            jax.ShapeDtypeStruct(block, jnp.float32),
            jax.ShapeDtypeStruct(block, jnp.bfloat16),
        ),
        in_specs=[smem, smem, vmem, vmem],
        out_specs=(vmem, vmem, vmem),
        scratch_shapes=[
            pltpu.VMEM((KEY_ROWS, 128), jnp.bfloat16),
            pltpu.VMEM((KEY_ROWS, 128), jnp.float32),
            pltpu.VMEM((SPAN, 6 * CHUNK), jnp.float32),
            pltpu.VMEM((SPAN, 6 * CHUNK), jnp.float32),
        ],
        compiler_params=pltpu.CompilerParams(vmem_limit_bytes=VMEM_LIMIT),
        name="attend",
    )(core, tiles, own, other)


def weight_kernel(place_ref, grads_ref, tokens_ref, upstream_ref, out_ref, held_ref):
    core, odd = place_ref[0], place_ref[1]
    number, step = pl.program_id(0), pl.program_id(1)

    @pl.when(step == 0)
    def _():
        low = low_lanes(SPAN)
        for sequence in range(2):
            for block in range(2):
                holder = jnp.bitwise_xor(odd, block)
                first = (2 * sequence + block) * SPAN
                rows = pl.ds(pl.multiple_of(number * SPAN, SPAN), SPAN)
                for pair in range(HEADS // 2):
                    one = grads_ref[holder, sequence, 2 * pair, rows, :].astype(jnp.float32)
                    two = grads_ref[holder, sequence, 2 * pair + 1, rows, :].astype(jnp.float32)
                    lower = jnp.where(low, one, pltpu.roll(two, HEAD, 1))
                    upper = jnp.where(low, pltpu.roll(one, HEAD, 1), two)
                    held_ref[first : first + SPAN, 128 * pair : 128 * pair + 128] = jnp.where(
                        core == 0, lower, upper
                    ).astype(jnp.bfloat16)

    use_upstream = jnp.logical_and(core == 1, number == 0)
    left = jnp.where(use_upstream, upstream_ref[...], tokens_ref[...]).reshape(4 * SPAN, D // 4)
    result = lax.dot_general(
        left, held_ref[...], (((0,), (0,)), ((), ())), preferred_element_type=jnp.float32
    ).astype(jnp.bfloat16)
    for rank in range(4):
        for part in range(4):
            row = 64 * rank + 16 * part
            out_ref[part, rank] = result[row : row + 16]


def weight_terms(place, grads, tokens_pair, upstream_pair):
    tokens_spec = pl.BlockSpec((2, 2, SPAN, D // 4), lambda w, j, place: (0, 0, 0, j))
    return pl.pallas_call(
        weight_kernel,
        out_shape=jax.ShapeDtypeStruct((8, RANKS, 16, HQ), jnp.bfloat16),
        grid_spec=pltpu.PrefetchScalarGridSpec(
            num_scalar_prefetch=1,
            grid=(2, 4),
            in_specs=[
                pl.BlockSpec((2, 2, HEADS, 2 * SPAN, 128), lambda w, j, place: (0, 0, 0, 0, 0)),
                tokens_spec,
                tokens_spec,
            ],
            out_specs=pl.BlockSpec((4, 4, 16, HQ), lambda w, j, place: (w, j, 0, 0)),
            scratch_shapes=[pltpu.VMEM((4 * SPAN, HQ), jnp.bfloat16)],
        ),
        compiler_params=pltpu.CompilerParams(vmem_limit_bytes=VMEM_LIMIT),
        name="weight_terms",
    )(place, grads, tokens_pair, upstream_pair)


def output_kernel(place_ref, grads_ref, weights_ref, out_ref, input_grad_ref, held_ref):
    core, odd = place_ref[0], place_ref[1]

    @pl.when(pl.program_id(0) == 0)
    def _():
        low = low_lanes(SPAN)
        for block in range(2):
            holder = jnp.bitwise_xor(odd, block)
            rows = slice(SPAN * block, SPAN * block + SPAN)
            for half in range(2):
                place = slice(SPAN * half, SPAN * half + SPAN)
                for pair in range(HEADS // 2):
                    columns = slice(128 * pair, 128 * pair + 128)
                    one = grads_ref[holder, 0, 2 * pair, place, :].astype(jnp.float32)
                    two = grads_ref[holder, 0, 2 * pair + 1, place, :].astype(jnp.float32)
                    held_ref[2 * half, rows, columns] = jnp.where(
                        low, one, pltpu.roll(two, HEAD, 1)
                    ).astype(jnp.bfloat16)
                    held_ref[2 * half + 1, rows, columns] = jnp.where(
                        low, pltpu.roll(one, HEAD, 1), two
                    ).astype(jnp.bfloat16)

    def product(number, weight):
        return lax.dot_general(
            held_ref[number], weights_ref[weight], (((1,), (1,)), ((), ())),
            preferred_element_type=jnp.float32,
        )

    out_ref[...] = product(1, 3).astype(jnp.bfloat16).reshape(2, SPAN, D // 4)
    input_grad = product(0, 0) + product(2, 1) + product(3, 2)
    input_grad_ref[...] = input_grad.astype(jnp.bfloat16).reshape(2, SPAN, D // 4)


def outputs(place, grads, weights):
    shape = jax.ShapeDtypeStruct((2, SPAN, D), jnp.bfloat16)
    out_spec = pl.BlockSpec((2, SPAN, D // 4), lambda j, place: (0, 0, j))
    return pl.pallas_call(
        output_kernel,
        out_shape=(shape, shape),
        grid_spec=pltpu.PrefetchScalarGridSpec(
            num_scalar_prefetch=1,
            grid=(4,),
            in_specs=[
                pl.BlockSpec(
                    (2, 1, HEADS, 2 * SPAN, 128), lambda j, place: (0, place[0], 0, 0, 0)
                ),
                pl.BlockSpec((4, D // 4, HQ), lambda j, place: (0, j, 0)),
            ],
            out_specs=(out_spec, out_spec),
            scratch_shapes=[pltpu.VMEM((4, 2 * SPAN, HQ), jnp.bfloat16)],
        ),
        compiler_params=pltpu.CompilerParams(vmem_limit_bytes=VMEM_LIMIT),
        cost_estimate=pl.CostEstimate(
            flops=8 * 2 * SPAN * D * HQ, bytes_accessed=7 * 1024 * 1024, transcendentals=0
        ),
        name="outputs",
    )(place, grads, weights)


def per_device(tokens, sweep_tiles, weights, cotangent):
    core = lax.axis_index("dp") % 2
    rank = lax.axis_index("ctx")
    odd = rank % 2
    gather_pair = functools.partial(
        lax.all_gather, axis_name="dp", axis_index_groups=CORE_PAIRS, axis=0, tiled=True
    )
    tokens_pair = gather_pair(tokens.reshape(1, 2, SPAN, D))
    upstream_pair = gather_pair(cotangent.reshape(1, 2, SPAN, D))
    other_tiles = lax.ppermute(sweep_tiles, "dp", CORE_SWAP)
    block = jnp.bitwise_xor(core, odd).astype(jnp.int32).reshape(1)
    packed = project(block, tokens_pair, upstream_pair, weights).reshape(RANKS, 2 * SPAN, 128)
    own = lax.all_to_all(packed, "ctx", 0, 0)
    other = lax.ppermute(own[:, SPAN:], "dp", CORE_SWAP)
    tiles = jnp.where(rank // 8 == core, sweep_tiles, other_tiles).reshape(-1)
    query_part, own_grad, other_grad = attend(core.astype(jnp.int32).reshape(1), tiles, own, other)
    arrived = lax.ppermute(other_grad, "dp", CORE_SWAP)
    key_part = (own_grad + arrived.astype(jnp.float32)).astype(jnp.bfloat16)
    back = lax.all_to_all(jnp.concatenate([query_part, key_part], axis=1), "ctx", 0, 0)
    grads = gather_pair(back.reshape(1, 2, HEADS, 2 * SPAN, 128))
    place = jnp.stack([core, odd]).astype(jnp.int32)
    terms = weight_terms(place, grads, tokens_pair, upstream_pair)
    terms = lax.all_to_all(terms, "dp", 0, 0, axis_index_groups=SAME_CORE)
    attn_out, input_grad = outputs(place, grads, weights)

    def summed(parts):
        return jnp.sum(parts.astype(jnp.float32), axis=0)

    terms = summed(terms).astype(jnp.bfloat16).reshape(4, 4, 16, HQ)
    terms = lax.all_to_all(terms, "ctx", 0, 0, axis_index_groups=Y_LINES)
    terms = summed(terms).astype(jnp.bfloat16)
    terms = lax.all_to_all(terms, "ctx", 0, 0, axis_index_groups=Z_LINES)
    factor = float(16 * RANKS * 2 * SPAN) ** -0.5
    rows = (summed(terms) * factor).astype(jnp.bfloat16)
    spread = lax.all_to_all(jnp.broadcast_to(rows, (16, 16, HQ)), "dp", 0, 0)
    spread = spread.reshape(2, 4, 2, 16, HQ).transpose(2, 0, 1, 3, 4).reshape(4, 64, HQ)
    weight_grads = jnp.stack([spread[0], spread[1], spread[3], spread[2]])
    return (attn_out.reshape(tokens.shape), input_grad.reshape(tokens.shape), weight_grads)


def solution(mesh):
    placed = (
        P("dp", "ctx", None, None, None),
        P("dp", None),
        P(),
        P("dp", "ctx", None, None, None),
    )
    return jax.shard_map(
        per_device,
        mesh=mesh,
        in_specs=placed,
        out_specs=(
            P("dp", "ctx", None, None, None),
            P("dp", "ctx", None, None, None),
            P(None, "ctx", None),
        ),
        check_vma=False,
    )
```

```python
import functools

import jax
import jax.numpy as jnp
from jax import lax
from jax.experimental import pallas as pl
from jax.experimental.pallas import tpu as pltpu
from jax.sharding import PartitionSpec as P

D = 1024
HEADS = 8
HEAD = 64
HQ = HEADS * HEAD
SPAN = 96
RANKS = 16
TILES = 2 * RANKS
CHUNK = 256
KEY_ROWS = TILES * SPAN + CHUNK
NEGATIVE = -1e30
VMEM_LIMIT = 48 * 1024 * 1024

CORE_PAIRS = [[2 * i, 2 * i + 1] for i in range(8)]
CORE_SWAP = [(i, i ^ 1) for i in range(16)]
X_LINES = [[4 * x + 2 * z + core for x in range(4) for core in range(2)] for z in range(2)]
Z_SWAP = [(i, i ^ 2) for i in range(16)]


def low_lanes(rows):
    return lax.broadcasted_iota(jnp.int32, (rows, 128), 1) < HEAD


def project_kernel(block_ref, tokens_ref, upstream_ref, weights_ref, out_ref):
    inputs = tokens_ref[...].reshape(2 * SPAN, D)
    upstream = upstream_ref[...].reshape(2 * SPAN, D)

    def product(rows, number):
        return jnp.dot(rows, weights_ref[number], preferred_element_type=jnp.float32)

    queries, keys, values = (product(inputs, number) for number in range(3))
    grads = product(upstream, 3)
    low = low_lanes(2 * SPAN)
    for half, (first, second) in enumerate(((queries, grads), (keys, values))):
        for pair in range(2):
            one = first[:, 128 * pair : 128 * pair + 128]
            two = second[:, 128 * pair : 128 * pair + 128]
            even = jnp.where(low, one, pltpu.roll(two, HEAD, 1)).astype(jnp.bfloat16)
            odd = jnp.where(low, pltpu.roll(one, HEAD, 1), two).astype(jnp.bfloat16)
            for sequence in range(2):
                rows = slice(SPAN * sequence, SPAN * sequence + SPAN)
                place = slice(SPAN * half, SPAN * half + SPAN)
                out_ref[2 * pair, sequence, place, :] = even[rows]
                out_ref[2 * pair + 1, sequence, place, :] = odd[rows]


def project(block, tokens_pair, upstream_pair, weights):
    tokens_spec = pl.BlockSpec((2, 1, SPAN, D), lambda j, block: (0, block[0], 0, 0))
    return pl.pallas_call(
        project_kernel,
        out_shape=jax.ShapeDtypeStruct((HEADS, 2, 2 * SPAN, 128), jnp.bfloat16),
        grid_spec=pltpu.PrefetchScalarGridSpec(
            num_scalar_prefetch=1,
            grid=(2,),
            in_specs=[
                tokens_spec,
                tokens_spec,
                pl.BlockSpec((4, D, HQ // 2), lambda j, block: (0, 0, j)),
            ],
            out_specs=pl.BlockSpec((HEADS // 2, 2, 2 * SPAN, 128), lambda j, block: (j, 0, 0, 0)),
        ),
        compiler_params=pltpu.CompilerParams(vmem_limit_bytes=VMEM_LIMIT),
        name="project",
    )(block, tokens_pair, upstream_pair, weights)


def attend_kernel(
    core_ref, tiles_ref, own_ref, other_ref, out_ref, own_grad_ref, other_grad_ref,
    key_ref, grad_ref, score_ref, prob_grad_ref,
):
    core = core_ref[0]
    first = tiles_ref[0]
    second = first + tiles_ref[1]
    third = second + tiles_ref[2]
    grad_ref[...] = jnp.zeros_like(grad_ref)
    key_ref[TILES * SPAN :, :] = jnp.zeros((CHUNK, 128), jnp.bfloat16)

    def own_tile(rank):
        return jnp.where(rank % 2 == core, rank, TILES - 1 - rank)

    def tile_rows(tile):
        return pl.ds(pl.multiple_of(tile * SPAN, SPAN), SPAN)

    for rank in range(RANKS):
        tile = own_tile(rank)
        key_ref[tile_rows(tile), :] = own_ref[rank, SPAN:, :]
        key_ref[tile_rows(TILES - 1 - tile), :] = other_ref[rank]

    low = low_lanes(SPAN)
    scale = HEAD ** -0.5

    def attend(rank, tile, start, chunks):
        base = pl.multiple_of(start * SPAN, SPAN)
        packed = own_ref[rank, :SPAN, :]
        query_only = jnp.where(low, packed, jnp.zeros_like(packed))
        grad_only = jnp.where(low, jnp.zeros_like(packed), packed)
        left = jnp.concatenate([query_only, grad_only], axis=0)
        right = jnp.concatenate([grad_only, query_only], axis=0)

        def rows(j):
            return pl.ds(pl.multiple_of(base + CHUNK * j, 32), CHUNK)

        top = jnp.full((SPAN, 1), NEGATIVE, jnp.float32)
        for j in range(chunks):
            both = lax.dot_general(
                left, key_ref[rows(j), :], (((1,), (1,)), ((), ())),
                preferred_element_type=jnp.float32,
            )
            scores = both[:SPAN] * scale
            if j >= chunks - 2:
                gap = (tile - start) * SPAN - CHUNK * j
                ahead = lax.broadcasted_iota(jnp.int32, (SPAN, CHUNK), 1) - lax.broadcasted_iota(
                    jnp.int32, (SPAN, CHUNK), 0
                )
                scores = jnp.where(ahead <= gap, scores, NEGATIVE)
            place = slice(CHUNK * j, CHUNK * j + CHUNK)
            score_ref[:, place] = scores
            prob_grad_ref[:, place] = both[SPAN:]
            top = jnp.maximum(top, jnp.max(scores, axis=1, keepdims=True))
        total = jnp.zeros((SPAN, 1), jnp.float32)
        accum = jnp.zeros((SPAN, 128), jnp.float32)
        for j in range(chunks):
            place = slice(CHUNK * j, CHUNK * j + CHUNK)
            expo = jnp.exp(score_ref[:, place] - top)
            score_ref[:, place] = expo
            total = total + jnp.sum(expo, axis=1, keepdims=True)
            accum = accum + jnp.dot(
                expo.astype(jnp.bfloat16), key_ref[rows(j), :], preferred_element_type=jnp.float32
            )
        inverse = 1.0 / total
        context = (accum / total).astype(jnp.bfloat16)
        delta = jnp.sum(
            grad_only.astype(jnp.float32) * context.astype(jnp.float32), axis=1, keepdims=True
        )
        query_grad = jnp.zeros((SPAN, 128), jnp.float32)
        for j in range(chunks):
            place = slice(CHUNK * j, CHUNK * j + CHUNK)
            probs = score_ref[:, place] * inverse
            score_grad = (probs * (prob_grad_ref[:, place] - delta) * scale).astype(jnp.bfloat16)
            query_grad = query_grad + jnp.dot(
                score_grad, key_ref[rows(j), :], preferred_element_type=jnp.float32
            )
            stacked = jnp.concatenate([probs.astype(jnp.bfloat16), score_grad], axis=0)
            grad_ref[rows(j), :] += lax.dot_general(
                stacked, right, (((0,), (0,)), ((), ())), preferred_element_type=jnp.float32
            )
        out_ref[rank] = jnp.where(low, query_grad, context.astype(jnp.float32)).astype(jnp.bfloat16)

    def one_tile(rank, carry):
        tile = own_tile(rank)
        start = jnp.where(
            tile >= third, third, jnp.where(tile >= second, second, jnp.where(tile >= first, first, 0))
        )
        chunks = ((tile - start + 1) * SPAN + CHUNK - 1) // CHUNK
        for count in range(1, 7):
            @pl.when(chunks == count)
            def _():
                attend(rank, tile, start, count)
        return carry

    lax.fori_loop(0, RANKS, one_tile, 0)
    for rank in range(RANKS):
        tile = own_tile(rank)
        own_grad_ref[rank] = grad_ref[tile_rows(tile), :]
        other_grad_ref[rank] = grad_ref[tile_rows(TILES - 1 - tile), :].astype(jnp.bfloat16)


def attend(core, tiles, own, other):
    smem = pl.BlockSpec(memory_space=pltpu.SMEM)
    vmem = pl.BlockSpec(memory_space=pltpu.VMEM)
    block = (RANKS, SPAN, 128)
    return pl.pallas_call(
        attend_kernel,
        out_shape=(
            jax.ShapeDtypeStruct(block, jnp.bfloat16),
            jax.ShapeDtypeStruct(block, jnp.float32),
            jax.ShapeDtypeStruct(block, jnp.bfloat16),
        ),
        in_specs=[smem, smem, vmem, vmem],
        out_specs=(vmem, vmem, vmem),
        scratch_shapes=[
            pltpu.VMEM((KEY_ROWS, 128), jnp.bfloat16),
            pltpu.VMEM((KEY_ROWS, 128), jnp.float32),
            pltpu.VMEM((SPAN, 6 * CHUNK), jnp.float32),
            pltpu.VMEM((SPAN, 6 * CHUNK), jnp.float32),
        ],
        compiler_params=pltpu.CompilerParams(vmem_limit_bytes=VMEM_LIMIT),
        name="attend",
    )(core, tiles, own, other)


def weight_kernel(odd_ref, grads_ref, tokens_ref, upstream_ref, out_ref, held_ref):
    odd = odd_ref[0]

    @pl.when(pl.program_id(0) == 0)
    def _():
        for chip in range(4):
            for sequence in range(2):
                for block in range(2):
                    holder = 2 * chip + jnp.bitwise_xor(odd, block)
                    first = (4 * chip + 2 * sequence + block) * SPAN
                    for half in range(2):
                        held_ref[first : first + SPAN, 128 * half : 128 * half + 128] = grads_ref[
                            holder, sequence, SPAN * half : SPAN * half + SPAN, :
                        ]

    def product(rows_ref, columns):
        rows = rows_ref[...].reshape(16 * SPAN, D // 4)
        return lax.dot_general(
            rows, held_ref[:, :columns], (((0,), (0,)), ((), ())), preferred_element_type=jnp.float32
        )

    by_tokens = product(tokens_ref, 256)
    by_upstream = product(upstream_ref, 128)
    first = jnp.where(low_lanes(D // 4), by_tokens[:, :128], by_upstream)
    out_ref[:, :, :128] = first.astype(jnp.bfloat16).reshape(4, 64, 128)
    out_ref[:, :, 128:] = by_tokens[:, 128:].astype(jnp.bfloat16).reshape(4, 64, 128)


def weight_terms(odd, grads, tokens_line, upstream_line):
    tokens_spec = pl.BlockSpec((8, 2, SPAN, D // 4), lambda j, odd: (0, 0, 0, j))
    return pl.pallas_call(
        weight_kernel,
        out_shape=jax.ShapeDtypeStruct((RANKS, 64, 256), jnp.bfloat16),
        grid_spec=pltpu.PrefetchScalarGridSpec(
            num_scalar_prefetch=1,
            grid=(4,),
            in_specs=[
                pl.BlockSpec((8, 2, 2 * SPAN, 128), lambda j, odd: (0, 0, 0, 0)),
                tokens_spec,
                tokens_spec,
            ],
            out_specs=pl.BlockSpec((4, 64, 256), lambda j, odd: (j, 0, 0)),
            scratch_shapes=[pltpu.VMEM((16 * SPAN, 256), jnp.bfloat16)],
        ),
        compiler_params=pltpu.CompilerParams(vmem_limit_bytes=VMEM_LIMIT),
        name="weight_terms",
    )(odd, grads, tokens_line, upstream_line)


def spread_kernel(parts_ref, out_ref):
    low = low_lanes(64)
    for pair in range(HEADS // 2):
        columns = slice(128 * pair, 128 * pair + 128)
        for half, (lower, upper) in enumerate(((0, 3), (1, 2))):
            lanes = slice(128 * half, 128 * half + 128)
            one = parts_ref[2 * pair, :, lanes].astype(jnp.float32)
            two = parts_ref[2 * pair + 1, :, lanes].astype(jnp.float32)
            out_ref[lower, :, columns] = jnp.where(low, one, pltpu.roll(two, HEAD, 1)).astype(
                jnp.bfloat16
            )
            out_ref[upper, :, columns] = jnp.where(low, pltpu.roll(one, HEAD, 1), two).astype(
                jnp.bfloat16
            )


def spread_heads(parts):
    return pl.pallas_call(
        spread_kernel,
        out_shape=jax.ShapeDtypeStruct((4, 64, HQ), jnp.bfloat16),
        name="spread_heads",
    )(parts)


def output_kernel(place_ref, grads_ref, arrived_ref, weights_ref, out_ref, input_grad_ref, held_ref):
    core, odd = place_ref[0], place_ref[1]

    @pl.when(pl.program_id(0) == 0)
    def _():
        low = low_lanes(SPAN)
        for block in range(2):
            holder = jnp.bitwise_xor(odd, block)
            rows = slice(SPAN * block, SPAN * block + SPAN)
            for half in range(2):
                place = slice(SPAN * half, SPAN * half + SPAN)
                for pair in range(HEADS // 2):
                    columns = slice(128 * pair, 128 * pair + 128)
                    one, two = (
                        jnp.where(
                            holder == core,
                            grads_ref[head, 0, place, :].astype(jnp.float32),
                            arrived_ref[head, place, :].astype(jnp.float32),
                        )
                        for head in (2 * pair, 2 * pair + 1)
                    )
                    held_ref[2 * half, rows, columns] = jnp.where(
                        low, one, pltpu.roll(two, HEAD, 1)
                    ).astype(jnp.bfloat16)
                    held_ref[2 * half + 1, rows, columns] = jnp.where(
                        low, pltpu.roll(one, HEAD, 1), two
                    ).astype(jnp.bfloat16)

    def product(number, weight):
        return lax.dot_general(
            held_ref[number], weights_ref[weight], (((1,), (1,)), ((), ())),
            preferred_element_type=jnp.float32,
        )

    out_ref[...] = product(1, 3).astype(jnp.bfloat16).reshape(2, SPAN, D // 4)
    input_grad = product(0, 0) + product(2, 1) + product(3, 2)
    input_grad_ref[...] = input_grad.astype(jnp.bfloat16).reshape(2, SPAN, D // 4)


def outputs(place, grads, arrived, weights):
    shape = jax.ShapeDtypeStruct((2, SPAN, D), jnp.bfloat16)
    out_spec = pl.BlockSpec((2, SPAN, D // 4), lambda j, place: (0, 0, j))
    return pl.pallas_call(
        output_kernel,
        out_shape=(shape, shape),
        grid_spec=pltpu.PrefetchScalarGridSpec(
            num_scalar_prefetch=1,
            grid=(4,),
            in_specs=[
                pl.BlockSpec((HEADS, 1, 2 * SPAN, 128), lambda j, place: (0, place[0], 0, 0)),
                pl.BlockSpec((HEADS, 2 * SPAN, 128), lambda j, place: (0, 0, 0)),
                pl.BlockSpec((4, D // 4, HQ), lambda j, place: (0, j, 0)),
            ],
            out_specs=(out_spec, out_spec),
            scratch_shapes=[pltpu.VMEM((4, 2 * SPAN, HQ), jnp.bfloat16)],
        ),
        compiler_params=pltpu.CompilerParams(vmem_limit_bytes=VMEM_LIMIT),
        cost_estimate=pl.CostEstimate(
            flops=8 * 2 * SPAN * D * HQ, bytes_accessed=7 * 1024 * 1024, transcendentals=0
        ),
        name="outputs",
    )(place, grads, arrived, weights)


def per_device(tokens, sweep_tiles, weights, cotangent):
    core = lax.axis_index("dp") % 2
    rank = lax.axis_index("ctx")
    odd = rank % 2
    gather_pair = functools.partial(
        lax.all_gather, axis_name="dp", axis_index_groups=CORE_PAIRS, axis=0, tiled=True
    )
    tokens_pair = gather_pair(tokens.reshape(1, 2, SPAN, D))
    upstream_pair = gather_pair(cotangent.reshape(1, 2, SPAN, D))
    tokens_line, upstream_line = (
        lax.all_gather(
            rows.reshape(1, 2, SPAN, D), "dp", axis_index_groups=X_LINES, axis=0, tiled=True
        )
        for rows in (tokens, cotangent)
    )
    other_tiles = lax.ppermute(sweep_tiles, "dp", CORE_SWAP)
    block = jnp.bitwise_xor(core, odd).astype(jnp.int32).reshape(1)
    packed = project(block, tokens_pair, upstream_pair, weights).reshape(RANKS, 2 * SPAN, 128)
    own = lax.all_to_all(packed, "ctx", 0, 0)
    other = lax.ppermute(own[:, SPAN:], "dp", CORE_SWAP)
    tiles = jnp.where(odd == core, sweep_tiles, other_tiles).reshape(-1)
    query_part, own_grad, other_grad = attend(core.astype(jnp.int32).reshape(1), tiles, own, other)
    arrived = lax.ppermute(other_grad, "dp", CORE_SWAP)
    key_part = (own_grad + arrived.astype(jnp.float32)).astype(jnp.bfloat16)
    back = lax.all_to_all(jnp.concatenate([query_part, key_part], axis=1), "ctx", 0, 0)
    grads = back.reshape(HEADS, 2, 2 * SPAN, 128)
    line = lax.all_to_all(grads, "dp", 0, 0, axis_index_groups=X_LINES)
    terms = weight_terms(odd.astype(jnp.int32).reshape(1), line, tokens_line, upstream_line)
    terms = lax.all_to_all(terms, "ctx", 0, 0)
    swapped = lax.ppermute(
        lax.dynamic_index_in_dim(grads, 1 - core, 1, keepdims=False), "dp", CORE_SWAP
    )
    place = jnp.stack([core, odd]).astype(jnp.int32)
    attn_out, input_grad = outputs(place, grads, swapped, weights)
    rows = lax.reduce_precision(jnp.sum(terms.astype(jnp.float32), axis=0), 8, 7)
    other_rows = lax.ppermute(rows.astype(jnp.bfloat16), "dp", Z_SWAP)
    factor = float(16 * RANKS * 2 * SPAN) ** -0.5
    rows = ((rows + other_rows.astype(jnp.float32)) * factor).astype(jnp.bfloat16)
    parts = lax.all_to_all(
        jnp.broadcast_to(rows, (HEADS, 64, 256)), "dp", 0, 0, axis_index_groups=X_LINES
    )
    weight_grads = spread_heads(parts)
    return (attn_out.reshape(tokens.shape), input_grad.reshape(tokens.shape), weight_grads)


def solution(mesh):
    placed = (
        P("dp", "ctx", None, None, None),
        P("dp", None),
        P(),
        P("dp", "ctx", None, None, None),
    )
    return jax.shard_map(
        per_device,
        mesh=mesh,
        in_specs=placed,
        out_specs=(
            P("dp", "ctx", None, None, None),
            P("dp", "ctx", None, None, None),
            P(None, "ctx", None),
        ),
        check_vma=False,
    )
```

```python
import jax
import jax.numpy as jnp
from jax import lax
from jax.experimental import pallas as pl
from jax.experimental.pallas import tpu as pltpu
from jax.sharding import PartitionSpec as P

D = 1024
HEADS = 8
HEAD = 64
HQ = HEADS * HEAD
SPAN = 96
RANKS = 16
TILES = 2 * RANKS
CHUNK = 256
KEY_ROWS = TILES * SPAN + CHUNK
NEGATIVE = -1e30
VMEM_LIMIT = 48 * 1024 * 1024

CORE_SWAP = [(i, i ^ 1) for i in range(16)]
X_LINES = [[4 * x + 2 * z + core for x in range(4) for core in range(2)] for z in range(2)]
CHIP_LINES = [[4 * x + rest for x in range(4)] for rest in range(4)]
X_SHIFTS = [[(i, (i + 4 * shift) % 16) for i in range(16)] for shift in range(1, 4)]
Z_SWAP = [(i, i ^ 2) for i in range(16)]


def low_lanes(rows):
    return lax.broadcasted_iota(jnp.int32, (rows, 128), 1) < HEAD


def project_kernel(core_ref, mine_ref, arrived_ref, weights_ref, out_ref):
    core = core_ref[0]
    inputs = jnp.concatenate([mine_ref[0], arrived_ref[0]], axis=0)
    upstream = jnp.concatenate([mine_ref[1], arrived_ref[1]], axis=0)

    def product(rows, number):
        return jnp.dot(rows, weights_ref[number], preferred_element_type=jnp.float32)

    queries, keys, values = (product(inputs, number) for number in range(3))
    grads = product(upstream, 3)
    low = low_lanes(2 * SPAN)
    for half, (first, second) in enumerate(((queries, grads), (keys, values))):
        place = slice(SPAN * half, SPAN * half + SPAN)
        for pair in range(2):
            one = first[:, 128 * pair : 128 * pair + 128]
            two = second[:, 128 * pair : 128 * pair + 128]
            even = jnp.where(low, one, pltpu.roll(two, HEAD, 1)).astype(jnp.bfloat16)
            odd = jnp.where(low, pltpu.roll(one, HEAD, 1), two).astype(jnp.bfloat16)
            for part in range(2):
                rows = slice(SPAN * part, SPAN * part + SPAN)
                sequence = jnp.bitwise_xor(core, part)
                out_ref[2 * pair, sequence, place, :] = even[rows]
                out_ref[2 * pair + 1, sequence, place, :] = odd[rows]


def project(core, mine, arrived, weights):
    block_spec = pl.BlockSpec((2, SPAN, D), lambda j, core: (0, 0, 0))
    return pl.pallas_call(
        project_kernel,
        out_shape=jax.ShapeDtypeStruct((HEADS, 2, 2 * SPAN, 128), jnp.bfloat16),
        grid_spec=pltpu.PrefetchScalarGridSpec(
            num_scalar_prefetch=1,
            grid=(2,),
            in_specs=[
                block_spec,
                block_spec,
                pl.BlockSpec((4, D, HQ // 2), lambda j, core: (0, 0, j)),
            ],
            out_specs=pl.BlockSpec((HEADS // 2, 2, 2 * SPAN, 128), lambda j, core: (j, 0, 0, 0)),
        ),
        compiler_params=pltpu.CompilerParams(vmem_limit_bytes=VMEM_LIMIT),
        name="project",
    )(core, mine, arrived, weights)


def attend_kernel(
    core_ref, tiles_ref, own_ref, other_ref, out_ref, own_grad_ref, other_grad_ref,
    key_ref, grad_ref, score_ref, prob_grad_ref,
):
    core = core_ref[0]
    first = tiles_ref[0]
    second = first + tiles_ref[1]
    third = second + tiles_ref[2]
    grad_ref[...] = jnp.zeros_like(grad_ref)
    key_ref[TILES * SPAN :, :] = jnp.zeros((CHUNK, 128), jnp.bfloat16)

    def own_tile(rank):
        return jnp.where(rank % 2 == core, rank, TILES - 1 - rank)

    def tile_rows(tile):
        return pl.ds(pl.multiple_of(tile * SPAN, SPAN), SPAN)

    for rank in range(RANKS):
        tile = own_tile(rank)
        key_ref[tile_rows(tile), :] = own_ref[rank, SPAN:, :]
        key_ref[tile_rows(TILES - 1 - tile), :] = other_ref[rank]


    def tile_start(tile):
        return jnp.where(
            tile >= third, third, jnp.where(tile >= second, second, jnp.where(tile >= first, first, 0))
        )

    def holder(tile):
        return jnp.where(tile < RANKS, tile, TILES - 1 - tile)

    def two_tiles(tile, chunks):
        start, next_start = tile_start(tile), tile_start(tile + 2)
        base = pl.multiple_of(start * SPAN, SPAN)
        ranks = (holder(tile), holder(tile + 2))
        packed = jnp.concatenate([own_ref[rank, :SPAN, :] for rank in ranks], axis=0)
        low = low_lanes(2 * SPAN)
        query_only = jnp.where(low, packed, jnp.zeros_like(packed)) * jnp.bfloat16(HEAD ** -0.5)
        grad_only = jnp.where(low, jnp.zeros_like(packed), packed)
        left = jnp.concatenate([query_only, grad_only], axis=0)
        right = jnp.concatenate([grad_only, query_only], axis=0)
        row = lax.broadcasted_iota(jnp.int32, (2 * SPAN, CHUNK), 0)
        lane = lax.broadcasted_iota(jnp.int32, (2 * SPAN, CHUNK), 1)
        upper = row < SPAN
        last = row + (tile - start) * SPAN + jnp.where(upper, 0, SPAN) - lane
        earliest = jnp.where(upper, 0, (next_start - start) * SPAN) - lane

        def rows(j):
            return pl.ds(pl.multiple_of(base + CHUNK * j, 32), CHUNK)

        top = jnp.full((2 * SPAN, 1), NEGATIVE, jnp.float32)
        for j in range(chunks):
            both = lax.dot_general(
                left, key_ref[rows(j), :], (((1,), (1,)), ((), ())),
                preferred_element_type=jnp.float32,
            )
            allowed = earliest <= CHUNK * j
            if j >= chunks - 3:
                allowed = jnp.logical_and(allowed, last >= CHUNK * j)
            scores = jnp.where(allowed, both[: 2 * SPAN], NEGATIVE)
            place = slice(CHUNK * j, CHUNK * j + CHUNK)
            score_ref[:, place] = scores
            prob_grad_ref[:, place] = both[2 * SPAN :]
            top = jnp.maximum(top, jnp.max(scores, axis=1, keepdims=True))
        total = jnp.zeros((2 * SPAN, 1), jnp.float32)
        accum = jnp.zeros((2 * SPAN, 128), jnp.float32)
        for j in range(chunks):
            place = slice(CHUNK * j, CHUNK * j + CHUNK)
            expo = jnp.exp(score_ref[:, place] - top)
            score_ref[:, place] = expo
            total = total + jnp.sum(expo, axis=1, keepdims=True)
            accum = accum + jnp.dot(
                expo.astype(jnp.bfloat16), key_ref[rows(j), :], preferred_element_type=jnp.float32
            )
        inverse = 1.0 / total
        context = (accum / total).astype(jnp.bfloat16)
        delta = jnp.sum(
            grad_only.astype(jnp.float32) * context.astype(jnp.float32), axis=1, keepdims=True
        )
        query_grad = jnp.zeros((2 * SPAN, 128), jnp.float32)
        for j in range(chunks):
            place = slice(CHUNK * j, CHUNK * j + CHUNK)
            probs = score_ref[:, place] * inverse
            score_grad = (probs * (prob_grad_ref[:, place] - delta)).astype(jnp.bfloat16)
            query_grad = query_grad + jnp.dot(
                score_grad, key_ref[rows(j), :], preferred_element_type=jnp.float32
            )
            stacked = jnp.concatenate([probs.astype(jnp.bfloat16), score_grad], axis=0)
            grad_ref[rows(j), :] += lax.dot_general(
                stacked, right, (((0,), (0,)), ((), ())), preferred_element_type=jnp.float32
            )
        merged = jnp.where(low, query_grad * HEAD ** -0.5, context.astype(jnp.float32)).astype(jnp.bfloat16)
        out_ref[ranks[0]] = merged[:SPAN]
        out_ref[ranks[1]] = merged[SPAN:]

    def one_step(step, carry):
        tile = core + 4 * step
        chunks = ((tile + 3 - tile_start(tile)) * SPAN + CHUNK - 1) // CHUNK
        for count in range(2, 8):
            @pl.when(chunks == count)
            def _():
                two_tiles(tile, count)
        return carry

    lax.fori_loop(0, TILES // 4, one_step, 0)
    for rank in range(RANKS):
        tile = own_tile(rank)
        own_grad_ref[rank] = grad_ref[tile_rows(tile), :]
        other_grad_ref[rank] = grad_ref[tile_rows(TILES - 1 - tile), :].astype(jnp.bfloat16)


def attend(core, tiles, own, other):
    smem = pl.BlockSpec(memory_space=pltpu.SMEM)
    vmem = pl.BlockSpec(memory_space=pltpu.VMEM)
    block = (RANKS, SPAN, 128)
    return pl.pallas_call(
        attend_kernel,
        out_shape=(
            jax.ShapeDtypeStruct(block, jnp.bfloat16),
            jax.ShapeDtypeStruct(block, jnp.float32),
            jax.ShapeDtypeStruct(block, jnp.bfloat16),
        ),
        in_specs=[smem, smem, vmem, vmem],
        out_specs=(vmem, vmem, vmem),
        scratch_shapes=[
            pltpu.VMEM((KEY_ROWS, 128), jnp.bfloat16),
            pltpu.VMEM((KEY_ROWS, 128), jnp.float32),
            pltpu.VMEM((2 * SPAN, 7 * CHUNK), jnp.float32),
            pltpu.VMEM((2 * SPAN, 7 * CHUNK), jnp.float32),
        ],
        compiler_params=pltpu.CompilerParams(vmem_limit_bytes=VMEM_LIMIT),
        name="attend",
    )(core, tiles, own, other)


def weight_kernel(place_ref, grads_ref, *refs):
    line_refs, (keep_ref, give_ref, held_ref) = refs[:4], refs[4:]
    core, column = place_ref[0], place_ref[1]

    @pl.when(pl.program_id(0) == 0)
    def _():
        for shift in range(4):
            chip = jnp.bitwise_and(column + 4 - shift, 3)
            for part in range(2):
                sequence = jnp.bitwise_xor(core, part)
                first = (2 * shift + part) * SPAN
                for head in range(2):
                    for half in range(2):
                        lanes = 128 * (2 * half + head)
                        held_ref[first : first + SPAN, lanes : lanes + 128] = grads_ref[
                            chip, head, sequence, SPAN * half : SPAN * half + SPAN, :
                        ]

    def product(kind, columns):
        rows = jnp.concatenate([ref[part, kind] for ref in line_refs for part in range(2)], axis=0)
        return lax.dot_general(
            rows, held_ref[:, :columns], (((0,), (0,)), ((), ())), preferred_element_type=jnp.float32
        )

    by_tokens = product(0, 512)
    by_upstream = product(1, 256)
    low = low_lanes(D // 4)
    firsts = [
        jnp.where(low, by_tokens[:, 128 * i : 128 * i + 128], by_upstream[:, 128 * i : 128 * i + 128])
        for i in range(2)
    ]
    seconds = [by_tokens[:, 256:384], by_tokens[:, 384:]]
    for lanes, (zero, one) in ((slice(0, 128), firsts), (slice(128, 256), seconds)):
        kept = jnp.where(core == 0, zero, one).astype(jnp.bfloat16)
        given = jnp.where(core == 0, one, zero).astype(jnp.bfloat16)
        keep_ref[:, :, lanes] = kept.reshape(4, 64, 128)
        give_ref[:, :, lanes] = given.reshape(4, 64, 128)


def weight_terms(place, grads, lines):
    shape = jax.ShapeDtypeStruct((RANKS, 64, 256), jnp.bfloat16)
    line_spec = pl.BlockSpec((2, 2, SPAN, D // 4), lambda j, place: (0, 0, 0, j))
    out_spec = pl.BlockSpec((4, 64, 256), lambda j, place: (j, 0, 0))
    return pl.pallas_call(
        weight_kernel,
        out_shape=(shape, shape),
        grid_spec=pltpu.PrefetchScalarGridSpec(
            num_scalar_prefetch=1,
            grid=(4,),
            in_specs=[
                pl.BlockSpec((4, 2, 2, 2 * SPAN, 128), lambda j, place: (0, 0, 0, 0, 0)),
                line_spec, line_spec, line_spec, line_spec,
            ],
            out_specs=(out_spec, out_spec),
            scratch_shapes=[pltpu.VMEM((8 * SPAN, 512), jnp.bfloat16)],
        ),
        compiler_params=pltpu.CompilerParams(vmem_limit_bytes=VMEM_LIMIT),
        name="weight_terms",
    )(place, grads, *lines)


def spread_kernel(parts_ref, out_ref):
    low = low_lanes(64)
    for pair in range(HEADS // 2):
        columns = slice(128 * pair, 128 * pair + 128)
        for half, (lower, upper) in enumerate(((0, 3), (1, 2))):
            lanes = slice(128 * half, 128 * half + 128)
            one = parts_ref[2 * pair, :, lanes].astype(jnp.float32)
            two = parts_ref[2 * pair + 1, :, lanes].astype(jnp.float32)
            out_ref[lower, :, columns] = jnp.where(low, one, pltpu.roll(two, HEAD, 1)).astype(
                jnp.bfloat16
            )
            out_ref[upper, :, columns] = jnp.where(low, pltpu.roll(one, HEAD, 1), two).astype(
                jnp.bfloat16
            )


def spread_heads(parts):
    return pl.pallas_call(
        spread_kernel,
        out_shape=jax.ShapeDtypeStruct((4, 64, HQ), jnp.bfloat16),
        name="spread_heads",
    )(parts)


def output_kernel(place_ref, grads_ref, arrived_ref, weights_ref, out_ref, input_grad_ref, held_ref):
    core, odd = place_ref[0], place_ref[1]

    @pl.when(pl.program_id(0) == 0)
    def _():
        low = low_lanes(SPAN)
        for block in range(2):
            holder = jnp.bitwise_xor(odd, block)
            rows = slice(SPAN * block, SPAN * block + SPAN)
            for half in range(2):
                place = slice(SPAN * half, SPAN * half + SPAN)
                for pair in range(HEADS // 2):
                    columns = slice(128 * pair, 128 * pair + 128)
                    one, two = (
                        jnp.where(
                            holder == core,
                            grads_ref[head, 0, place, :].astype(jnp.float32),
                            arrived_ref[head, place, :].astype(jnp.float32),
                        )
                        for head in (2 * pair, 2 * pair + 1)
                    )
                    held_ref[2 * half, rows, columns] = jnp.where(
                        low, one, pltpu.roll(two, HEAD, 1)
                    ).astype(jnp.bfloat16)
                    held_ref[2 * half + 1, rows, columns] = jnp.where(
                        low, pltpu.roll(one, HEAD, 1), two
                    ).astype(jnp.bfloat16)

    def product(number, weight):
        return lax.dot_general(
            held_ref[number], weights_ref[weight], (((1,), (1,)), ((), ())),
            preferred_element_type=jnp.float32,
        )

    out_ref[...] = product(1, 3).astype(jnp.bfloat16).reshape(2, SPAN, D // 4)
    input_grad = product(0, 0) + product(2, 1) + product(3, 2)
    input_grad_ref[...] = input_grad.astype(jnp.bfloat16).reshape(2, SPAN, D // 4)


def outputs(place, grads, arrived, weights):
    shape = jax.ShapeDtypeStruct((2, SPAN, D), jnp.bfloat16)
    out_spec = pl.BlockSpec((2, SPAN, D // 4), lambda j, place: (0, 0, j))
    return pl.pallas_call(
        output_kernel,
        out_shape=(shape, shape),
        grid_spec=pltpu.PrefetchScalarGridSpec(
            num_scalar_prefetch=1,
            grid=(4,),
            in_specs=[
                pl.BlockSpec((HEADS, 1, 2 * SPAN, 128), lambda j, place: (0, place[0], 0, 0)),
                pl.BlockSpec((HEADS, 2 * SPAN, 128), lambda j, place: (0, 0, 0)),
                pl.BlockSpec((4, D // 4, HQ), lambda j, place: (0, j, 0)),
            ],
            out_specs=(out_spec, out_spec),
            scratch_shapes=[pltpu.VMEM((4, 2 * SPAN, HQ), jnp.bfloat16)],
        ),
        compiler_params=pltpu.CompilerParams(vmem_limit_bytes=VMEM_LIMIT),
        cost_estimate=pl.CostEstimate(
            flops=8 * 2 * SPAN * D * HQ, bytes_accessed=7 * 1024 * 1024, transcendentals=0
        ),
        name="outputs",
    )(place, grads, arrived, weights)


def per_device(tokens, sweep_tiles, weights, cotangent):
    core = lax.axis_index("dp") % 2
    column = lax.axis_index("dp") // 4
    rank = lax.axis_index("ctx")
    odd = rank % 2
    block = jnp.bitwise_xor(core, odd)

    def chosen(number):
        return jnp.stack(
            [
                lax.dynamic_index_in_dim(rows.reshape(2, SPAN, D), number, 0, keepdims=False)
                for rows in (tokens, cotangent)
            ]
        )

    mine = chosen(block)
    arrived = lax.ppermute(chosen(1 - block), "dp", CORE_SWAP)
    other_tiles = lax.ppermute(sweep_tiles, "dp", CORE_SWAP)
    core_number = core.astype(jnp.int32).reshape(1)
    packed = project(core_number, mine, arrived, weights).reshape(RANKS, 2 * SPAN, 128)
    line = jnp.stack([mine, arrived])
    lines = [line] + [lax.ppermute(line, "dp", shift) for shift in X_SHIFTS]
    own = lax.all_to_all(packed, "ctx", 0, 0)
    other = lax.ppermute(own[:, SPAN:], "dp", CORE_SWAP)
    tiles = jnp.where(odd == core, sweep_tiles, other_tiles).reshape(-1)
    query_part, own_grad, other_grad = attend(core_number, tiles, own, other)
    arrived = lax.ppermute(other_grad, "dp", CORE_SWAP)
    key_part = (own_grad + arrived.astype(jnp.float32)).astype(jnp.bfloat16)
    back = lax.all_to_all(jnp.concatenate([query_part, key_part], axis=1), "ctx", 0, 0)
    grads = back.reshape(HEADS, 2, 2 * SPAN, 128)
    line_grads = lax.all_to_all(
        back.reshape(4, 2, 2, 2 * SPAN, 128), "dp", 0, 0, axis_index_groups=CHIP_LINES
    )
    keep, give = weight_terms(
        jnp.stack([core, column]).astype(jnp.int32), line_grads, lines
    )
    given = lax.ppermute(give, "dp", CORE_SWAP)
    terms = (keep.astype(jnp.float32) + given.astype(jnp.float32)).astype(jnp.bfloat16)
    terms = lax.all_to_all(terms, "ctx", 0, 0)
    swapped = lax.ppermute(
        lax.dynamic_index_in_dim(grads, 1 - core, 1, keepdims=False), "dp", CORE_SWAP
    )
    place = jnp.stack([core, odd]).astype(jnp.int32)
    attn_out, input_grad = outputs(place, grads, swapped, weights)
    terms, attn_out, input_grad = lax.optimization_barrier((terms, attn_out, input_grad))
    rows = lax.reduce_precision(jnp.sum(terms.astype(jnp.float32), axis=0), 8, 7)
    other_rows = lax.ppermute(rows.astype(jnp.bfloat16), "dp", Z_SWAP)
    factor = float(16 * RANKS * 2 * SPAN) ** -0.5
    rows = ((rows + other_rows.astype(jnp.float32)) * factor).astype(jnp.bfloat16)
    parts = lax.all_to_all(
        jnp.broadcast_to(rows, (HEADS, 64, 256)), "dp", 0, 0, axis_index_groups=X_LINES
    )
    weight_grads = spread_heads(parts)
    return (attn_out.reshape(tokens.shape), input_grad.reshape(tokens.shape), weight_grads)


def solution(mesh):
    placed = (
        P("dp", "ctx", None, None, None),
        P("dp", None),
        P(),
        P("dp", "ctx", None, None, None),
    )
    return jax.shard_map(
        per_device,
        mesh=mesh,
        in_specs=placed,
        out_specs=(
            P("dp", "ctx", None, None, None),
            P("dp", "ctx", None, None, None),
            P(None, "ctx", None),
        ),
        check_vma=False,
    )
```

```python
import jax
import jax.numpy as jnp
from jax import lax
from jax.experimental import pallas as pl
from jax.experimental.pallas import tpu as pltpu
from jax.sharding import PartitionSpec as P

D = 1024
HEADS = 8
HEAD = 64
HQ = HEADS * HEAD
SPAN = 96
RANKS = 16
TILES = 2 * RANKS
CHUNK = 256
KEY_ROWS = TILES * SPAN + CHUNK
NEGATIVE = -1e30
VMEM_LIMIT = 48 * 1024 * 1024
PROJECT_VMEM = 51 * 1024 * 1024

CORE_SWAP = [(i, i ^ 1) for i in range(16)]
CHIP_LINES = [[4 * x + rest for x in range(4)] for rest in range(4)]
X_SHIFTS = [[(i, (i + 4 * shift) % 16) for i in range(16)] for shift in range(1, 4)]


def low_lanes(rows):
    return lax.broadcasted_iota(jnp.int32, (rows, 128), 1) < HEAD


def project_kernel(
    place_ref, tokens_ref, other_tokens_ref, upstream_ref, other_upstream_ref, weights_ref,
    out_ref, line_ref,
):
    core = place_ref[0]
    inputs = jnp.concatenate([tokens_ref[0], other_tokens_ref[0]], axis=0)
    upstream = jnp.concatenate([upstream_ref[0], other_upstream_ref[0]], axis=0)

    @pl.when(pl.program_id(0) == 0)
    def _():
        line_ref[0, 0] = tokens_ref[0]
        line_ref[0, 1] = upstream_ref[0]
        line_ref[1, 0] = other_tokens_ref[0]
        line_ref[1, 1] = other_upstream_ref[0]

    def product(rows, number):
        return jnp.dot(rows, weights_ref[number], preferred_element_type=jnp.float32)

    queries, keys, values = (product(inputs, number) for number in range(3))
    grads = product(upstream, 3)
    low = low_lanes(2 * SPAN)
    for half, (first, second) in enumerate(((queries, grads), (keys, values))):
        place = slice(SPAN * half, SPAN * half + SPAN)
        for pair in range(2):
            one = first[:, 128 * pair : 128 * pair + 128]
            two = second[:, 128 * pair : 128 * pair + 128]
            even = jnp.where(low, one, pltpu.roll(two, HEAD, 1)).astype(jnp.bfloat16)
            odd = jnp.where(low, pltpu.roll(one, HEAD, 1), two).astype(jnp.bfloat16)
            for part in range(2):
                rows = slice(SPAN * part, SPAN * part + SPAN)
                sequence = jnp.bitwise_xor(core, part)
                out_ref[2 * pair, sequence, place, :] = even[rows]
                out_ref[2 * pair + 1, sequence, place, :] = odd[rows]


def project(place, rows, weights):
    block_spec = pl.BlockSpec((1, SPAN, D), lambda j, place: (place[1], 0, 0))
    return pl.pallas_call(
        project_kernel,
        out_shape=(
            jax.ShapeDtypeStruct((HEADS, 2, 2 * SPAN, 128), jnp.bfloat16),
            jax.ShapeDtypeStruct((2, 2, SPAN, D), jnp.bfloat16),
        ),
        grid_spec=pltpu.PrefetchScalarGridSpec(
            num_scalar_prefetch=1,
            grid=(2,),
            in_specs=[
                block_spec, block_spec, block_spec, block_spec,
                pl.BlockSpec((4, D, HQ // 2), lambda j, place: (0, 0, j)),
            ],
            out_specs=(
                pl.BlockSpec((HEADS // 2, 2, 2 * SPAN, 128), lambda j, place: (j, 0, 0, 0)),
                pl.BlockSpec((2, 2, SPAN, D), lambda j, place: (0, 0, 0, 0)),
            ),
        ),
        compiler_params=pltpu.CompilerParams(vmem_limit_bytes=PROJECT_VMEM),
        name="project",
    )(place, *rows, weights)


def attend_kernel(
    core_ref, tiles_ref, own_ref, other_ref, out_ref, own_grad_ref, other_grad_ref,
    key_ref, grad_ref, score_ref, prob_grad_ref,
):
    core = core_ref[0]
    first = tiles_ref[0]
    second = first + tiles_ref[1]
    third = second + tiles_ref[2]
    grad_ref[...] = jnp.zeros_like(grad_ref)
    key_ref[TILES * SPAN :, :] = jnp.zeros((CHUNK, 128), jnp.bfloat16)

    def own_tile(rank):
        return jnp.where(rank % 2 == core, rank, TILES - 1 - rank)

    def tile_rows(tile):
        return pl.ds(pl.multiple_of(tile * SPAN, SPAN), SPAN)

    for rank in range(RANKS):
        tile = own_tile(rank)
        key_ref[tile_rows(tile), :] = own_ref[rank, SPAN:, :]
        key_ref[tile_rows(TILES - 1 - tile), :] = other_ref[rank]


    def tile_start(tile):
        return jnp.where(
            tile >= third, third, jnp.where(tile >= second, second, jnp.where(tile >= first, first, 0))
        )

    def holder(tile):
        return jnp.where(tile < RANKS, tile, TILES - 1 - tile)

    def two_tiles(tile, chunks):
        start, next_start = tile_start(tile), tile_start(tile + 2)
        base = pl.multiple_of(start * SPAN, SPAN)
        ranks = (holder(tile), holder(tile + 2))
        packed = jnp.concatenate([own_ref[rank, :SPAN, :] for rank in ranks], axis=0)
        low = low_lanes(2 * SPAN)
        query_only = jnp.where(low, packed, jnp.zeros_like(packed)) * jnp.bfloat16(HEAD ** -0.5)
        grad_only = jnp.where(low, jnp.zeros_like(packed), packed)
        left = jnp.concatenate([query_only, grad_only], axis=0)
        right = jnp.concatenate([grad_only, query_only], axis=0)
        row = lax.broadcasted_iota(jnp.int32, (2 * SPAN, CHUNK), 0)
        lane = lax.broadcasted_iota(jnp.int32, (2 * SPAN, CHUNK), 1)
        upper = row < SPAN
        last = row + (tile - start) * SPAN + jnp.where(upper, 0, SPAN) - lane
        earliest = jnp.where(upper, 0, (next_start - start) * SPAN) - lane

        def rows(j):
            return pl.ds(pl.multiple_of(base + CHUNK * j, 32), CHUNK)

        top = jnp.full((2 * SPAN, 1), NEGATIVE, jnp.float32)
        for j in range(chunks):
            both = lax.dot_general(
                left, key_ref[rows(j), :], (((1,), (1,)), ((), ())),
                preferred_element_type=jnp.float32,
            )
            allowed = earliest <= CHUNK * j
            if j >= chunks - 3:
                allowed = jnp.logical_and(allowed, last >= CHUNK * j)
            scores = jnp.where(allowed, both[: 2 * SPAN], NEGATIVE)
            place = slice(CHUNK * j, CHUNK * j + CHUNK)
            score_ref[:, place] = scores
            prob_grad_ref[:, place] = both[2 * SPAN :]
            top = jnp.maximum(top, jnp.max(scores, axis=1, keepdims=True))
        total = jnp.zeros((2 * SPAN, 1), jnp.float32)
        accum = jnp.zeros((2 * SPAN, 128), jnp.float32)
        for j in range(chunks):
            place = slice(CHUNK * j, CHUNK * j + CHUNK)
            expo = jnp.exp(score_ref[:, place] - top)
            score_ref[:, place] = expo
            total = total + jnp.sum(expo, axis=1, keepdims=True)
            accum = accum + jnp.dot(
                expo.astype(jnp.bfloat16), key_ref[rows(j), :], preferred_element_type=jnp.float32
            )
        inverse = 1.0 / total
        context = (accum / total).astype(jnp.bfloat16)
        delta = jnp.sum(
            grad_only.astype(jnp.float32) * context.astype(jnp.float32), axis=1, keepdims=True
        )
        query_grad = jnp.zeros((2 * SPAN, 128), jnp.float32)
        for j in range(chunks):
            place = slice(CHUNK * j, CHUNK * j + CHUNK)
            probs = score_ref[:, place] * inverse
            score_grad = (probs * (prob_grad_ref[:, place] - delta)).astype(jnp.bfloat16)
            query_grad = query_grad + jnp.dot(
                score_grad, key_ref[rows(j), :], preferred_element_type=jnp.float32
            )
            stacked = jnp.concatenate([probs.astype(jnp.bfloat16), score_grad], axis=0)
            grad_ref[rows(j), :] += lax.dot_general(
                stacked, right, (((0,), (0,)), ((), ())), preferred_element_type=jnp.float32
            )
        merged = jnp.where(low, query_grad * HEAD ** -0.5, context.astype(jnp.float32)).astype(jnp.bfloat16)
        out_ref[ranks[0]] = merged[:SPAN]
        out_ref[ranks[1]] = merged[SPAN:]

    def one_step(step, carry):
        tile = core + 4 * step
        chunks = ((tile + 3 - tile_start(tile)) * SPAN + CHUNK - 1) // CHUNK
        for count in range(2, 8):
            @pl.when(chunks == count)
            def _():
                two_tiles(tile, count)
        return carry

    lax.fori_loop(0, TILES // 4, one_step, 0)
    for rank in range(RANKS):
        tile = own_tile(rank)
        own_grad_ref[rank] = grad_ref[tile_rows(tile), :]
        other_grad_ref[rank] = grad_ref[tile_rows(TILES - 1 - tile), :].astype(jnp.bfloat16)


def attend(core, tiles, own, other):
    smem = pl.BlockSpec(memory_space=pltpu.SMEM)
    vmem = pl.BlockSpec(memory_space=pltpu.VMEM)
    block = (RANKS, SPAN, 128)
    return pl.pallas_call(
        attend_kernel,
        out_shape=(
            jax.ShapeDtypeStruct(block, jnp.bfloat16),
            jax.ShapeDtypeStruct(block, jnp.float32),
            jax.ShapeDtypeStruct(block, jnp.bfloat16),
        ),
        in_specs=[smem, smem, vmem, vmem],
        out_specs=(vmem, vmem, vmem),
        scratch_shapes=[
            pltpu.VMEM((KEY_ROWS, 128), jnp.bfloat16),
            pltpu.VMEM((KEY_ROWS, 128), jnp.float32),
            pltpu.VMEM((2 * SPAN, 7 * CHUNK), jnp.float32),
            pltpu.VMEM((2 * SPAN, 7 * CHUNK), jnp.float32),
        ],
        compiler_params=pltpu.CompilerParams(vmem_limit_bytes=VMEM_LIMIT),
        name="attend",
    )(core, tiles, own, other)


def weight_kernel(place_ref, grads_ref, *refs):
    line_refs, (keep_ref, give_ref, held_ref) = refs[:4], refs[4:]
    core, column = place_ref[0], place_ref[1]

    @pl.when(pl.program_id(0) == 0)
    def _():
        for shift in range(4):
            chip = jnp.bitwise_and(column + 4 - shift, 3)
            for part in range(2):
                sequence = jnp.bitwise_xor(core, part)
                first = (2 * shift + part) * SPAN
                for head in range(2):
                    for half in range(2):
                        lanes = 128 * (2 * half + head)
                        held_ref[first : first + SPAN, lanes : lanes + 128] = grads_ref[
                            chip, head, sequence, SPAN * half : SPAN * half + SPAN, :
                        ]

    def product(kind, columns):
        rows = jnp.concatenate([ref[part, kind] for ref in line_refs for part in range(2)], axis=0)
        return lax.dot_general(
            rows, held_ref[:, :columns], (((0,), (0,)), ((), ())), preferred_element_type=jnp.float32
        )

    by_tokens = product(0, 512)
    by_upstream = product(1, 256)
    low = low_lanes(D // 4)
    firsts = [
        jnp.where(low, by_tokens[:, 128 * i : 128 * i + 128], by_upstream[:, 128 * i : 128 * i + 128])
        for i in range(2)
    ]
    seconds = [by_tokens[:, 256:384], by_tokens[:, 384:]]
    for lanes, (zero, one) in ((slice(0, 128), firsts), (slice(128, 256), seconds)):
        kept = jnp.where(core == 0, zero, one).astype(jnp.bfloat16)
        given = jnp.where(core == 0, one, zero).astype(jnp.bfloat16)
        keep_ref[:, :, lanes] = kept.reshape(4, 64, 128)
        give_ref[:, :, lanes] = given.reshape(4, 64, 128)


def weight_terms(place, grads, lines):
    shape = jax.ShapeDtypeStruct((RANKS, 64, 256), jnp.bfloat16)
    line_spec = pl.BlockSpec((2, 2, SPAN, D // 4), lambda j, place: (0, 0, 0, j))
    out_spec = pl.BlockSpec((4, 64, 256), lambda j, place: (j, 0, 0))
    return pl.pallas_call(
        weight_kernel,
        out_shape=(shape, shape),
        grid_spec=pltpu.PrefetchScalarGridSpec(
            num_scalar_prefetch=1,
            grid=(4,),
            in_specs=[
                pl.BlockSpec((4, 2, 2, 2 * SPAN, 128), lambda j, place: (0, 0, 0, 0, 0)),
                line_spec, line_spec, line_spec, line_spec,
            ],
            out_specs=(out_spec, out_spec),
            scratch_shapes=[pltpu.VMEM((8 * SPAN, 512), jnp.bfloat16)],
        ),
        compiler_params=pltpu.CompilerParams(vmem_limit_bytes=VMEM_LIMIT),
        name="weight_terms",
    )(place, grads, *lines)


def spread_kernel(parts_ref, out_ref):
    low = low_lanes(64)
    factor = float(16 * RANKS * 2 * SPAN) ** -0.5
    for column in range(4):
        columns = slice(128 * column, 128 * column + 128)
        for half, (lower, upper) in enumerate(((0, 3), (1, 2))):
            lanes = slice(128 * half, 128 * half + 128)
            one, two = (
                factor
                * (
                    parts_ref[column, 0, core, :, lanes].astype(jnp.float32)
                    + parts_ref[column, 1, core, :, lanes].astype(jnp.float32)
                )
                for core in range(2)
            )
            out_ref[lower, :, columns] = jnp.where(low, one, pltpu.roll(two, HEAD, 1)).astype(
                jnp.bfloat16
            )
            out_ref[upper, :, columns] = jnp.where(low, pltpu.roll(one, HEAD, 1), two).astype(
                jnp.bfloat16
            )


def spread_heads(parts):
    return pl.pallas_call(
        spread_kernel,
        out_shape=jax.ShapeDtypeStruct((4, 64, HQ), jnp.bfloat16),
        name="spread_heads",
    )(parts)


def output_kernel(place_ref, grads_ref, arrived_ref, weights_ref, out_ref, input_grad_ref, held_ref):
    core, odd = place_ref[0], place_ref[1]

    @pl.when(pl.program_id(0) == 0)
    def _():
        low = low_lanes(SPAN)
        for block in range(2):
            holder = jnp.bitwise_xor(odd, block)
            rows = slice(SPAN * block, SPAN * block + SPAN)
            for half in range(2):
                place = slice(SPAN * half, SPAN * half + SPAN)
                for pair in range(HEADS // 2):
                    columns = slice(128 * pair, 128 * pair + 128)
                    one, two = (
                        jnp.where(
                            holder == core,
                            grads_ref[head, 0, place, :].astype(jnp.float32),
                            arrived_ref[head, place, :].astype(jnp.float32),
                        )
                        for head in (2 * pair, 2 * pair + 1)
                    )
                    held_ref[2 * half, rows, columns] = jnp.where(
                        low, one, pltpu.roll(two, HEAD, 1)
                    ).astype(jnp.bfloat16)
                    held_ref[2 * half + 1, rows, columns] = jnp.where(
                        low, pltpu.roll(one, HEAD, 1), two
                    ).astype(jnp.bfloat16)

    def product(number, weight):
        return lax.dot_general(
            held_ref[number], weights_ref[weight], (((1,), (1,)), ((), ())),
            preferred_element_type=jnp.float32,
        )

    out_ref[...] = product(1, 3).astype(jnp.bfloat16).reshape(2, SPAN, D // 4)
    input_grad = product(0, 0) + product(2, 1) + product(3, 2)
    input_grad_ref[...] = input_grad.astype(jnp.bfloat16).reshape(2, SPAN, D // 4)


def outputs(place, grads, arrived, weights):
    shape = jax.ShapeDtypeStruct((2, SPAN, D), jnp.bfloat16)
    out_spec = pl.BlockSpec((2, SPAN, D // 4), lambda j, place: (0, 0, j))
    return pl.pallas_call(
        output_kernel,
        out_shape=(shape, shape),
        grid_spec=pltpu.PrefetchScalarGridSpec(
            num_scalar_prefetch=1,
            grid=(4,),
            in_specs=[
                pl.BlockSpec((HEADS, 1, 2 * SPAN, 128), lambda j, place: (0, place[0], 0, 0)),
                pl.BlockSpec((HEADS, 2 * SPAN, 128), lambda j, place: (0, 0, 0)),
                pl.BlockSpec((4, D // 4, HQ), lambda j, place: (0, j, 0)),
            ],
            out_specs=(out_spec, out_spec),
            scratch_shapes=[pltpu.VMEM((4, 2 * SPAN, HQ), jnp.bfloat16)],
        ),
        compiler_params=pltpu.CompilerParams(vmem_limit_bytes=VMEM_LIMIT),
        cost_estimate=pl.CostEstimate(
            flops=8 * 2 * SPAN * D * HQ, bytes_accessed=7 * 1024 * 1024, transcendentals=0
        ),
        name="outputs",
    )(place, grads, arrived, weights)


def per_device(tokens, sweep_tiles, weights, cotangent):
    core = lax.axis_index("dp") % 2
    column = lax.axis_index("dp") // 4
    rank = lax.axis_index("ctx")
    odd = rank % 2
    block = jnp.bitwise_xor(core, odd)

    rows = tokens.reshape(2, SPAN, D)
    upstream = cotangent.reshape(2, SPAN, D)
    other_rows = lax.ppermute(rows, "dp", CORE_SWAP)
    other_upstream = lax.ppermute(upstream, "dp", CORE_SWAP)
    other_tiles = lax.ppermute(sweep_tiles, "dp", CORE_SWAP)
    core_number = core.astype(jnp.int32).reshape(1)
    packed, line = project(
        jnp.stack([core, block]).astype(jnp.int32),
        (rows, other_rows, upstream, other_upstream),
        weights,
    )
    packed = packed.reshape(RANKS, 2 * SPAN, 128)
    shifted = [lax.ppermute(line, "dp", shift) for shift in X_SHIFTS]
    own = lax.all_to_all(packed, "ctx", 0, 0)
    own, *shifted = lax.optimization_barrier((own, *shifted))
    other = lax.ppermute(own[:, SPAN:], "dp", CORE_SWAP)
    lines = [line, *shifted]
    tiles = jnp.where(odd == core, sweep_tiles, other_tiles).reshape(-1)
    query_part, own_grad, other_grad = attend(core_number, tiles, own, other)
    arrived = lax.ppermute(other_grad, "dp", CORE_SWAP)
    key_part = (own_grad + arrived.astype(jnp.float32)).astype(jnp.bfloat16)
    back = lax.all_to_all(jnp.concatenate([query_part, key_part], axis=1), "ctx", 0, 0)
    grads = back.reshape(HEADS, 2, 2 * SPAN, 128)
    line_grads = lax.all_to_all(
        back.reshape(4, 2, 2, 2 * SPAN, 128), "dp", 0, 0, axis_index_groups=CHIP_LINES
    )
    keep, give = weight_terms(
        jnp.stack([core, column]).astype(jnp.int32), line_grads, lines
    )
    given = lax.ppermute(give, "dp", CORE_SWAP)
    terms = (keep.astype(jnp.float32) + given.astype(jnp.float32)).astype(jnp.bfloat16)
    terms, own_grads = lax.optimization_barrier((terms, grads))
    terms = lax.all_to_all(terms, "ctx", 0, 0)
    swapped = lax.ppermute(
        lax.dynamic_index_in_dim(grads, 1 - core, 1, keepdims=False), "dp", CORE_SWAP
    )
    place = jnp.stack([core, odd]).astype(jnp.int32)
    attn_out, input_grad = outputs(place, own_grads, swapped, weights)
    terms, attn_out, input_grad = lax.optimization_barrier((terms, attn_out, input_grad))
    rows = jnp.sum(terms.astype(jnp.float32), axis=0).astype(jnp.bfloat16)
    parts = lax.all_to_all(jnp.broadcast_to(rows, (16, 64, 256)), "dp", 0, 0)
    weight_grads = spread_heads(parts.reshape(4, 2, 2, 64, 256))
    return (attn_out.reshape(tokens.shape), input_grad.reshape(tokens.shape), weight_grads)


def solution(mesh):
    placed = (
        P("dp", "ctx", None, None, None),
        P("dp", None),
        P(),
        P("dp", "ctx", None, None, None),
    )
    return jax.shard_map(
        per_device,
        mesh=mesh,
        in_specs=placed,
        out_specs=(
            P("dp", "ctx", None, None, None),
            P("dp", "ctx", None, None, None),
            P(None, "ctx", None),
        ),
        check_vma=False,
    )
```

```python
import jax
import jax.numpy as jnp
from jax import lax
from jax.experimental import pallas as pl
from jax.experimental.pallas import tpu as pltpu
from jax.sharding import PartitionSpec as P

D = 1024
HEADS = 8
HEAD = 64
HQ = HEADS * HEAD
SPAN = 96
RANKS = 16
TILES = 2 * RANKS
CHUNK = 256
KEY_ROWS = TILES * SPAN + CHUNK
NEGATIVE = -1e30
VMEM_LIMIT = 48 * 1024 * 1024

CORE_SWAP = [(i, i ^ 1) for i in range(16)]
CHIP_LINES = [[4 * x + rest for x in range(4)] for rest in range(4)]
X_SHIFTS = [[(i, (i + 4 * shift) % 16) for i in range(16)] for shift in range(1, 4)]


def low_lanes(rows):
    return lax.broadcasted_iota(jnp.int32, (rows, 128), 1) < HEAD


def project_kernel(place_ref, tokens_ref, upstream_ref, weights_ref, *refs):
    out_ref, line_ref = refs[-2:]
    inputs = tokens_ref[0]
    upstream = upstream_ref[0]

    @pl.when(pl.program_id(0) == 0)
    def _():
        line_ref[0, 0] = inputs
        line_ref[0, 1] = upstream

    def product(rows, number):
        return jnp.dot(rows, weights_ref[number], preferred_element_type=jnp.float32)

    queries, keys, values = (product(inputs, number) for number in range(3))
    grads = product(upstream, 3)
    low = low_lanes(SPAN)
    for half, (first, second) in enumerate(((queries, grads), (keys, values))):
        place = slice(SPAN * half, SPAN * half + SPAN)
        for pair in range(2):
            one = first[:, 128 * pair : 128 * pair + 128]
            two = second[:, 128 * pair : 128 * pair + 128]
            even = jnp.where(low, one, pltpu.roll(two, HEAD, 1)).astype(jnp.bfloat16)
            odd = jnp.where(low, pltpu.roll(one, HEAD, 1), two).astype(jnp.bfloat16)
            out_ref[2 * pair, 0, place, :] = even
            out_ref[2 * pair + 1, 0, place, :] = odd


def project(place, part, tokens, upstream, weights, *filled):
    block_spec = pl.BlockSpec((1, SPAN, D), lambda j, place: (place[0], 0, 0))
    return pl.pallas_call(
        project_kernel,
        out_shape=(
            jax.ShapeDtypeStruct((HEADS, 2, 2 * SPAN, 128), jnp.bfloat16),
            jax.ShapeDtypeStruct((2, 2, SPAN, D), jnp.bfloat16),
        ),
        grid_spec=pltpu.PrefetchScalarGridSpec(
            num_scalar_prefetch=1,
            grid=(2,),
            in_specs=[
                block_spec,
                block_spec,
                pl.BlockSpec((4, D, HQ // 2), lambda j, place: (0, 0, j)),
            ]
            + [pl.BlockSpec(memory_space=pl.ANY)] * len(filled),
            out_specs=(
                pl.BlockSpec((HEADS // 2, 1, 2 * SPAN, 128), lambda j, place: (j, place[1], 0, 0)),
                pl.BlockSpec((1, 2, SPAN, D), lambda j, place: (part, 0, 0, 0)),
            ),
        ),
        input_output_aliases={4 + i: i for i in range(len(filled))},
        compiler_params=pltpu.CompilerParams(vmem_limit_bytes=VMEM_LIMIT),
        name="project",
    )(place, tokens, upstream, weights, *filled)


def attend_kernel(
    core_ref, tiles_ref, own_ref, other_ref, out_ref, own_grad_ref, other_grad_ref,
    key_ref, grad_ref, score_ref, prob_grad_ref,
):
    core = core_ref[0]
    first = tiles_ref[0]
    second = first + tiles_ref[1]
    third = second + tiles_ref[2]
    grad_ref[...] = jnp.zeros_like(grad_ref)
    key_ref[TILES * SPAN :, :] = jnp.zeros((CHUNK, 128), jnp.bfloat16)

    def own_tile(rank):
        return jnp.where(rank % 2 == core, rank, TILES - 1 - rank)

    def tile_rows(tile):
        return pl.ds(pl.multiple_of(tile * SPAN, SPAN), SPAN)

    for rank in range(RANKS):
        tile = own_tile(rank)
        key_ref[tile_rows(tile), :] = own_ref[rank, SPAN:, :]
        key_ref[tile_rows(TILES - 1 - tile), :] = other_ref[rank]


    def tile_start(tile):
        return jnp.where(
            tile >= third, third, jnp.where(tile >= second, second, jnp.where(tile >= first, first, 0))
        )

    def holder(tile):
        return jnp.where(tile < RANKS, tile, TILES - 1 - tile)

    def two_tiles(tile, chunks):
        start, next_start = tile_start(tile), tile_start(tile + 2)
        base = pl.multiple_of(start * SPAN, SPAN)
        ranks = (holder(tile), holder(tile + 2))
        packed = jnp.concatenate([own_ref[rank, :SPAN, :] for rank in ranks], axis=0)
        low = low_lanes(2 * SPAN)
        query_only = jnp.where(low, packed, jnp.zeros_like(packed)) * jnp.bfloat16(HEAD ** -0.5)
        grad_only = jnp.where(low, jnp.zeros_like(packed), packed)
        left = jnp.concatenate([query_only, grad_only], axis=0)
        right = jnp.concatenate([grad_only, query_only], axis=0)
        row = lax.broadcasted_iota(jnp.int32, (2 * SPAN, CHUNK), 0)
        lane = lax.broadcasted_iota(jnp.int32, (2 * SPAN, CHUNK), 1)
        upper = row < SPAN
        last = row + (tile - start) * SPAN + jnp.where(upper, 0, SPAN) - lane
        earliest = jnp.where(upper, 0, (next_start - start) * SPAN) - lane

        def rows(j):
            return pl.ds(pl.multiple_of(base + CHUNK * j, 32), CHUNK)

        top = jnp.full((2 * SPAN, 1), NEGATIVE, jnp.float32)
        for j in range(chunks):
            both = lax.dot_general(
                left, key_ref[rows(j), :], (((1,), (1,)), ((), ())),
                preferred_element_type=jnp.float32,
            )
            allowed = earliest <= CHUNK * j
            if j >= chunks - 3:
                allowed = jnp.logical_and(allowed, last >= CHUNK * j)
            scores = jnp.where(allowed, both[: 2 * SPAN], NEGATIVE)
            place = slice(CHUNK * j, CHUNK * j + CHUNK)
            score_ref[:, place] = scores
            prob_grad_ref[:, place] = both[2 * SPAN :]
            top = jnp.maximum(top, jnp.max(scores, axis=1, keepdims=True))
        total = jnp.zeros((2 * SPAN, 1), jnp.float32)
        accum = jnp.zeros((2 * SPAN, 128), jnp.float32)
        for j in range(chunks):
            place = slice(CHUNK * j, CHUNK * j + CHUNK)
            expo = jnp.exp(score_ref[:, place] - top)
            score_ref[:, place] = expo
            total = total + jnp.sum(expo, axis=1, keepdims=True)
            accum = accum + jnp.dot(
                expo.astype(jnp.bfloat16), key_ref[rows(j), :], preferred_element_type=jnp.float32
            )
        inverse = 1.0 / total
        context = (accum / total).astype(jnp.bfloat16)
        delta = jnp.sum(
            grad_only.astype(jnp.float32) * context.astype(jnp.float32), axis=1, keepdims=True
        )
        query_grad = jnp.zeros((2 * SPAN, 128), jnp.float32)
        for j in range(chunks):
            place = slice(CHUNK * j, CHUNK * j + CHUNK)
            probs = score_ref[:, place] * inverse
            score_grad = (probs * (prob_grad_ref[:, place] - delta)).astype(jnp.bfloat16)
            query_grad = query_grad + jnp.dot(
                score_grad, key_ref[rows(j), :], preferred_element_type=jnp.float32
            )
            stacked = jnp.concatenate([probs.astype(jnp.bfloat16), score_grad], axis=0)
            grad_ref[rows(j), :] += lax.dot_general(
                stacked, right, (((0,), (0,)), ((), ())), preferred_element_type=jnp.float32
            )
        merged = jnp.where(low, query_grad * HEAD ** -0.5, context.astype(jnp.float32)).astype(jnp.bfloat16)
        out_ref[ranks[0]] = merged[:SPAN]
        out_ref[ranks[1]] = merged[SPAN:]

    def one_step(step, carry):
        tile = core + 4 * step
        chunks = ((tile + 3 - tile_start(tile)) * SPAN + CHUNK - 1) // CHUNK
        for count in range(2, 8):
            @pl.when(chunks == count)
            def _():
                two_tiles(tile, count)
        return carry

    lax.fori_loop(0, TILES // 4, one_step, 0)
    for rank in range(RANKS):
        tile = own_tile(rank)
        own_grad_ref[rank] = grad_ref[tile_rows(tile), :]
        other_grad_ref[rank] = grad_ref[tile_rows(TILES - 1 - tile), :].astype(jnp.bfloat16)


def attend(core, tiles, own, other):
    smem = pl.BlockSpec(memory_space=pltpu.SMEM)
    vmem = pl.BlockSpec(memory_space=pltpu.VMEM)
    block = (RANKS, SPAN, 128)
    return pl.pallas_call(
        attend_kernel,
        out_shape=(
            jax.ShapeDtypeStruct(block, jnp.bfloat16),
            jax.ShapeDtypeStruct(block, jnp.float32),
            jax.ShapeDtypeStruct(block, jnp.bfloat16),
        ),
        in_specs=[smem, smem, vmem, vmem],
        out_specs=(vmem, vmem, vmem),
        scratch_shapes=[
            pltpu.VMEM((KEY_ROWS, 128), jnp.bfloat16),
            pltpu.VMEM((KEY_ROWS, 128), jnp.float32),
            pltpu.VMEM((2 * SPAN, 7 * CHUNK), jnp.float32),
            pltpu.VMEM((2 * SPAN, 7 * CHUNK), jnp.float32),
        ],
        compiler_params=pltpu.CompilerParams(vmem_limit_bytes=VMEM_LIMIT),
        name="attend",
    )(core, tiles, own, other)


def weight_kernel(place_ref, grads_ref, *refs):
    line_refs, (keep_ref, give_ref, held_ref) = refs[:4], refs[4:]
    core, column = place_ref[0], place_ref[1]

    @pl.when(pl.program_id(0) == 0)
    def _():
        for shift in range(4):
            chip = jnp.bitwise_and(column + 4 - shift, 3)
            for part in range(2):
                sequence = jnp.bitwise_xor(core, part)
                first = (2 * shift + part) * SPAN
                for head in range(2):
                    for half in range(2):
                        lanes = 128 * (2 * half + head)
                        held_ref[first : first + SPAN, lanes : lanes + 128] = grads_ref[
                            chip, head, sequence, SPAN * half : SPAN * half + SPAN, :
                        ]

    def product(kind, columns):
        rows = jnp.concatenate([ref[part, kind] for ref in line_refs for part in range(2)], axis=0)
        return lax.dot_general(
            rows, held_ref[:, :columns], (((0,), (0,)), ((), ())), preferred_element_type=jnp.float32
        )

    by_tokens = product(0, 512)
    by_upstream = product(1, 256)
    low = low_lanes(D // 4)
    firsts = [
        jnp.where(low, by_tokens[:, 128 * i : 128 * i + 128], by_upstream[:, 128 * i : 128 * i + 128])
        for i in range(2)
    ]
    seconds = [by_tokens[:, 256:384], by_tokens[:, 384:]]
    for lanes, (zero, one) in ((slice(0, 128), firsts), (slice(128, 256), seconds)):
        kept = jnp.where(core == 0, zero, one).astype(jnp.bfloat16)
        given = jnp.where(core == 0, one, zero).astype(jnp.bfloat16)
        keep_ref[:, :, lanes] = kept.reshape(4, 64, 128)
        give_ref[:, :, lanes] = given.reshape(4, 64, 128)


def weight_terms(place, grads, lines):
    shape = jax.ShapeDtypeStruct((RANKS, 64, 256), jnp.bfloat16)
    line_spec = pl.BlockSpec((2, 2, SPAN, D // 4), lambda j, place: (0, 0, 0, j))
    out_spec = pl.BlockSpec((4, 64, 256), lambda j, place: (j, 0, 0))
    return pl.pallas_call(
        weight_kernel,
        out_shape=(shape, shape),
        grid_spec=pltpu.PrefetchScalarGridSpec(
            num_scalar_prefetch=1,
            grid=(4,),
            in_specs=[
                pl.BlockSpec((4, 2, 2, 2 * SPAN, 128), lambda j, place: (0, 0, 0, 0, 0)),
                line_spec, line_spec, line_spec, line_spec,
            ],
            out_specs=(out_spec, out_spec),
            scratch_shapes=[pltpu.VMEM((8 * SPAN, 512), jnp.bfloat16)],
        ),
        compiler_params=pltpu.CompilerParams(vmem_limit_bytes=VMEM_LIMIT),
        name="weight_terms",
    )(place, grads, *lines)


def spread_kernel(parts_ref, out_ref):
    low = low_lanes(64)
    factor = float(16 * RANKS * 2 * SPAN) ** -0.5
    for column in range(4):
        columns = slice(128 * column, 128 * column + 128)
        for half, (lower, upper) in enumerate(((0, 3), (1, 2))):
            lanes = slice(128 * half, 128 * half + 128)
            one, two = (
                factor
                * (
                    parts_ref[column, 0, core, :, lanes].astype(jnp.float32)
                    + parts_ref[column, 1, core, :, lanes].astype(jnp.float32)
                )
                for core in range(2)
            )
            out_ref[lower, :, columns] = jnp.where(low, one, pltpu.roll(two, HEAD, 1)).astype(
                jnp.bfloat16
            )
            out_ref[upper, :, columns] = jnp.where(low, pltpu.roll(one, HEAD, 1), two).astype(
                jnp.bfloat16
            )


def spread_heads(parts):
    return pl.pallas_call(
        spread_kernel,
        out_shape=jax.ShapeDtypeStruct((4, 64, HQ), jnp.bfloat16),
        name="spread_heads",
    )(parts)


def output_kernel(place_ref, grads_ref, arrived_ref, weights_ref, out_ref, input_grad_ref, held_ref):
    core, odd = place_ref[0], place_ref[1]

    @pl.when(pl.program_id(0) == 0)
    def _():
        low = low_lanes(SPAN)
        for block in range(2):
            holder = jnp.bitwise_xor(odd, block)
            rows = slice(SPAN * block, SPAN * block + SPAN)
            for half in range(2):
                place = slice(SPAN * half, SPAN * half + SPAN)
                for pair in range(HEADS // 2):
                    columns = slice(128 * pair, 128 * pair + 128)
                    one, two = (
                        jnp.where(
                            holder == core,
                            grads_ref[head, 0, place, :].astype(jnp.float32),
                            arrived_ref[head, place, :].astype(jnp.float32),
                        )
                        for head in (2 * pair, 2 * pair + 1)
                    )
                    held_ref[2 * half, rows, columns] = jnp.where(
                        low, one, pltpu.roll(two, HEAD, 1)
                    ).astype(jnp.bfloat16)
                    held_ref[2 * half + 1, rows, columns] = jnp.where(
                        low, pltpu.roll(one, HEAD, 1), two
                    ).astype(jnp.bfloat16)

    def product(number, weight):
        return lax.dot_general(
            held_ref[number], weights_ref[weight], (((1,), (1,)), ((), ())),
            preferred_element_type=jnp.float32,
        )

    out_ref[...] = product(1, 3).astype(jnp.bfloat16).reshape(2, SPAN, D // 4)
    input_grad = product(0, 0) + product(2, 1) + product(3, 2)
    input_grad_ref[...] = input_grad.astype(jnp.bfloat16).reshape(2, SPAN, D // 4)


def outputs(place, grads, arrived, weights):
    shape = jax.ShapeDtypeStruct((2, SPAN, D), jnp.bfloat16)
    out_spec = pl.BlockSpec((2, SPAN, D // 4), lambda j, place: (0, 0, j))
    return pl.pallas_call(
        output_kernel,
        out_shape=(shape, shape),
        grid_spec=pltpu.PrefetchScalarGridSpec(
            num_scalar_prefetch=1,
            grid=(4,),
            in_specs=[
                pl.BlockSpec((HEADS, 1, 2 * SPAN, 128), lambda j, place: (0, place[0], 0, 0)),
                pl.BlockSpec((HEADS, 2 * SPAN, 128), lambda j, place: (0, 0, 0)),
                pl.BlockSpec((4, D // 4, HQ), lambda j, place: (0, j, 0)),
            ],
            out_specs=(out_spec, out_spec),
            scratch_shapes=[pltpu.VMEM((4, 2 * SPAN, HQ), jnp.bfloat16)],
        ),
        compiler_params=pltpu.CompilerParams(vmem_limit_bytes=VMEM_LIMIT),
        cost_estimate=pl.CostEstimate(
            flops=8 * 2 * SPAN * D * HQ, bytes_accessed=7 * 1024 * 1024, transcendentals=0
        ),
        name="outputs",
    )(place, grads, arrived, weights)


def per_device(tokens, sweep_tiles, weights, cotangent):
    core = lax.axis_index("dp") % 2
    column = lax.axis_index("dp") // 4
    rank = lax.axis_index("ctx")
    odd = rank % 2
    block = jnp.bitwise_xor(core, odd)

    rows = tokens.reshape(2, SPAN, D)
    upstream = cotangent.reshape(2, SPAN, D)
    other_rows = lax.ppermute(rows, "dp", CORE_SWAP)
    other_upstream = lax.ppermute(upstream, "dp", CORE_SWAP)
    other_tiles = lax.ppermute(sweep_tiles, "dp", CORE_SWAP)
    core_number = core.astype(jnp.int32).reshape(1)
    filled = project(
        jnp.stack([block, core]).astype(jnp.int32), 0, rows, upstream, weights
    )
    packed, line = project(
        jnp.stack([block, 1 - core]).astype(jnp.int32),
        1, other_rows, other_upstream, weights, *filled,
    )
    packed = packed.reshape(RANKS, 2 * SPAN, 128)
    shifted = [lax.ppermute(line, "dp", shift) for shift in X_SHIFTS]
    own = lax.all_to_all(packed, "ctx", 0, 0)
    near, far, back_near = shifted
    own, near, back_near = lax.optimization_barrier((own, near, back_near))
    other = lax.ppermute(own[:, SPAN:], "dp", CORE_SWAP)
    tiles = jnp.where(odd == core, sweep_tiles, other_tiles).reshape(-1)
    query_part, own_grad, other_grad = attend(core_number, tiles, own, other)
    arrived = lax.ppermute(other_grad, "dp", CORE_SWAP)
    key_part = (own_grad + arrived.astype(jnp.float32)).astype(jnp.bfloat16)
    back = lax.all_to_all(jnp.concatenate([query_part, key_part], axis=1), "ctx", 0, 0)
    back, far = lax.optimization_barrier((back, far))
    grads = back.reshape(HEADS, 2, 2 * SPAN, 128)
    lines = [line, near, far, back_near]
    line_grads = lax.all_to_all(
        back.reshape(4, 2, 2, 2 * SPAN, 128), "dp", 0, 0, axis_index_groups=CHIP_LINES
    )
    keep, give = weight_terms(
        jnp.stack([core, column]).astype(jnp.int32), line_grads, lines
    )
    given = lax.ppermute(give, "dp", CORE_SWAP)
    terms = (keep.astype(jnp.float32) + given.astype(jnp.float32)).astype(jnp.bfloat16)
    terms, own_grads = lax.optimization_barrier((terms, grads))
    terms = lax.all_to_all(terms, "ctx", 0, 0)
    swapped = lax.ppermute(
        lax.dynamic_index_in_dim(grads, 1 - core, 1, keepdims=False), "dp", CORE_SWAP
    )
    place = jnp.stack([core, odd]).astype(jnp.int32)
    attn_out, input_grad = outputs(place, own_grads, swapped, weights)
    terms, attn_out, input_grad = lax.optimization_barrier((terms, attn_out, input_grad))
    rows = jnp.sum(terms.astype(jnp.float32), axis=0).astype(jnp.bfloat16)
    parts = lax.all_to_all(jnp.broadcast_to(rows, (16, 64, 256)), "dp", 0, 0)
    weight_grads = spread_heads(parts.reshape(4, 2, 2, 64, 256))
    return (attn_out.reshape(tokens.shape), input_grad.reshape(tokens.shape), weight_grads)


def solution(mesh):
    placed = (
        P("dp", "ctx", None, None, None),
        P("dp", None),
        P(),
        P("dp", "ctx", None, None, None),
    )
    return jax.shard_map(
        per_device,
        mesh=mesh,
        in_specs=placed,
        out_specs=(
            P("dp", "ctx", None, None, None),
            P("dp", "ctx", None, None, None),
            P(None, "ctx", None),
        ),
        check_vma=False,
    )
```

```python
import jax
import jax.numpy as jnp
from jax import lax
from jax.experimental import pallas as pl
from jax.experimental.pallas import tpu as pltpu
from jax.sharding import PartitionSpec as P

D = 1024
HEADS = 8
HEAD = 64
HQ = HEADS * HEAD
SPAN = 96
RANKS = 16
TILES = 2 * RANKS
CHUNK = 256
KEY_ROWS = TILES * SPAN + CHUNK
NEGATIVE = -1e30
SMALL_VMEM = 24 * 1024 * 1024
STAGE_VMEM = 47 * 1024 * 1024

CORE_SWAP = [(i, i ^ 1) for i in range(16)]
CHIP_LINES = [[4 * x + rest for x in range(4)] for rest in range(4)]
X_SHIFTS = [[(i, (i + 4 * shift) % 16) for i in range(16)] for shift in range(1, 4)]


def low_lanes(rows):
    return lax.broadcasted_iota(jnp.int32, (rows, 128), 1) < HEAD


def stage_kernel(weights_ref, held_ref, sem):
    copy = pltpu.make_async_copy(weights_ref, held_ref, sem)
    copy.start()
    copy.wait()


def stage(weights):
    return pl.pallas_call(
        stage_kernel,
        out_shape=jax.ShapeDtypeStruct(weights.shape, weights.dtype),
        in_specs=[pl.BlockSpec(memory_space=pl.ANY)],
        out_specs=pl.BlockSpec(memory_space=pltpu.VMEM),
        scratch_shapes=[pltpu.SemaphoreType.DMA],
        compiler_params=pltpu.CompilerParams(vmem_limit_bytes=STAGE_VMEM),
        name="stage",
    )(weights)


def project_kernel(place_ref, mine_ref, other_ref, weights_ref, out_ref, line_ref):
    core, block = place_ref[0], place_ref[1]
    inputs, upstream = (
        jnp.concatenate([mine_ref[kind, block], other_ref[kind, block]], axis=0)
        for kind in range(2)
    )
    for part in range(2):
        rows = slice(SPAN * part, SPAN * part + SPAN)
        line_ref[part, 0] = inputs[rows]
        line_ref[part, 1] = upstream[rows]
    low = low_lanes(2 * SPAN)
    for quarter in range(2):
        columns = slice(256 * quarter, 256 * quarter + 256)

        def product(rows, number):
            return jnp.dot(
                rows, weights_ref[number, :, columns], preferred_element_type=jnp.float32
            )

        queries, keys, values = (product(inputs, number) for number in range(3))
        grads = product(upstream, 3)
        for half, (first, second) in enumerate(((queries, grads), (keys, values))):
            place = slice(SPAN * half, SPAN * half + SPAN)
            for pair in range(2):
                one = first[:, 128 * pair : 128 * pair + 128]
                two = second[:, 128 * pair : 128 * pair + 128]
                even = jnp.where(low, one, pltpu.roll(two, HEAD, 1)).astype(jnp.bfloat16)
                odd = jnp.where(low, pltpu.roll(one, HEAD, 1), two).astype(jnp.bfloat16)
                head = 4 * quarter + 2 * pair
                for part in range(2):
                    rows = slice(SPAN * part, SPAN * part + SPAN)
                    sequence = jnp.bitwise_xor(core, part)
                    out_ref[head, sequence, place, :] = even[rows]
                    out_ref[head + 1, sequence, place, :] = odd[rows]


def project(place, mine, other, weights):
    vmem = pl.BlockSpec(memory_space=pltpu.VMEM)
    return pl.pallas_call(
        project_kernel,
        out_shape=(
            jax.ShapeDtypeStruct((HEADS, 2, 2 * SPAN, 128), jnp.bfloat16),
            jax.ShapeDtypeStruct((2, 2, SPAN, D), jnp.bfloat16),
        ),
        in_specs=[pl.BlockSpec(memory_space=pltpu.SMEM), vmem, vmem, vmem],
        out_specs=(vmem, vmem),
        compiler_params=pltpu.CompilerParams(vmem_limit_bytes=SMALL_VMEM),
        name="project",
    )(place, mine, other, weights)


def attend_kernel(
    core_ref, tiles_ref, own_ref, other_ref, out_ref, own_grad_ref, other_grad_ref,
    key_ref, grad_ref, score_ref, prob_grad_ref,
):
    core = core_ref[0]
    first = tiles_ref[0]
    second = first + tiles_ref[1]
    third = second + tiles_ref[2]
    grad_ref[...] = jnp.zeros_like(grad_ref)
    key_ref[TILES * SPAN :, :] = jnp.zeros((CHUNK, 128), jnp.bfloat16)

    def own_tile(rank):
        return jnp.where(rank % 2 == core, rank, TILES - 1 - rank)

    def tile_rows(tile):
        return pl.ds(pl.multiple_of(tile * SPAN, SPAN), SPAN)

    for rank in range(RANKS):
        tile = own_tile(rank)
        key_ref[tile_rows(tile), :] = own_ref[rank, SPAN:, :]
        key_ref[tile_rows(TILES - 1 - tile), :] = other_ref[rank]


    def tile_start(tile):
        return jnp.where(
            tile >= third, third, jnp.where(tile >= second, second, jnp.where(tile >= first, first, 0))
        )

    def holder(tile):
        return jnp.where(tile < RANKS, tile, TILES - 1 - tile)

    def two_tiles(tile, chunks):
        start, next_start = tile_start(tile), tile_start(tile + 2)
        base = pl.multiple_of(start * SPAN, SPAN)
        ranks = (holder(tile), holder(tile + 2))
        packed = jnp.concatenate([own_ref[rank, :SPAN, :] for rank in ranks], axis=0)
        low = low_lanes(2 * SPAN)
        query_only = jnp.where(low, packed, jnp.zeros_like(packed)) * jnp.bfloat16(HEAD ** -0.5)
        grad_only = jnp.where(low, jnp.zeros_like(packed), packed)
        left = jnp.concatenate([query_only, grad_only], axis=0)
        right = jnp.concatenate([grad_only, query_only], axis=0)
        row = lax.broadcasted_iota(jnp.int32, (2 * SPAN, CHUNK), 0)
        lane = lax.broadcasted_iota(jnp.int32, (2 * SPAN, CHUNK), 1)
        upper = row < SPAN
        last = row + (tile - start) * SPAN + jnp.where(upper, 0, SPAN) - lane
        earliest = jnp.where(upper, 0, (next_start - start) * SPAN) - lane

        def rows(j):
            return pl.ds(pl.multiple_of(base + CHUNK * j, 32), CHUNK)

        top = jnp.full((2 * SPAN, 1), NEGATIVE, jnp.float32)
        for j in range(chunks):
            both = lax.dot_general(
                left, key_ref[rows(j), :], (((1,), (1,)), ((), ())),
                preferred_element_type=jnp.float32,
            )
            allowed = earliest <= CHUNK * j
            if j >= chunks - 3:
                allowed = jnp.logical_and(allowed, last >= CHUNK * j)
            scores = jnp.where(allowed, both[: 2 * SPAN], NEGATIVE)
            place = slice(CHUNK * j, CHUNK * j + CHUNK)
            score_ref[:, place] = scores
            prob_grad_ref[:, place] = both[2 * SPAN :]
            top = jnp.maximum(top, jnp.max(scores, axis=1, keepdims=True))
        total = jnp.zeros((2 * SPAN, 1), jnp.float32)
        accum = jnp.zeros((2 * SPAN, 128), jnp.float32)
        for j in range(chunks):
            place = slice(CHUNK * j, CHUNK * j + CHUNK)
            expo = jnp.exp(score_ref[:, place] - top)
            score_ref[:, place] = expo
            total = total + jnp.sum(expo, axis=1, keepdims=True)
            accum = accum + jnp.dot(
                expo.astype(jnp.bfloat16), key_ref[rows(j), :], preferred_element_type=jnp.float32
            )
        inverse = 1.0 / total
        context = (accum / total).astype(jnp.bfloat16)
        delta = jnp.sum(
            grad_only.astype(jnp.float32) * context.astype(jnp.float32), axis=1, keepdims=True
        )
        query_grad = jnp.zeros((2 * SPAN, 128), jnp.float32)
        for j in range(chunks):
            place = slice(CHUNK * j, CHUNK * j + CHUNK)
            probs = score_ref[:, place] * inverse
            score_grad = (probs * (prob_grad_ref[:, place] - delta)).astype(jnp.bfloat16)
            query_grad = query_grad + jnp.dot(
                score_grad, key_ref[rows(j), :], preferred_element_type=jnp.float32
            )
            stacked = jnp.concatenate([probs.astype(jnp.bfloat16), score_grad], axis=0)
            grad_ref[rows(j), :] += lax.dot_general(
                stacked, right, (((0,), (0,)), ((), ())), preferred_element_type=jnp.float32
            )
        merged = jnp.where(low, query_grad * HEAD ** -0.5, context.astype(jnp.float32)).astype(jnp.bfloat16)
        out_ref[ranks[0]] = merged[:SPAN]
        out_ref[ranks[1]] = merged[SPAN:]

    def one_step(step, carry):
        tile = core + 4 * step
        chunks = ((tile + 3 - tile_start(tile)) * SPAN + CHUNK - 1) // CHUNK
        for count in range(2, 8):
            @pl.when(chunks == count)
            def _():
                two_tiles(tile, count)
        return carry

    lax.fori_loop(0, TILES // 4, one_step, 0)
    for rank in range(RANKS):
        tile = own_tile(rank)
        own_grad_ref[rank] = grad_ref[tile_rows(tile), :]
        other_grad_ref[rank] = grad_ref[tile_rows(TILES - 1 - tile), :].astype(jnp.bfloat16)


def attend(core, tiles, own, other_keys):
    smem = pl.BlockSpec(memory_space=pltpu.SMEM)
    vmem = pl.BlockSpec(memory_space=pltpu.VMEM)
    block = (RANKS, SPAN, 128)
    return pl.pallas_call(
        attend_kernel,
        out_shape=(
            jax.ShapeDtypeStruct(block, jnp.bfloat16),
            jax.ShapeDtypeStruct(block, jnp.float32),
            jax.ShapeDtypeStruct(block, jnp.bfloat16),
        ),
        in_specs=[smem, smem, vmem, vmem],
        out_specs=(vmem, vmem, vmem),
        scratch_shapes=[
            pltpu.VMEM((KEY_ROWS, 128), jnp.bfloat16),
            pltpu.VMEM((KEY_ROWS, 128), jnp.float32),
            pltpu.VMEM((2 * SPAN, 7 * CHUNK), jnp.float32),
            pltpu.VMEM((2 * SPAN, 7 * CHUNK), jnp.float32),
        ],
        compiler_params=pltpu.CompilerParams(vmem_limit_bytes=SMALL_VMEM),
        name="attend",
    )(core, tiles, own, other_keys)


def weight_kernel(place_ref, grads_ref, *refs):
    line_refs, (keep_ref, give_ref, held_ref) = refs[:4], refs[4:]
    core, column = place_ref[0], place_ref[1]

    @pl.when(pl.program_id(0) == 0)
    def _():
        for shift in range(4):
            chip = jnp.bitwise_and(column + 4 - shift, 3)
            for part in range(2):
                sequence = jnp.bitwise_xor(core, part)
                first = (2 * shift + part) * SPAN
                for head in range(2):
                    for half in range(2):
                        lanes = 128 * (2 * half + head)
                        held_ref[first : first + SPAN, lanes : lanes + 128] = grads_ref[
                            chip, head, sequence, SPAN * half : SPAN * half + SPAN, :
                        ]

    def product(kind, columns):
        rows = jnp.concatenate([ref[part, kind] for ref in line_refs for part in range(2)], axis=0)
        return lax.dot_general(
            rows, held_ref[:, :columns], (((0,), (0,)), ((), ())), preferred_element_type=jnp.float32
        )

    by_tokens = product(0, 512)
    by_upstream = product(1, 256)
    low = low_lanes(D // 4)
    firsts = [
        jnp.where(low, by_tokens[:, 128 * i : 128 * i + 128], by_upstream[:, 128 * i : 128 * i + 128])
        for i in range(2)
    ]
    seconds = [by_tokens[:, 256:384], by_tokens[:, 384:]]
    for lanes, (zero, one) in ((slice(0, 128), firsts), (slice(128, 256), seconds)):
        kept = jnp.where(core == 0, zero, one).astype(jnp.bfloat16)
        given = jnp.where(core == 0, one, zero).astype(jnp.bfloat16)
        keep_ref[:, :, lanes] = kept.reshape(4, 64, 128)
        give_ref[:, :, lanes] = given.reshape(4, 64, 128)


def weight_terms(place, grads, lines):
    shape = jax.ShapeDtypeStruct((RANKS, 64, 256), jnp.bfloat16)
    line_spec = pl.BlockSpec((2, 2, SPAN, D // 4), lambda j, place: (0, 0, 0, j))
    out_spec = pl.BlockSpec((4, 64, 256), lambda j, place: (j, 0, 0))
    return pl.pallas_call(
        weight_kernel,
        out_shape=(shape, shape),
        grid_spec=pltpu.PrefetchScalarGridSpec(
            num_scalar_prefetch=1,
            grid=(4,),
            in_specs=[
                pl.BlockSpec((4, 2, 2, 2 * SPAN, 128), lambda j, place: (0, 0, 0, 0, 0)),
                line_spec, line_spec, line_spec, line_spec,
            ],
            out_specs=(out_spec, out_spec),
            scratch_shapes=[pltpu.VMEM((8 * SPAN, 512), jnp.bfloat16)],
        ),
        compiler_params=pltpu.CompilerParams(vmem_limit_bytes=SMALL_VMEM),
        name="weight_terms",
    )(place, grads, *lines)


def spread_kernel(parts_ref, out_ref):
    low = low_lanes(64)
    factor = float(16 * RANKS * 2 * SPAN) ** -0.5
    for column in range(4):
        columns = slice(128 * column, 128 * column + 128)
        for half, (lower, upper) in enumerate(((0, 3), (1, 2))):
            lanes = slice(128 * half, 128 * half + 128)
            one, two = (
                factor
                * (
                    parts_ref[column, 0, core, :, lanes].astype(jnp.float32)
                    + parts_ref[column, 1, core, :, lanes].astype(jnp.float32)
                )
                for core in range(2)
            )
            out_ref[lower, :, columns] = jnp.where(low, one, pltpu.roll(two, HEAD, 1)).astype(
                jnp.bfloat16
            )
            out_ref[upper, :, columns] = jnp.where(low, pltpu.roll(one, HEAD, 1), two).astype(
                jnp.bfloat16
            )


def spread_heads(parts):
    return pl.pallas_call(
        spread_kernel,
        out_shape=jax.ShapeDtypeStruct((4, 64, HQ), jnp.bfloat16),
        name="spread_heads",
    )(parts)


def output_kernel(place_ref, grads_ref, arrived_ref, weights_ref, out_ref, input_grad_ref, held_ref):
    core, odd = place_ref[0], place_ref[1]

    @pl.when(pl.program_id(0) == 0)
    def _():
        low = low_lanes(SPAN)
        for block in range(2):
            holder = jnp.bitwise_xor(odd, block)
            rows = slice(SPAN * block, SPAN * block + SPAN)
            for half in range(2):
                place = slice(SPAN * half, SPAN * half + SPAN)
                for pair in range(HEADS // 2):
                    columns = slice(128 * pair, 128 * pair + 128)
                    one, two = (
                        jnp.where(
                            holder == core,
                            grads_ref[head, 0, place, :].astype(jnp.float32),
                            arrived_ref[head, place, :].astype(jnp.float32),
                        )
                        for head in (2 * pair, 2 * pair + 1)
                    )
                    held_ref[2 * half, rows, columns] = jnp.where(
                        low, one, pltpu.roll(two, HEAD, 1)
                    ).astype(jnp.bfloat16)
                    held_ref[2 * half + 1, rows, columns] = jnp.where(
                        low, pltpu.roll(one, HEAD, 1), two
                    ).astype(jnp.bfloat16)

    def product(number, weight):
        return lax.dot_general(
            held_ref[number], weights_ref[weight], (((1,), (1,)), ((), ())),
            preferred_element_type=jnp.float32,
        )

    out_ref[...] = product(1, 3).astype(jnp.bfloat16).reshape(2, SPAN, D // 4)
    input_grad = product(0, 0) + product(2, 1) + product(3, 2)
    input_grad_ref[...] = input_grad.astype(jnp.bfloat16).reshape(2, SPAN, D // 4)


def outputs(place, grads, arrived, weights):
    shape = jax.ShapeDtypeStruct((2, SPAN, D), jnp.bfloat16)
    out_spec = pl.BlockSpec((2, SPAN, D // 4), lambda j, place: (0, 0, j))
    return pl.pallas_call(
        output_kernel,
        out_shape=(shape, shape),
        grid_spec=pltpu.PrefetchScalarGridSpec(
            num_scalar_prefetch=1,
            grid=(4,),
            in_specs=[
                pl.BlockSpec((HEADS, 1, 2 * SPAN, 128), lambda j, place: (0, place[0], 0, 0)),
                pl.BlockSpec((HEADS, 2 * SPAN, 128), lambda j, place: (0, 0, 0)),
                pl.BlockSpec((4, D // 4, HQ), lambda j, place: (0, j, 0)),
            ],
            out_specs=(out_spec, out_spec),
            scratch_shapes=[pltpu.VMEM((4, 2 * SPAN, HQ), jnp.bfloat16)],
        ),
        compiler_params=pltpu.CompilerParams(vmem_limit_bytes=SMALL_VMEM),
        cost_estimate=pl.CostEstimate(
            flops=8 * 2 * SPAN * D * HQ, bytes_accessed=7 * 1024 * 1024, transcendentals=0
        ),
        name="outputs",
    )(place, grads, arrived, weights)


def per_device(tokens, sweep_tiles, weights, cotangent):
    core = lax.axis_index("dp") % 2
    column = lax.axis_index("dp") // 4
    rank = lax.axis_index("ctx")
    odd = rank % 2
    block = jnp.bitwise_xor(core, odd)

    mine = jnp.stack([rows.reshape(2, SPAN, D) for rows in (tokens, cotangent)])
    other = lax.ppermute(mine, "dp", CORE_SWAP)
    other_tiles = lax.ppermute(sweep_tiles, "dp", CORE_SWAP)
    core_number = core.astype(jnp.int32).reshape(1)
    packed, line = project(
        jnp.stack([core, block]).astype(jnp.int32), mine, other, stage(weights)
    )
    packed, other_tiles = lax.optimization_barrier((packed, other_tiles))
    packed = packed.reshape(RANKS, 2 * SPAN, 128)
    shifted = [lax.ppermute(line, "dp", shift) for shift in X_SHIFTS]
    own = lax.all_to_all(packed, "ctx", 0, 0)
    near, far, back_near = shifted
    own, near, back_near = lax.optimization_barrier((own, near, back_near))
    other_keys = lax.ppermute(own[:, SPAN:], "dp", CORE_SWAP)
    tiles = jnp.where(odd == core, sweep_tiles, other_tiles).reshape(-1)
    query_part, own_grad, other_grad = attend(core_number, tiles, own, other_keys)
    arrived = lax.ppermute(other_grad, "dp", CORE_SWAP)
    key_part = (own_grad + arrived.astype(jnp.float32)).astype(jnp.bfloat16)
    back = lax.all_to_all(jnp.concatenate([query_part, key_part], axis=1), "ctx", 0, 0)
    back, far = lax.optimization_barrier((back, far))
    grads = back.reshape(HEADS, 2, 2 * SPAN, 128)
    lines = [line, near, far, back_near]
    line_grads = lax.all_to_all(
        back.reshape(4, 2, 2, 2 * SPAN, 128), "dp", 0, 0, axis_index_groups=CHIP_LINES
    )
    keep, give = weight_terms(
        jnp.stack([core, column]).astype(jnp.int32), line_grads, lines
    )
    given = lax.ppermute(give, "dp", CORE_SWAP)
    terms = (keep.astype(jnp.float32) + given.astype(jnp.float32)).astype(jnp.bfloat16)
    terms, own_grads = lax.optimization_barrier((terms, grads))
    terms = lax.all_to_all(terms, "ctx", 0, 0)
    swapped = lax.ppermute(
        lax.dynamic_index_in_dim(grads, 1 - core, 1, keepdims=False), "dp", CORE_SWAP
    )
    place = jnp.stack([core, odd]).astype(jnp.int32)
    attn_out, input_grad = outputs(place, own_grads, swapped, weights)
    terms, attn_out, input_grad = lax.optimization_barrier((terms, attn_out, input_grad))
    rows = jnp.sum(terms.astype(jnp.float32), axis=0).astype(jnp.bfloat16)
    parts = lax.all_to_all(jnp.broadcast_to(rows, (16, 64, 256)), "dp", 0, 0)
    weight_grads = spread_heads(parts.reshape(4, 2, 2, 64, 256))
    return (attn_out.reshape(tokens.shape), input_grad.reshape(tokens.shape), weight_grads)


def solution(mesh):
    placed = (
        P("dp", "ctx", None, None, None),
        P("dp", None),
        P(),
        P("dp", "ctx", None, None, None),
    )
    return jax.shard_map(
        per_device,
        mesh=mesh,
        in_specs=placed,
        out_specs=(
            P("dp", "ctx", None, None, None),
            P("dp", "ctx", None, None, None),
            P(None, "ctx", None),
        ),
        check_vma=False,
    )
```

```python
import jax
import jax.numpy as jnp
from jax import lax
from jax.experimental import pallas as pl
from jax.experimental.pallas import tpu as pltpu
from jax.sharding import PartitionSpec as P

D = 1024
HEADS = 8
HEAD = 64
HQ = HEADS * HEAD
SPAN = 96
RANKS = 16
TILES = 2 * RANKS
CHUNK = 256
KEY_ROWS = TILES * SPAN + CHUNK
NEGATIVE = -1e30
SMALL_VMEM = 24 * 1024 * 1024
PROJECT_VMEM = 60 * 1024 * 1024

CORE_SWAP = [(i, i ^ 1) for i in range(16)]
CHIP_LINES = [[4 * x + rest for x in range(4)] for rest in range(4)]
X_SHIFTS = [[(i, (i + 4 * shift) % 16) for i in range(16)] for shift in range(1, 4)]


def low_lanes(rows):
    return lax.broadcasted_iota(jnp.int32, (rows, 128), 1) < HEAD


def project_kernel(place_ref, tokens_ref, upstream_ref, weights_ref, keep_ref, give_ref):
    keep_first = place_ref[1] == 0
    inputs = tokens_ref[...].reshape(2 * SPAN, D)
    upstream = upstream_ref[...].reshape(2 * SPAN, D)

    def product(rows, number):
        return jnp.dot(rows, weights_ref[number], preferred_element_type=jnp.float32)

    queries, keys, values = (product(inputs, number) for number in range(3))
    grads = product(upstream, 3)
    low = low_lanes(2 * SPAN)
    for half, (first, second) in enumerate(((queries, grads), (keys, values))):
        place = slice(SPAN * half, SPAN * half + SPAN)
        for pair in range(2):
            one = first[:, 128 * pair : 128 * pair + 128]
            two = second[:, 128 * pair : 128 * pair + 128]
            even = jnp.where(low, one, pltpu.roll(two, HEAD, 1))
            odd = jnp.where(low, pltpu.roll(one, HEAD, 1), two)
            for head, rows in ((2 * pair, even), (2 * pair + 1, odd)):
                zero, other = rows[:SPAN], rows[SPAN:]
                keep_ref[head, 0, place, :] = jnp.where(keep_first, zero, other).astype(
                    jnp.bfloat16
                )
                give_ref[head, place, :] = jnp.where(keep_first, other, zero).astype(jnp.bfloat16)


def project(place, tokens, upstream, weights):
    rows_spec = pl.BlockSpec((2, SPAN, D), lambda j, place: (0, 0, 0))
    return pl.pallas_call(
        project_kernel,
        out_shape=(
            jax.ShapeDtypeStruct((HEADS, 2, 2 * SPAN, 128), jnp.bfloat16),
            jax.ShapeDtypeStruct((HEADS, 2 * SPAN, 128), jnp.bfloat16),
        ),
        grid_spec=pltpu.PrefetchScalarGridSpec(
            num_scalar_prefetch=1,
            grid=(2,),
            in_specs=[
                rows_spec,
                rows_spec,
                pl.BlockSpec((4, D, HQ // 2), lambda j, place: (0, 0, j)),
            ],
            out_specs=(
                pl.BlockSpec((HEADS // 2, 1, 2 * SPAN, 128), lambda j, place: (j, place[0], 0, 0)),
                pl.BlockSpec((HEADS // 2, 2 * SPAN, 128), lambda j, place: (j, 0, 0)),
            ),
        ),
        compiler_params=pltpu.CompilerParams(vmem_limit_bytes=PROJECT_VMEM),
        name="project",
    )(place, tokens, upstream, weights)


def attend_kernel(
    core_ref, tiles_ref, own_ref, other_ref, out_ref, own_grad_ref, other_grad_ref,
    key_ref, grad_ref, score_ref, prob_grad_ref,
):
    core = core_ref[0]
    first = tiles_ref[0]
    second = first + tiles_ref[1]
    third = second + tiles_ref[2]
    grad_ref[...] = jnp.zeros_like(grad_ref)
    key_ref[TILES * SPAN :, :] = jnp.zeros((CHUNK, 128), jnp.bfloat16)

    def own_tile(rank):
        return jnp.where(rank % 2 == core, rank, TILES - 1 - rank)

    def tile_rows(tile):
        return pl.ds(pl.multiple_of(tile * SPAN, SPAN), SPAN)

    for rank in range(RANKS):
        tile = own_tile(rank)
        key_ref[tile_rows(tile), :] = own_ref[rank, SPAN:, :]
        key_ref[tile_rows(TILES - 1 - tile), :] = other_ref[rank]


    def tile_start(tile):
        return jnp.where(
            tile >= third, third, jnp.where(tile >= second, second, jnp.where(tile >= first, first, 0))
        )

    def holder(tile):
        return jnp.where(tile < RANKS, tile, TILES - 1 - tile)

    def two_tiles(tile, chunks):
        start, next_start = tile_start(tile), tile_start(tile + 2)
        base = pl.multiple_of(start * SPAN, SPAN)
        ranks = (holder(tile), holder(tile + 2))
        packed = jnp.concatenate([own_ref[rank, :SPAN, :] for rank in ranks], axis=0)
        low = low_lanes(2 * SPAN)
        query_only = jnp.where(low, packed, jnp.zeros_like(packed)) * jnp.bfloat16(HEAD ** -0.5)
        grad_only = jnp.where(low, jnp.zeros_like(packed), packed)
        left = jnp.concatenate([query_only, grad_only], axis=0)
        right = jnp.concatenate([grad_only, query_only], axis=0)
        row = lax.broadcasted_iota(jnp.int32, (2 * SPAN, CHUNK), 0)
        lane = lax.broadcasted_iota(jnp.int32, (2 * SPAN, CHUNK), 1)
        upper = row < SPAN
        last = row + (tile - start) * SPAN + jnp.where(upper, 0, SPAN) - lane
        earliest = jnp.where(upper, 0, (next_start - start) * SPAN) - lane

        def rows(j):
            return pl.ds(pl.multiple_of(base + CHUNK * j, 32), CHUNK)

        top = jnp.full((2 * SPAN, 1), NEGATIVE, jnp.float32)
        for j in range(chunks):
            both = lax.dot_general(
                left, key_ref[rows(j), :], (((1,), (1,)), ((), ())),
                preferred_element_type=jnp.float32,
            )
            allowed = earliest <= CHUNK * j
            if j >= chunks - 3:
                allowed = jnp.logical_and(allowed, last >= CHUNK * j)
            scores = jnp.where(allowed, both[: 2 * SPAN], NEGATIVE)
            place = slice(CHUNK * j, CHUNK * j + CHUNK)
            score_ref[:, place] = scores
            prob_grad_ref[:, place] = both[2 * SPAN :]
            top = jnp.maximum(top, jnp.max(scores, axis=1, keepdims=True))
        total = jnp.zeros((2 * SPAN, 1), jnp.float32)
        accum = jnp.zeros((2 * SPAN, 128), jnp.float32)
        for j in range(chunks):
            place = slice(CHUNK * j, CHUNK * j + CHUNK)
            expo = jnp.exp(score_ref[:, place] - top)
            score_ref[:, place] = expo
            total = total + jnp.sum(expo, axis=1, keepdims=True)
            accum = accum + jnp.dot(
                expo.astype(jnp.bfloat16), key_ref[rows(j), :], preferred_element_type=jnp.float32
            )
        inverse = 1.0 / total
        context = (accum / total).astype(jnp.bfloat16)
        delta = jnp.sum(
            grad_only.astype(jnp.float32) * context.astype(jnp.float32), axis=1, keepdims=True
        )
        query_grad = jnp.zeros((2 * SPAN, 128), jnp.float32)
        for j in range(chunks):
            place = slice(CHUNK * j, CHUNK * j + CHUNK)
            probs = score_ref[:, place] * inverse
            score_grad = (probs * (prob_grad_ref[:, place] - delta)).astype(jnp.bfloat16)
            query_grad = query_grad + jnp.dot(
                score_grad, key_ref[rows(j), :], preferred_element_type=jnp.float32
            )
            stacked = jnp.concatenate([probs.astype(jnp.bfloat16), score_grad], axis=0)
            grad_ref[rows(j), :] += lax.dot_general(
                stacked, right, (((0,), (0,)), ((), ())), preferred_element_type=jnp.float32
            )
        merged = jnp.where(low, query_grad * HEAD ** -0.5, context.astype(jnp.float32)).astype(jnp.bfloat16)
        out_ref[ranks[0]] = merged[:SPAN]
        out_ref[ranks[1]] = merged[SPAN:]

    def one_step(step, carry):
        tile = core + 4 * step
        chunks = ((tile + 3 - tile_start(tile)) * SPAN + CHUNK - 1) // CHUNK
        for count in range(2, 8):
            @pl.when(chunks == count)
            def _():
                two_tiles(tile, count)
        return carry

    lax.fori_loop(0, TILES // 4, one_step, 0)
    for rank in range(RANKS):
        tile = own_tile(rank)
        own_grad_ref[rank] = grad_ref[tile_rows(tile), :]
        other_grad_ref[rank] = grad_ref[tile_rows(TILES - 1 - tile), :].astype(jnp.bfloat16)


def attend(core, tiles, own, other_keys):
    smem = pl.BlockSpec(memory_space=pltpu.SMEM)
    vmem = pl.BlockSpec(memory_space=pltpu.VMEM)
    block = (RANKS, SPAN, 128)
    return pl.pallas_call(
        attend_kernel,
        out_shape=(
            jax.ShapeDtypeStruct(block, jnp.bfloat16),
            jax.ShapeDtypeStruct(block, jnp.float32),
            jax.ShapeDtypeStruct(block, jnp.bfloat16),
        ),
        in_specs=[smem, smem, vmem, vmem],
        out_specs=(vmem, vmem, vmem),
        scratch_shapes=[
            pltpu.VMEM((KEY_ROWS, 128), jnp.bfloat16),
            pltpu.VMEM((KEY_ROWS, 128), jnp.float32),
            pltpu.VMEM((2 * SPAN, 7 * CHUNK), jnp.float32),
            pltpu.VMEM((2 * SPAN, 7 * CHUNK), jnp.float32),
        ],
        compiler_params=pltpu.CompilerParams(vmem_limit_bytes=SMALL_VMEM),
        name="attend",
    )(core, tiles, own, other_keys)


def weight_kernel(place_ref, grads_ref, *refs):
    line_refs, (keep_ref, give_ref, held_ref) = refs[:4], refs[4:]
    core, column = place_ref[0], place_ref[1]

    @pl.when(pl.program_id(0) == 0)
    def _():
        for shift in range(4):
            chip = jnp.bitwise_and(column + 4 - shift, 3)
            for part in range(2):
                sequence = jnp.bitwise_xor(core, part)
                first = (2 * shift + part) * SPAN
                for head in range(2):
                    for half in range(2):
                        lanes = 128 * (2 * half + head)
                        held_ref[first : first + SPAN, lanes : lanes + 128] = grads_ref[
                            chip, head, sequence, SPAN * half : SPAN * half + SPAN, :
                        ]

    def product(kind, columns):
        rows = jnp.concatenate([ref[part, kind] for ref in line_refs for part in range(2)], axis=0)
        return lax.dot_general(
            rows, held_ref[:, :columns], (((0,), (0,)), ((), ())), preferred_element_type=jnp.float32
        )

    by_tokens = product(0, 512)
    by_upstream = product(1, 256)
    low = low_lanes(D // 4)
    firsts = [
        jnp.where(low, by_tokens[:, 128 * i : 128 * i + 128], by_upstream[:, 128 * i : 128 * i + 128])
        for i in range(2)
    ]
    seconds = [by_tokens[:, 256:384], by_tokens[:, 384:]]
    for lanes, (zero, one) in ((slice(0, 128), firsts), (slice(128, 256), seconds)):
        kept = jnp.where(core == 0, zero, one).astype(jnp.bfloat16)
        given = jnp.where(core == 0, one, zero).astype(jnp.bfloat16)
        keep_ref[:, :, lanes] = kept.reshape(4, 64, 128)
        give_ref[:, :, lanes] = given.reshape(4, 64, 128)


def weight_terms(place, grads, lines):
    shape = jax.ShapeDtypeStruct((RANKS, 64, 256), jnp.bfloat16)
    line_spec = pl.BlockSpec((2, 2, SPAN, D // 4), lambda j, place: (0, 0, 0, j))
    out_spec = pl.BlockSpec((4, 64, 256), lambda j, place: (j, 0, 0))
    return pl.pallas_call(
        weight_kernel,
        out_shape=(shape, shape),
        grid_spec=pltpu.PrefetchScalarGridSpec(
            num_scalar_prefetch=1,
            grid=(4,),
            in_specs=[
                pl.BlockSpec((4, 2, 2, 2 * SPAN, 128), lambda j, place: (0, 0, 0, 0, 0)),
                line_spec, line_spec, line_spec, line_spec,
            ],
            out_specs=(out_spec, out_spec),
            scratch_shapes=[pltpu.VMEM((8 * SPAN, 512), jnp.bfloat16)],
        ),
        compiler_params=pltpu.CompilerParams(vmem_limit_bytes=SMALL_VMEM),
        name="weight_terms",
    )(place, grads, *lines)


def spread_kernel(parts_ref, out_ref):
    low = low_lanes(64)
    factor = float(16 * RANKS * 2 * SPAN) ** -0.5
    for column in range(4):
        columns = slice(128 * column, 128 * column + 128)
        for half, (lower, upper) in enumerate(((0, 3), (1, 2))):
            lanes = slice(128 * half, 128 * half + 128)
            one, two = (
                factor
                * (
                    parts_ref[column, 0, core, :, lanes].astype(jnp.float32)
                    + parts_ref[column, 1, core, :, lanes].astype(jnp.float32)
                )
                for core in range(2)
            )
            out_ref[lower, :, columns] = jnp.where(low, one, pltpu.roll(two, HEAD, 1)).astype(
                jnp.bfloat16
            )
            out_ref[upper, :, columns] = jnp.where(low, pltpu.roll(one, HEAD, 1), two).astype(
                jnp.bfloat16
            )


def spread_heads(parts):
    return pl.pallas_call(
        spread_kernel,
        out_shape=jax.ShapeDtypeStruct((4, 64, HQ), jnp.bfloat16),
        name="spread_heads",
    )(parts)


def output_kernel(place_ref, grads_ref, arrived_ref, weights_ref, out_ref, input_grad_ref, held_ref):
    core, odd = place_ref[0], place_ref[1]

    @pl.when(pl.program_id(0) == 0)
    def _():
        low = low_lanes(SPAN)
        for block in range(2):
            holder = jnp.bitwise_xor(odd, block)
            rows = slice(SPAN * block, SPAN * block + SPAN)
            for half in range(2):
                place = slice(SPAN * half, SPAN * half + SPAN)
                for pair in range(HEADS // 2):
                    columns = slice(128 * pair, 128 * pair + 128)
                    one, two = (
                        jnp.where(
                            holder == core,
                            grads_ref[head, 0, place, :].astype(jnp.float32),
                            arrived_ref[head, place, :].astype(jnp.float32),
                        )
                        for head in (2 * pair, 2 * pair + 1)
                    )
                    held_ref[2 * half, rows, columns] = jnp.where(
                        low, one, pltpu.roll(two, HEAD, 1)
                    ).astype(jnp.bfloat16)
                    held_ref[2 * half + 1, rows, columns] = jnp.where(
                        low, pltpu.roll(one, HEAD, 1), two
                    ).astype(jnp.bfloat16)

    def product(number, weight):
        return lax.dot_general(
            held_ref[number], weights_ref[weight], (((1,), (1,)), ((), ())),
            preferred_element_type=jnp.float32,
        )

    out_ref[...] = product(1, 3).astype(jnp.bfloat16).reshape(2, SPAN, D // 4)
    input_grad = product(0, 0) + product(2, 1) + product(3, 2)
    input_grad_ref[...] = input_grad.astype(jnp.bfloat16).reshape(2, SPAN, D // 4)


def outputs(place, grads, arrived, weights):
    shape = jax.ShapeDtypeStruct((2, SPAN, D), jnp.bfloat16)
    out_spec = pl.BlockSpec((2, SPAN, D // 4), lambda j, place: (0, 0, j))
    return pl.pallas_call(
        output_kernel,
        out_shape=(shape, shape),
        grid_spec=pltpu.PrefetchScalarGridSpec(
            num_scalar_prefetch=1,
            grid=(4,),
            in_specs=[
                pl.BlockSpec((HEADS, 1, 2 * SPAN, 128), lambda j, place: (0, place[0], 0, 0)),
                pl.BlockSpec((HEADS, 2 * SPAN, 128), lambda j, place: (0, 0, 0)),
                pl.BlockSpec((4, D // 4, HQ), lambda j, place: (0, j, 0)),
            ],
            out_specs=(out_spec, out_spec),
            scratch_shapes=[pltpu.VMEM((4, 2 * SPAN, HQ), jnp.bfloat16)],
        ),
        compiler_params=pltpu.CompilerParams(vmem_limit_bytes=SMALL_VMEM),
        cost_estimate=pl.CostEstimate(
            flops=8 * 2 * SPAN * D * HQ, bytes_accessed=7 * 1024 * 1024, transcendentals=0
        ),
        name="outputs",
    )(place, grads, arrived, weights)


def per_device(tokens, sweep_tiles, weights, cotangent):
    core = lax.axis_index("dp") % 2
    column = lax.axis_index("dp") // 4
    rank = lax.axis_index("ctx")
    odd = rank % 2
    block = jnp.bitwise_xor(core, odd)

    rows = tokens.reshape(2, SPAN, D)
    upstream = cotangent.reshape(2, SPAN, D)
    other_tiles = lax.ppermute(sweep_tiles, "dp", CORE_SWAP)
    core_number = core.astype(jnp.int32).reshape(1)
    packed, give = project(
        jnp.stack([core, block]).astype(jnp.int32), rows, upstream, weights
    )
    given = lax.ppermute(give, "dp", CORE_SWAP)
    packed = lax.dynamic_update_index_in_dim(packed, given, 1 - core, 1)

    def chosen(number):
        return jnp.stack(
            [lax.dynamic_index_in_dim(x, number, 0, keepdims=False) for x in (rows, upstream)]
        )

    line = jnp.stack([chosen(block), lax.ppermute(chosen(1 - block), "dp", CORE_SWAP)])
    packed, other_tiles = lax.optimization_barrier((packed, other_tiles))
    packed = packed.reshape(RANKS, 2 * SPAN, 128)
    shifted = [lax.ppermute(line, "dp", shift) for shift in X_SHIFTS]
    own = lax.all_to_all(packed, "ctx", 0, 0)
    near, far, back_near = shifted
    own, near, back_near = lax.optimization_barrier((own, near, back_near))
    other_keys = lax.ppermute(own[:, SPAN:], "dp", CORE_SWAP)
    tiles = jnp.where(odd == core, sweep_tiles, other_tiles).reshape(-1)
    query_part, own_grad, other_grad = attend(core_number, tiles, own, other_keys)
    arrived = lax.ppermute(other_grad, "dp", CORE_SWAP)
    key_part = (own_grad + arrived.astype(jnp.float32)).astype(jnp.bfloat16)
    back = lax.all_to_all(jnp.concatenate([query_part, key_part], axis=1), "ctx", 0, 0)
    back, far = lax.optimization_barrier((back, far))
    grads = back.reshape(HEADS, 2, 2 * SPAN, 128)
    lines = [line, near, far, back_near]
    line_grads = lax.all_to_all(
        back.reshape(4, 2, 2, 2 * SPAN, 128), "dp", 0, 0, axis_index_groups=CHIP_LINES
    )
    keep, give = weight_terms(
        jnp.stack([core, column]).astype(jnp.int32), line_grads, lines
    )
    given = lax.ppermute(give, "dp", CORE_SWAP)
    terms = (keep.astype(jnp.float32) + given.astype(jnp.float32)).astype(jnp.bfloat16)
    terms, own_grads = lax.optimization_barrier((terms, grads))
    terms = lax.all_to_all(terms, "ctx", 0, 0)
    swapped = lax.ppermute(
        lax.dynamic_index_in_dim(grads, 1 - core, 1, keepdims=False), "dp", CORE_SWAP
    )
    place = jnp.stack([core, odd]).astype(jnp.int32)
    attn_out, input_grad = outputs(place, own_grads, swapped, weights)
    terms, attn_out, input_grad = lax.optimization_barrier((terms, attn_out, input_grad))
    rows = jnp.sum(terms.astype(jnp.float32), axis=0).astype(jnp.bfloat16)
    parts = lax.all_to_all(jnp.broadcast_to(rows, (16, 64, 256)), "dp", 0, 0)
    weight_grads = spread_heads(parts.reshape(4, 2, 2, 64, 256))
    return (attn_out.reshape(tokens.shape), input_grad.reshape(tokens.shape), weight_grads)


def solution(mesh):
    placed = (
        P("dp", "ctx", None, None, None),
        P("dp", None),
        P(),
        P("dp", "ctx", None, None, None),
    )
    return jax.shard_map(
        per_device,
        mesh=mesh,
        in_specs=placed,
        out_specs=(
            P("dp", "ctx", None, None, None),
            P("dp", "ctx", None, None, None),
            P(None, "ctx", None),
        ),
        check_vma=False,
    )
```

```python
import jax
import jax.numpy as jnp
from jax import lax
from jax.experimental import pallas as pl
from jax.experimental.pallas import tpu as pltpu
from jax.sharding import PartitionSpec as P

D = 1024
HEADS = 8
HEAD = 64
HQ = HEADS * HEAD
SPAN = 96
RANKS = 16
TILES = 2 * RANKS
CHUNK = 256
KEY_ROWS = TILES * SPAN + CHUNK
NEGATIVE = -1e30
SMALL_VMEM = 24 * 1024 * 1024
PROJECT_VMEM = 60 * 1024 * 1024

CORE_SWAP = [(i, i ^ 1) for i in range(16)]
CHIP_LINES = [[4 * x + rest for x in range(4)] for rest in range(4)]
X_SHIFTS = [[(i, (i + 4 * shift) % 16) for i in range(16)] for shift in range(1, 4)]


def low_lanes(rows):
    return lax.broadcasted_iota(jnp.int32, (rows, 128), 1) < HEAD


def project_kernel(place_ref, tokens_ref, upstream_ref, weights_ref, keep_ref, give_ref):
    keep_first = place_ref[1] == 0
    inputs = tokens_ref[...].reshape(2 * SPAN, D)
    upstream = upstream_ref[...].reshape(2 * SPAN, D)

    def product(rows, number):
        return jnp.dot(rows, weights_ref[number], preferred_element_type=jnp.float32)

    queries, keys, values = (product(inputs, number) for number in range(3))
    grads = product(upstream, 3)
    low = low_lanes(2 * SPAN)
    for half, (first, second) in enumerate(((queries, grads), (keys, values))):
        place = slice(SPAN * half, SPAN * half + SPAN)
        for pair in range(2):
            one = first[:, 128 * pair : 128 * pair + 128]
            two = second[:, 128 * pair : 128 * pair + 128]
            even = jnp.where(low, one, pltpu.roll(two, HEAD, 1))
            odd = jnp.where(low, pltpu.roll(one, HEAD, 1), two)
            for head, rows in ((2 * pair, even), (2 * pair + 1, odd)):
                zero, other = rows[:SPAN], rows[SPAN:]
                keep_ref[head, 0, place, :] = jnp.where(keep_first, zero, other).astype(
                    jnp.bfloat16
                )
                give_ref[head, place, :] = jnp.where(keep_first, other, zero).astype(jnp.bfloat16)


def project(place, tokens, upstream, weights):
    rows_spec = pl.BlockSpec((2, SPAN, D), lambda j, place: (0, 0, 0))
    return pl.pallas_call(
        project_kernel,
        out_shape=(
            jax.ShapeDtypeStruct((HEADS, 2, 2 * SPAN, 128), jnp.bfloat16),
            jax.ShapeDtypeStruct((HEADS, 2 * SPAN, 128), jnp.bfloat16),
        ),
        grid_spec=pltpu.PrefetchScalarGridSpec(
            num_scalar_prefetch=1,
            grid=(2,),
            in_specs=[
                rows_spec,
                rows_spec,
                pl.BlockSpec((4, D, HQ // 2), lambda j, place: (0, 0, j)),
            ],
            out_specs=(
                pl.BlockSpec((HEADS // 2, 1, 2 * SPAN, 128), lambda j, place: (j, place[0], 0, 0)),
                pl.BlockSpec((HEADS // 2, 2 * SPAN, 128), lambda j, place: (j, 0, 0)),
            ),
        ),
        compiler_params=pltpu.CompilerParams(vmem_limit_bytes=PROJECT_VMEM),
        name="project",
    )(place, tokens, upstream, weights)


def attend_kernel(
    core_ref, tiles_ref, own_ref, other_ref, out_ref, own_grad_ref, other_grad_ref,
    key_ref, grad_ref, score_ref, prob_grad_ref,
):
    core = core_ref[0]
    first = tiles_ref[0]
    second = first + tiles_ref[1]
    third = second + tiles_ref[2]
    grad_ref[...] = jnp.zeros_like(grad_ref)
    key_ref[TILES * SPAN :, :] = jnp.zeros((CHUNK, 128), jnp.bfloat16)

    def own_tile(rank):
        return jnp.where(rank % 2 == core, rank, TILES - 1 - rank)

    def tile_rows(tile):
        return pl.ds(pl.multiple_of(tile * SPAN, SPAN), SPAN)

    for rank in range(RANKS):
        tile = own_tile(rank)
        key_ref[tile_rows(tile), :] = own_ref[rank, SPAN:, :]
        key_ref[tile_rows(TILES - 1 - tile), :] = other_ref[rank]


    def tile_start(tile):
        return jnp.where(
            tile >= third, third, jnp.where(tile >= second, second, jnp.where(tile >= first, first, 0))
        )

    def holder(tile):
        return jnp.where(tile < RANKS, tile, TILES - 1 - tile)

    def two_tiles(tile, chunks):
        start, next_start = tile_start(tile), tile_start(tile + 2)
        base = pl.multiple_of(start * SPAN, SPAN)
        ranks = (holder(tile), holder(tile + 2))
        packed = jnp.concatenate([own_ref[rank, :SPAN, :] for rank in ranks], axis=0)
        low = low_lanes(2 * SPAN)
        query_only = jnp.where(low, packed, jnp.zeros_like(packed)) * jnp.bfloat16(HEAD ** -0.5)
        grad_only = jnp.where(low, jnp.zeros_like(packed), packed)
        left = jnp.concatenate([query_only, grad_only], axis=0)
        right = jnp.concatenate([grad_only, query_only], axis=0)
        row = lax.broadcasted_iota(jnp.int32, (2 * SPAN, CHUNK), 0)
        lane = lax.broadcasted_iota(jnp.int32, (2 * SPAN, CHUNK), 1)
        upper = row < SPAN
        last = row + (tile - start) * SPAN + jnp.where(upper, 0, SPAN) - lane
        earliest = jnp.where(upper, 0, (next_start - start) * SPAN) - lane

        def rows(j):
            return pl.ds(pl.multiple_of(base + CHUNK * j, 32), CHUNK)

        top = jnp.full((2 * SPAN, 1), NEGATIVE, jnp.float32)
        for j in range(chunks):
            both = lax.dot_general(
                left, key_ref[rows(j), :], (((1,), (1,)), ((), ())),
                preferred_element_type=jnp.float32,
            )
            allowed = earliest <= CHUNK * j
            if j >= chunks - 3:
                allowed = jnp.logical_and(allowed, last >= CHUNK * j)
            scores = jnp.where(allowed, both[: 2 * SPAN], NEGATIVE)
            place = slice(CHUNK * j, CHUNK * j + CHUNK)
            score_ref[:, place] = scores
            prob_grad_ref[:, place] = both[2 * SPAN :]
            top = jnp.maximum(top, jnp.max(scores, axis=1, keepdims=True))
        total = jnp.zeros((2 * SPAN, 1), jnp.float32)
        accum = jnp.zeros((2 * SPAN, 128), jnp.float32)
        for j in range(chunks):
            place = slice(CHUNK * j, CHUNK * j + CHUNK)
            expo = jnp.exp(score_ref[:, place] - top)
            score_ref[:, place] = expo
            total = total + jnp.sum(expo, axis=1, keepdims=True)
            accum = accum + jnp.dot(
                expo.astype(jnp.bfloat16), key_ref[rows(j), :], preferred_element_type=jnp.float32
            )
        inverse = 1.0 / total
        context = (accum / total).astype(jnp.bfloat16)
        delta = jnp.sum(
            grad_only.astype(jnp.float32) * context.astype(jnp.float32), axis=1, keepdims=True
        )
        query_grad = jnp.zeros((2 * SPAN, 128), jnp.float32)
        for j in range(chunks):
            place = slice(CHUNK * j, CHUNK * j + CHUNK)
            probs = score_ref[:, place] * inverse
            score_grad = (probs * (prob_grad_ref[:, place] - delta)).astype(jnp.bfloat16)
            query_grad = query_grad + jnp.dot(
                score_grad, key_ref[rows(j), :], preferred_element_type=jnp.float32
            )
            stacked = jnp.concatenate([probs.astype(jnp.bfloat16), score_grad], axis=0)
            grad_ref[rows(j), :] += lax.dot_general(
                stacked, right, (((0,), (0,)), ((), ())), preferred_element_type=jnp.float32
            )
        merged = jnp.where(low, query_grad * HEAD ** -0.5, context.astype(jnp.float32)).astype(jnp.bfloat16)
        out_ref[ranks[0]] = merged[:SPAN]
        out_ref[ranks[1]] = merged[SPAN:]

    def one_step(step, carry):
        tile = core + 4 * step
        chunks = ((tile + 3 - tile_start(tile)) * SPAN + CHUNK - 1) // CHUNK
        for count in range(2, 8):
            @pl.when(chunks == count)
            def _():
                two_tiles(tile, count)
        return carry

    lax.fori_loop(0, TILES // 4, one_step, 0)
    for rank in range(RANKS):
        tile = own_tile(rank)
        own_grad_ref[rank] = grad_ref[tile_rows(tile), :]
        other_grad_ref[rank] = grad_ref[tile_rows(TILES - 1 - tile), :].astype(jnp.bfloat16)


def attend(core, tiles, own, other_keys):
    smem = pl.BlockSpec(memory_space=pltpu.SMEM)
    vmem = pl.BlockSpec(memory_space=pltpu.VMEM)
    block = (RANKS, SPAN, 128)
    return pl.pallas_call(
        attend_kernel,
        out_shape=(
            jax.ShapeDtypeStruct(block, jnp.bfloat16),
            jax.ShapeDtypeStruct(block, jnp.float32),
            jax.ShapeDtypeStruct(block, jnp.bfloat16),
        ),
        in_specs=[smem, smem, vmem, vmem],
        out_specs=(vmem, vmem, vmem),
        scratch_shapes=[
            pltpu.VMEM((KEY_ROWS, 128), jnp.bfloat16),
            pltpu.VMEM((KEY_ROWS, 128), jnp.float32),
            pltpu.VMEM((2 * SPAN, 7 * CHUNK), jnp.float32),
            pltpu.VMEM((2 * SPAN, 7 * CHUNK), jnp.float32),
        ],
        compiler_params=pltpu.CompilerParams(vmem_limit_bytes=SMALL_VMEM),
        cost_estimate=pl.CostEstimate(
            flops=12_000_000_000, bytes_accessed=4 * 1024 * 1024, transcendentals=0
        ),
        name="attend",
    )(core, tiles, own, other_keys)


def weight_kernel(
    place_ref, grads_ref, own_ref, near_ref, back_ref, far_tokens_ref, far_upstream_ref,
    keep_ref, give_ref, held_ref,
):
    core, column = place_ref[0], place_ref[1]

    @pl.when(pl.program_id(0) == 0)
    def _():
        for shift in range(4):
            chip = jnp.bitwise_and(column + 4 - shift, 3)
            for part in range(2):
                sequence = jnp.bitwise_xor(core, part)
                first = (2 * shift + part) * SPAN
                for head in range(2):
                    for half in range(2):
                        lanes = 128 * (2 * half + head)
                        held_ref[first : first + SPAN, lanes : lanes + 128] = grads_ref[
                            chip, head, sequence, SPAN * half : SPAN * half + SPAN, :
                        ]

    def product(kind, columns):
        far_ref = (far_tokens_ref, far_upstream_ref)[kind]
        lines = (own_ref[kind], near_ref[kind], far_ref[...], back_ref[kind])
        rows = jnp.concatenate([line.reshape(2 * SPAN, D // 4) for line in lines], axis=0)
        return lax.dot_general(
            rows, held_ref[:, :columns], (((0,), (0,)), ((), ())), preferred_element_type=jnp.float32
        )

    by_tokens = product(0, 512)
    by_upstream = product(1, 256)
    low = low_lanes(D // 4)
    firsts = [
        jnp.where(low, by_tokens[:, 128 * i : 128 * i + 128], by_upstream[:, 128 * i : 128 * i + 128])
        for i in range(2)
    ]
    seconds = [by_tokens[:, 256:384], by_tokens[:, 384:]]
    for lanes, (zero, one) in ((slice(0, 128), firsts), (slice(128, 256), seconds)):
        kept = jnp.where(core == 0, zero, one).astype(jnp.bfloat16)
        given = jnp.where(core == 0, one, zero).astype(jnp.bfloat16)
        keep_ref[:, :, lanes] = kept.reshape(4, 64, 128)
        give_ref[:, :, lanes] = given.reshape(4, 64, 128)


def weight_terms(place, grads, lines):
    shape = jax.ShapeDtypeStruct((RANKS, 64, 256), jnp.bfloat16)
    line_spec = pl.BlockSpec((2, 2, SPAN, D // 4), lambda j, place: (0, 0, 0, j))
    half_spec = pl.BlockSpec((2, SPAN, D // 4), lambda j, place: (0, 0, j))
    out_spec = pl.BlockSpec((4, 64, 256), lambda j, place: (j, 0, 0))
    return pl.pallas_call(
        weight_kernel,
        out_shape=(shape, shape),
        grid_spec=pltpu.PrefetchScalarGridSpec(
            num_scalar_prefetch=1,
            grid=(4,),
            in_specs=[
                pl.BlockSpec((4, 2, 2, 2 * SPAN, 128), lambda j, place: (0, 0, 0, 0, 0)),
                line_spec, line_spec, line_spec, half_spec, half_spec,
            ],
            out_specs=(out_spec, out_spec),
            scratch_shapes=[pltpu.VMEM((8 * SPAN, 512), jnp.bfloat16)],
        ),
        compiler_params=pltpu.CompilerParams(vmem_limit_bytes=SMALL_VMEM),
        name="weight_terms",
    )(place, grads, *lines)


def spread_kernel(parts_ref, out_ref):
    low = low_lanes(64)
    factor = float(16 * RANKS * 2 * SPAN) ** -0.5
    for column in range(4):
        columns = slice(128 * column, 128 * column + 128)
        for half, (lower, upper) in enumerate(((0, 3), (1, 2))):
            lanes = slice(128 * half, 128 * half + 128)
            one, two = (
                factor
                * (
                    parts_ref[column, 0, core, :, lanes].astype(jnp.float32)
                    + parts_ref[column, 1, core, :, lanes].astype(jnp.float32)
                )
                for core in range(2)
            )
            out_ref[lower, :, columns] = jnp.where(low, one, pltpu.roll(two, HEAD, 1)).astype(
                jnp.bfloat16
            )
            out_ref[upper, :, columns] = jnp.where(low, pltpu.roll(one, HEAD, 1), two).astype(
                jnp.bfloat16
            )


def spread_heads(parts):
    return pl.pallas_call(
        spread_kernel,
        out_shape=jax.ShapeDtypeStruct((4, 64, HQ), jnp.bfloat16),
        name="spread_heads",
    )(parts)


def output_kernel(place_ref, grads_ref, arrived_ref, weights_ref, out_ref, input_grad_ref, held_ref):
    core, odd = place_ref[0], place_ref[1]

    @pl.when(pl.program_id(0) == 0)
    def _():
        low = low_lanes(SPAN)
        for block in range(2):
            holder = jnp.bitwise_xor(odd, block)
            rows = slice(SPAN * block, SPAN * block + SPAN)
            for half in range(2):
                place = slice(SPAN * half, SPAN * half + SPAN)
                for pair in range(HEADS // 2):
                    columns = slice(128 * pair, 128 * pair + 128)
                    one, two = (
                        jnp.where(
                            holder == core,
                            grads_ref[head, 0, place, :].astype(jnp.float32),
                            arrived_ref[head, place, :].astype(jnp.float32),
                        )
                        for head in (2 * pair, 2 * pair + 1)
                    )
                    held_ref[2 * half, rows, columns] = jnp.where(
                        low, one, pltpu.roll(two, HEAD, 1)
                    ).astype(jnp.bfloat16)
                    held_ref[2 * half + 1, rows, columns] = jnp.where(
                        low, pltpu.roll(one, HEAD, 1), two
                    ).astype(jnp.bfloat16)

    def product(number, weight):
        return lax.dot_general(
            held_ref[number], weights_ref[weight], (((1,), (1,)), ((), ())),
            preferred_element_type=jnp.float32,
        )

    out_ref[...] = product(1, 3).astype(jnp.bfloat16).reshape(2, SPAN, D // 4)
    input_grad = product(0, 0) + product(2, 1) + product(3, 2)
    input_grad_ref[...] = input_grad.astype(jnp.bfloat16).reshape(2, SPAN, D // 4)


def outputs(place, grads, arrived, weights):
    shape = jax.ShapeDtypeStruct((2, SPAN, D), jnp.bfloat16)
    out_spec = pl.BlockSpec((2, SPAN, D // 4), lambda j, place: (0, 0, j))
    return pl.pallas_call(
        output_kernel,
        out_shape=(shape, shape),
        grid_spec=pltpu.PrefetchScalarGridSpec(
            num_scalar_prefetch=1,
            grid=(4,),
            in_specs=[
                pl.BlockSpec((HEADS, 1, 2 * SPAN, 128), lambda j, place: (0, place[0], 0, 0)),
                pl.BlockSpec((HEADS, 2 * SPAN, 128), lambda j, place: (0, 0, 0)),
                pl.BlockSpec((4, D // 4, HQ), lambda j, place: (0, j, 0)),
            ],
            out_specs=(out_spec, out_spec),
            scratch_shapes=[pltpu.VMEM((4, 2 * SPAN, HQ), jnp.bfloat16)],
        ),
        compiler_params=pltpu.CompilerParams(vmem_limit_bytes=SMALL_VMEM),
        cost_estimate=pl.CostEstimate(
            flops=8 * 2 * SPAN * D * HQ, bytes_accessed=7 * 1024 * 1024, transcendentals=0
        ),
        name="outputs",
    )(place, grads, arrived, weights)


def per_device(tokens, sweep_tiles, weights, cotangent):
    core = lax.axis_index("dp") % 2
    column = lax.axis_index("dp") // 4
    rank = lax.axis_index("ctx")
    odd = rank % 2
    block = jnp.bitwise_xor(core, odd)

    rows = tokens.reshape(2, SPAN, D)
    upstream = cotangent.reshape(2, SPAN, D)
    other_tiles = lax.ppermute(sweep_tiles, "dp", CORE_SWAP)
    core_number = core.astype(jnp.int32).reshape(1)
    packed, give = project(
        jnp.stack([core, block]).astype(jnp.int32), rows, upstream, weights
    )
    given = lax.ppermute(give, "dp", CORE_SWAP)
    packed = lax.dynamic_update_index_in_dim(packed, given, 1 - core, 1)

    def chosen(number):
        return jnp.stack(
            [lax.dynamic_index_in_dim(x, number, 0, keepdims=False) for x in (rows, upstream)]
        )

    line = jnp.stack([chosen(block), lax.ppermute(chosen(1 - block), "dp", CORE_SWAP)], axis=1)
    packed, other_tiles = lax.optimization_barrier((packed, other_tiles))
    packed = packed.reshape(RANKS, 2 * SPAN, 128)
    near, back_near = (lax.ppermute(line, "dp", X_SHIFTS[i]) for i in (0, 2))
    far_tokens, far_upstream = (lax.ppermute(half, "dp", X_SHIFTS[1]) for half in line)
    own = lax.all_to_all(packed, "ctx", 0, 0)
    own, far_tokens = lax.optimization_barrier((own, far_tokens))
    other_keys = lax.ppermute(own[:, SPAN:], "dp", CORE_SWAP)
    tiles = jnp.where(odd == core, sweep_tiles, other_tiles).reshape(-1)
    query_part, own_grad, other_grad = attend(core_number, tiles, own, other_keys)
    arrived = lax.ppermute(other_grad, "dp", CORE_SWAP)
    key_part = (own_grad + arrived.astype(jnp.float32)).astype(jnp.bfloat16)
    key_part, near, back_near = lax.optimization_barrier((key_part, near, back_near))
    back = lax.all_to_all(jnp.concatenate([query_part, key_part], axis=1), "ctx", 0, 0)
    back, far_upstream = lax.optimization_barrier((back, far_upstream))
    grads = back.reshape(HEADS, 2, 2 * SPAN, 128)
    lines = [line, near, back_near, far_tokens, far_upstream]
    line_grads = lax.all_to_all(
        back.reshape(4, 2, 2, 2 * SPAN, 128), "dp", 0, 0, axis_index_groups=CHIP_LINES
    )
    keep, give = weight_terms(
        jnp.stack([core, column]).astype(jnp.int32), line_grads, lines
    )
    given = lax.ppermute(give, "dp", CORE_SWAP)
    terms = (keep.astype(jnp.float32) + given.astype(jnp.float32)).astype(jnp.bfloat16)
    terms, own_grads = lax.optimization_barrier((terms, grads))
    terms = lax.all_to_all(terms, "ctx", 0, 0)
    swapped = lax.ppermute(
        lax.dynamic_index_in_dim(grads, 1 - core, 1, keepdims=False), "dp", CORE_SWAP
    )
    place = jnp.stack([core, odd]).astype(jnp.int32)
    attn_out, input_grad = outputs(place, own_grads, swapped, weights)
    terms, attn_out, input_grad = lax.optimization_barrier((terms, attn_out, input_grad))
    rows = jnp.sum(terms.astype(jnp.float32), axis=0).astype(jnp.bfloat16)
    parts = lax.all_to_all(jnp.broadcast_to(rows, (16, 64, 256)), "dp", 0, 0)
    weight_grads = spread_heads(parts.reshape(4, 2, 2, 64, 256))
    return (attn_out.reshape(tokens.shape), input_grad.reshape(tokens.shape), weight_grads)


def solution(mesh):
    placed = (
        P("dp", "ctx", None, None, None),
        P("dp", None),
        P(),
        P("dp", "ctx", None, None, None),
    )
    return jax.shard_map(
        per_device,
        mesh=mesh,
        in_specs=placed,
        out_specs=(
            P("dp", "ctx", None, None, None),
            P("dp", "ctx", None, None, None),
            P(None, "ctx", None),
        ),
        check_vma=False,
    )
```

```python
import jax
import jax.numpy as jnp
from jax import lax
from jax.experimental import pallas as pl
from jax.experimental.pallas import tpu as pltpu
from jax.sharding import PartitionSpec as P

D = 1024
HEADS = 8
HEAD = 64
HQ = HEADS * HEAD
SPAN = 96
RANKS = 16
TILES = 2 * RANKS
CHUNK = 256
KEY_ROWS = TILES * SPAN + CHUNK
NEGATIVE = -1e30
SMALL_VMEM = 24 * 1024 * 1024
PROJECT_VMEM = 60 * 1024 * 1024

CORE_SWAP = [(i, i ^ 1) for i in range(16)]
CHIP_LINES = [[4 * x + rest for x in range(4)] for rest in range(4)]
X_SHIFTS = [[(i, (i + 4 * shift) % 16) for i in range(16)] for shift in range(1, 4)]


def low_lanes(rows):
    return lax.broadcasted_iota(jnp.int32, (rows, 128), 1) < HEAD


def project_kernel(place_ref, tokens_ref, upstream_ref, weights_ref, keep_ref, give_ref):
    keep_first = place_ref[1] == 0
    inputs = tokens_ref[...].reshape(2 * SPAN, D)
    upstream = upstream_ref[...].reshape(2 * SPAN, D)

    def product(rows, number):
        return jnp.dot(rows, weights_ref[number], preferred_element_type=jnp.float32)

    queries, keys, values = (product(inputs, number) for number in range(3))
    grads = product(upstream, 3)
    low = low_lanes(2 * SPAN)
    for half, (first, second) in enumerate(((queries, grads), (keys, values))):
        place = slice(SPAN * half, SPAN * half + SPAN)
        for pair in range(2):
            one = first[:, 128 * pair : 128 * pair + 128]
            two = second[:, 128 * pair : 128 * pair + 128]
            even = jnp.where(low, one, pltpu.roll(two, HEAD, 1))
            odd = jnp.where(low, pltpu.roll(one, HEAD, 1), two)
            for head, rows in ((2 * pair, even), (2 * pair + 1, odd)):
                zero, other = rows[:SPAN], rows[SPAN:]
                keep_ref[head, 0, place, :] = jnp.where(keep_first, zero, other).astype(
                    jnp.bfloat16
                )
                give_ref[head, place, :] = jnp.where(keep_first, other, zero).astype(jnp.bfloat16)


def project(place, tokens, upstream, weights):
    rows_spec = pl.BlockSpec((2, SPAN, D), lambda j, place: (0, 0, 0))
    return pl.pallas_call(
        project_kernel,
        out_shape=(
            jax.ShapeDtypeStruct((HEADS, 2, 2 * SPAN, 128), jnp.bfloat16),
            jax.ShapeDtypeStruct((HEADS, 2 * SPAN, 128), jnp.bfloat16),
        ),
        grid_spec=pltpu.PrefetchScalarGridSpec(
            num_scalar_prefetch=1,
            grid=(2,),
            in_specs=[
                rows_spec,
                rows_spec,
                pl.BlockSpec((4, D, HQ // 2), lambda j, place: (0, 0, j)),
            ],
            out_specs=(
                pl.BlockSpec((HEADS // 2, 1, 2 * SPAN, 128), lambda j, place: (j, place[0], 0, 0)),
                pl.BlockSpec((HEADS // 2, 2 * SPAN, 128), lambda j, place: (j, 0, 0)),
            ),
        ),
        compiler_params=pltpu.CompilerParams(vmem_limit_bytes=PROJECT_VMEM),
        name="project",
    )(place, tokens, upstream, weights)


def attend_kernel(
    core_ref, tiles_ref, own_ref, other_ref, out_ref, own_grad_ref, other_grad_ref,
    key_ref, grad_ref, score_ref, prob_grad_ref,
):
    core = core_ref[0]
    first = tiles_ref[0]
    second = first + tiles_ref[1]
    third = second + tiles_ref[2]
    grad_ref[...] = jnp.zeros_like(grad_ref)
    key_ref[TILES * SPAN :, :] = jnp.zeros((CHUNK, 128), jnp.bfloat16)

    def own_tile(rank):
        return jnp.where(rank % 2 == core, rank, TILES - 1 - rank)

    def tile_rows(tile):
        return pl.ds(pl.multiple_of(tile * SPAN, SPAN), SPAN)

    for rank in range(RANKS):
        tile = own_tile(rank)
        key_ref[tile_rows(tile), :] = own_ref[rank, SPAN:, :]
        key_ref[tile_rows(TILES - 1 - tile), :] = other_ref[rank]


    def tile_start(tile):
        return jnp.where(
            tile >= third, third, jnp.where(tile >= second, second, jnp.where(tile >= first, first, 0))
        )

    def holder(tile):
        return jnp.where(tile < RANKS, tile, TILES - 1 - tile)

    def two_tiles(tile, chunks):
        start, next_start = tile_start(tile), tile_start(tile + 2)
        base = pl.multiple_of(start * SPAN, SPAN)
        ranks = (holder(tile), holder(tile + 2))
        packed = jnp.concatenate([own_ref[rank, :SPAN, :] for rank in ranks], axis=0)
        low = low_lanes(2 * SPAN)
        query_only = jnp.where(low, packed, jnp.zeros_like(packed)) * jnp.bfloat16(HEAD ** -0.5)
        grad_only = jnp.where(low, jnp.zeros_like(packed), packed)
        left = jnp.concatenate([query_only, grad_only], axis=0)
        right = jnp.concatenate([grad_only, query_only], axis=0)
        row = lax.broadcasted_iota(jnp.int32, (2 * SPAN, CHUNK), 0)
        lane = lax.broadcasted_iota(jnp.int32, (2 * SPAN, CHUNK), 1)
        upper = row < SPAN
        last = row + (tile - start) * SPAN + jnp.where(upper, 0, SPAN) - lane
        earliest = jnp.where(upper, 0, (next_start - start) * SPAN) - lane

        def rows(j):
            return pl.ds(pl.multiple_of(base + CHUNK * j, 32), CHUNK)

        top = jnp.full((2 * SPAN, 1), NEGATIVE, jnp.float32)
        for j in range(chunks):
            both = lax.dot_general(
                left, key_ref[rows(j), :], (((1,), (1,)), ((), ())),
                preferred_element_type=jnp.float32,
            )
            allowed = earliest <= CHUNK * j
            if j >= chunks - 3:
                allowed = jnp.logical_and(allowed, last >= CHUNK * j)
            scores = jnp.where(allowed, both[: 2 * SPAN], NEGATIVE)
            place = slice(CHUNK * j, CHUNK * j + CHUNK)
            score_ref[:, place] = scores
            prob_grad_ref[:, place] = both[2 * SPAN :]
            top = jnp.maximum(top, jnp.max(scores, axis=1, keepdims=True))
        total = jnp.zeros((2 * SPAN, 1), jnp.float32)
        accum = jnp.zeros((2 * SPAN, 128), jnp.float32)
        for j in range(chunks):
            place = slice(CHUNK * j, CHUNK * j + CHUNK)
            expo = jnp.exp(score_ref[:, place] - top)
            score_ref[:, place] = expo
            total = total + jnp.sum(expo, axis=1, keepdims=True)
            accum = accum + jnp.dot(
                expo.astype(jnp.bfloat16), key_ref[rows(j), :], preferred_element_type=jnp.float32
            )
        inverse = 1.0 / total
        context = (accum / total).astype(jnp.bfloat16)
        delta = jnp.sum(
            grad_only.astype(jnp.float32) * context.astype(jnp.float32), axis=1, keepdims=True
        )
        query_grad = jnp.zeros((2 * SPAN, 128), jnp.float32)
        for j in range(chunks):
            place = slice(CHUNK * j, CHUNK * j + CHUNK)
            probs = score_ref[:, place] * inverse
            score_grad = (probs * (prob_grad_ref[:, place] - delta)).astype(jnp.bfloat16)
            query_grad = query_grad + jnp.dot(
                score_grad, key_ref[rows(j), :], preferred_element_type=jnp.float32
            )
            stacked = jnp.concatenate([probs.astype(jnp.bfloat16), score_grad], axis=0)
            grad_ref[rows(j), :] += lax.dot_general(
                stacked, right, (((0,), (0,)), ((), ())), preferred_element_type=jnp.float32
            )
        merged = jnp.where(low, query_grad * HEAD ** -0.5, context.astype(jnp.float32)).astype(jnp.bfloat16)
        out_ref[ranks[0]] = merged[:SPAN]
        out_ref[ranks[1]] = merged[SPAN:]

    def one_step(step, carry):
        tile = core + 4 * step
        chunks = ((tile + 3 - tile_start(tile)) * SPAN + CHUNK - 1) // CHUNK
        for count in range(2, 8):
            @pl.when(chunks == count)
            def _():
                two_tiles(tile, count)
        return carry

    lax.fori_loop(0, TILES // 4, one_step, 0)
    for rank in range(RANKS):
        tile = own_tile(rank)
        own_grad_ref[rank] = grad_ref[tile_rows(tile), :]
        other_grad_ref[rank] = grad_ref[tile_rows(TILES - 1 - tile), :].astype(jnp.bfloat16)


def attend(core, tiles, own, other_keys):
    smem = pl.BlockSpec(memory_space=pltpu.SMEM)
    vmem = pl.BlockSpec(memory_space=pltpu.VMEM)
    block = (RANKS, SPAN, 128)
    return pl.pallas_call(
        attend_kernel,
        out_shape=(
            jax.ShapeDtypeStruct(block, jnp.bfloat16),
            jax.ShapeDtypeStruct(block, jnp.float32),
            jax.ShapeDtypeStruct(block, jnp.bfloat16),
        ),
        in_specs=[smem, smem, vmem, vmem],
        out_specs=(vmem, vmem, vmem),
        scratch_shapes=[
            pltpu.VMEM((KEY_ROWS, 128), jnp.bfloat16),
            pltpu.VMEM((KEY_ROWS, 128), jnp.float32),
            pltpu.VMEM((2 * SPAN, 7 * CHUNK), jnp.float32),
            pltpu.VMEM((2 * SPAN, 7 * CHUNK), jnp.float32),
        ],
        compiler_params=pltpu.CompilerParams(vmem_limit_bytes=SMALL_VMEM),
        cost_estimate=pl.CostEstimate(
            flops=12_000_000_000, bytes_accessed=4 * 1024 * 1024, transcendentals=0
        ),
        name="attend",
    )(core, tiles, own, other_keys)


def weight_kernel(place_ref, grads_ref, *refs):
    line_refs, (keep_ref, give_ref, held_ref) = refs[:8], refs[8:]
    core, column = place_ref[0], place_ref[1]

    @pl.when(pl.program_id(0) == 0)
    def _():
        for shift in range(4):
            chip = jnp.bitwise_and(column + 4 - shift, 3)
            for part in range(2):
                sequence = jnp.bitwise_xor(core, part)
                first = (2 * shift + part) * SPAN
                for head in range(2):
                    for half in range(2):
                        lanes = 128 * (2 * half + head)
                        held_ref[first : first + SPAN, lanes : lanes + 128] = grads_ref[
                            chip, head, sequence, SPAN * half : SPAN * half + SPAN, :
                        ]

    def product(kind, columns):
        rows = jnp.concatenate(
            [ref[...].reshape(2 * SPAN, D // 4) for ref in line_refs[kind::2]], axis=0
        )
        return lax.dot_general(
            rows, held_ref[:, :columns], (((0,), (0,)), ((), ())), preferred_element_type=jnp.float32
        )

    by_tokens = product(0, 512)
    by_upstream = product(1, 256)
    low = low_lanes(D // 4)
    firsts = [
        jnp.where(low, by_tokens[:, 128 * i : 128 * i + 128], by_upstream[:, 128 * i : 128 * i + 128])
        for i in range(2)
    ]
    seconds = [by_tokens[:, 256:384], by_tokens[:, 384:]]
    for lanes, (zero, one) in ((slice(0, 128), firsts), (slice(128, 256), seconds)):
        kept = jnp.where(core == 0, zero, one).astype(jnp.bfloat16)
        given = jnp.where(core == 0, one, zero).astype(jnp.bfloat16)
        keep_ref[:, :, lanes] = kept.reshape(4, 64, 128)
        give_ref[:, :, lanes] = given.reshape(4, 64, 128)


def weight_terms(place, grads, lines):
    shape = jax.ShapeDtypeStruct((RANKS, 64, 256), jnp.bfloat16)
    line_spec = pl.BlockSpec((2, SPAN, D // 4), lambda j, place: (0, 0, j))
    out_spec = pl.BlockSpec((4, 64, 256), lambda j, place: (j, 0, 0))
    return pl.pallas_call(
        weight_kernel,
        out_shape=(shape, shape),
        grid_spec=pltpu.PrefetchScalarGridSpec(
            num_scalar_prefetch=1,
            grid=(4,),
            in_specs=[
                pl.BlockSpec((4, 2, 2, 2 * SPAN, 128), lambda j, place: (0, 0, 0, 0, 0)),
                *[line_spec] * 8,
            ],
            out_specs=(out_spec, out_spec),
            scratch_shapes=[pltpu.VMEM((8 * SPAN, 512), jnp.bfloat16)],
        ),
        compiler_params=pltpu.CompilerParams(vmem_limit_bytes=SMALL_VMEM),
        name="weight_terms",
    )(place, grads, *lines)


def spread_kernel(parts_ref, out_ref):
    low = low_lanes(64)
    factor = float(16 * RANKS * 2 * SPAN) ** -0.5
    for column in range(4):
        columns = slice(128 * column, 128 * column + 128)
        for half, (lower, upper) in enumerate(((0, 3), (1, 2))):
            lanes = slice(128 * half, 128 * half + 128)
            one, two = (
                factor
                * (
                    parts_ref[column, 0, core, :, lanes].astype(jnp.float32)
                    + parts_ref[column, 1, core, :, lanes].astype(jnp.float32)
                )
                for core in range(2)
            )
            out_ref[lower, :, columns] = jnp.where(low, one, pltpu.roll(two, HEAD, 1)).astype(
                jnp.bfloat16
            )
            out_ref[upper, :, columns] = jnp.where(low, pltpu.roll(one, HEAD, 1), two).astype(
                jnp.bfloat16
            )


def spread_heads(parts):
    return pl.pallas_call(
        spread_kernel,
        out_shape=jax.ShapeDtypeStruct((4, 64, HQ), jnp.bfloat16),
        name="spread_heads",
    )(parts)


def output_kernel(place_ref, grads_ref, arrived_ref, weights_ref, out_ref, input_grad_ref, held_ref):
    core, odd = place_ref[0], place_ref[1]

    @pl.when(pl.program_id(0) == 0)
    def _():
        low = low_lanes(SPAN)
        for block in range(2):
            holder = jnp.bitwise_xor(odd, block)
            rows = slice(SPAN * block, SPAN * block + SPAN)
            for half in range(2):
                place = slice(SPAN * half, SPAN * half + SPAN)
                for pair in range(HEADS // 2):
                    columns = slice(128 * pair, 128 * pair + 128)
                    one, two = (
                        jnp.where(
                            holder == core,
                            grads_ref[head, 0, place, :].astype(jnp.float32),
                            arrived_ref[head, place, :].astype(jnp.float32),
                        )
                        for head in (2 * pair, 2 * pair + 1)
                    )
                    held_ref[2 * half, rows, columns] = jnp.where(
                        low, one, pltpu.roll(two, HEAD, 1)
                    ).astype(jnp.bfloat16)
                    held_ref[2 * half + 1, rows, columns] = jnp.where(
                        low, pltpu.roll(one, HEAD, 1), two
                    ).astype(jnp.bfloat16)

    def product(number, weight):
        return lax.dot_general(
            held_ref[number], weights_ref[weight], (((1,), (1,)), ((), ())),
            preferred_element_type=jnp.float32,
        )

    out_ref[...] = product(1, 3).astype(jnp.bfloat16).reshape(2, SPAN, D // 4)
    input_grad = product(0, 0) + product(2, 1) + product(3, 2)
    input_grad_ref[...] = input_grad.astype(jnp.bfloat16).reshape(2, SPAN, D // 4)


def outputs(place, grads, arrived, weights):
    shape = jax.ShapeDtypeStruct((2, SPAN, D), jnp.bfloat16)
    out_spec = pl.BlockSpec((2, SPAN, D // 4), lambda j, place: (0, 0, j))
    return pl.pallas_call(
        output_kernel,
        out_shape=(shape, shape),
        grid_spec=pltpu.PrefetchScalarGridSpec(
            num_scalar_prefetch=1,
            grid=(4,),
            in_specs=[
                pl.BlockSpec((HEADS, 1, 2 * SPAN, 128), lambda j, place: (0, place[0], 0, 0)),
                pl.BlockSpec((HEADS, 2 * SPAN, 128), lambda j, place: (0, 0, 0)),
                pl.BlockSpec((4, D // 4, HQ), lambda j, place: (0, j, 0)),
            ],
            out_specs=(out_spec, out_spec),
            scratch_shapes=[pltpu.VMEM((4, 2 * SPAN, HQ), jnp.bfloat16)],
        ),
        compiler_params=pltpu.CompilerParams(vmem_limit_bytes=SMALL_VMEM),
        cost_estimate=pl.CostEstimate(
            flops=8 * 2 * SPAN * D * HQ, bytes_accessed=7 * 1024 * 1024, transcendentals=0
        ),
        name="outputs",
    )(place, grads, arrived, weights)


def per_device(tokens, sweep_tiles, weights, cotangent):
    core = lax.axis_index("dp") % 2
    column = lax.axis_index("dp") // 4
    rank = lax.axis_index("ctx")
    odd = rank % 2
    block = jnp.bitwise_xor(core, odd)

    rows = tokens.reshape(2, SPAN, D)
    upstream = cotangent.reshape(2, SPAN, D)
    other_tiles = lax.ppermute(sweep_tiles, "dp", CORE_SWAP)
    core_number = core.astype(jnp.int32).reshape(1)
    packed, give = project(
        jnp.stack([core, block]).astype(jnp.int32), rows, upstream, weights
    )
    given = lax.ppermute(give, "dp", CORE_SWAP)
    packed = lax.dynamic_update_index_in_dim(packed, given, 1 - core, 1)

    def chosen(x, number):
        return lax.dynamic_index_in_dim(x, number, 0, keepdims=False)

    arrived = lax.ppermute(
        jnp.stack([chosen(x, 1 - block) for x in (rows, upstream)]), "dp", CORE_SWAP
    )
    own_line = [
        jnp.stack([chosen(x, block), arrived[kind]]) for kind, x in enumerate((rows, upstream))
    ]
    packed, other_tiles = lax.optimization_barrier((packed, other_tiles))
    packed = packed.reshape(RANKS, 2 * SPAN, 128)
    near, far, back_near = (
        [lax.ppermute(half, "dp", shift) for half in own_line] for shift in X_SHIFTS
    )
    own = lax.all_to_all(packed, "ctx", 0, 0)
    own, near, back_near, own_line = lax.optimization_barrier((own, near, back_near, own_line))
    other_keys = lax.ppermute(own[:, SPAN:], "dp", CORE_SWAP)
    tiles = jnp.where(odd == core, sweep_tiles, other_tiles).reshape(-1)
    query_part, own_grad, other_grad = attend(core_number, tiles, own, other_keys)
    other_grad, far[0] = lax.optimization_barrier((other_grad, far[0]))
    arrived = lax.ppermute(other_grad, "dp", CORE_SWAP)
    key_part = (own_grad + arrived.astype(jnp.float32)).astype(jnp.bfloat16)
    back = lax.all_to_all(jnp.concatenate([query_part, key_part], axis=1), "ctx", 0, 0)
    back, far[1] = lax.optimization_barrier((back, far[1]))
    grads = back.reshape(HEADS, 2, 2 * SPAN, 128)
    lines = [*own_line, *near, *far, *back_near]
    line_grads = lax.all_to_all(
        back.reshape(4, 2, 2, 2 * SPAN, 128), "dp", 0, 0, axis_index_groups=CHIP_LINES
    )
    keep, give = weight_terms(
        jnp.stack([core, column]).astype(jnp.int32), line_grads, lines
    )
    given = lax.ppermute(give, "dp", CORE_SWAP)
    terms = (keep.astype(jnp.float32) + given.astype(jnp.float32)).astype(jnp.bfloat16)
    terms, own_grads = lax.optimization_barrier((terms, grads))
    terms = lax.all_to_all(terms, "ctx", 0, 0)
    swapped = lax.ppermute(
        lax.dynamic_index_in_dim(grads, 1 - core, 1, keepdims=False), "dp", CORE_SWAP
    )
    place = jnp.stack([core, odd]).astype(jnp.int32)
    attn_out, input_grad = outputs(place, own_grads, swapped, weights)
    terms, attn_out, input_grad = lax.optimization_barrier((terms, attn_out, input_grad))
    rows = jnp.sum(terms.astype(jnp.float32), axis=0).astype(jnp.bfloat16)
    parts = lax.all_to_all(jnp.broadcast_to(rows, (16, 64, 256)), "dp", 0, 0)
    weight_grads = spread_heads(parts.reshape(4, 2, 2, 64, 256))
    return (attn_out.reshape(tokens.shape), input_grad.reshape(tokens.shape), weight_grads)


def solution(mesh):
    placed = (
        P("dp", "ctx", None, None, None),
        P("dp", None),
        P(),
        P("dp", "ctx", None, None, None),
    )
    return jax.shard_map(
        per_device,
        mesh=mesh,
        in_specs=placed,
        out_specs=(
            P("dp", "ctx", None, None, None),
            P("dp", "ctx", None, None, None),
            P(None, "ctx", None),
        ),
        check_vma=False,
    )
```

```python
import jax
import jax.numpy as jnp
from jax import lax
from jax.experimental import pallas as pl
from jax.experimental.pallas import tpu as pltpu
from jax.sharding import PartitionSpec as P

D = 1024
HEADS = 8
HEAD = 64
HQ = HEADS * HEAD
SPAN = 96
RANKS = 16
TILES = 2 * RANKS
CHUNK = 256
KEY_ROWS = TILES * SPAN + CHUNK
NEGATIVE = -1e30
SMALL_VMEM = 24 * 1024 * 1024
PROJECT_VMEM = 60 * 1024 * 1024

CORE_SWAP = [(i, i ^ 1) for i in range(16)]
CHIP_LINES = [[4 * x + rest for x in range(4)] for rest in range(4)]
X_SHIFTS = [[(i, (i + 4 * shift) % 16) for i in range(16)] for shift in range(1, 4)]


def low_lanes(rows):
    return lax.broadcasted_iota(jnp.int32, (rows, 128), 1) < HEAD


def project_kernel(place_ref, tokens_ref, upstream_ref, weights_ref, keep_ref, give_ref):
    keep_first = place_ref[1] == 0
    inputs = tokens_ref[...].reshape(2 * SPAN, D)
    upstream = upstream_ref[...].reshape(2 * SPAN, D)

    def product(rows, number):
        return jnp.dot(rows, weights_ref[number], preferred_element_type=jnp.float32)

    queries, keys, values = (product(inputs, number) for number in range(3))
    grads = product(upstream, 3)
    low = low_lanes(2 * SPAN)
    for half, (first, second) in enumerate(((queries, grads), (keys, values))):
        place = slice(SPAN * half, SPAN * half + SPAN)
        for pair in range(2):
            one = first[:, 128 * pair : 128 * pair + 128]
            two = second[:, 128 * pair : 128 * pair + 128]
            even = jnp.where(low, one, pltpu.roll(two, HEAD, 1))
            odd = jnp.where(low, pltpu.roll(one, HEAD, 1), two)
            for head, rows in ((2 * pair, even), (2 * pair + 1, odd)):
                zero, other = rows[:SPAN], rows[SPAN:]
                keep_ref[head, 0, place, :] = jnp.where(keep_first, zero, other).astype(
                    jnp.bfloat16
                )
                give_ref[head, place, :] = jnp.where(keep_first, other, zero).astype(jnp.bfloat16)


def project(place, tokens, upstream, weights):
    rows_spec = pl.BlockSpec((2, SPAN, D), lambda j, place: (0, 0, 0))
    return pl.pallas_call(
        project_kernel,
        out_shape=(
            jax.ShapeDtypeStruct((HEADS, 2, 2 * SPAN, 128), jnp.bfloat16),
            jax.ShapeDtypeStruct((HEADS, 2 * SPAN, 128), jnp.bfloat16),
        ),
        grid_spec=pltpu.PrefetchScalarGridSpec(
            num_scalar_prefetch=1,
            grid=(2,),
            in_specs=[
                rows_spec,
                rows_spec,
                pl.BlockSpec((4, D, HQ // 2), lambda j, place: (0, 0, j)),
            ],
            out_specs=(
                pl.BlockSpec((HEADS // 2, 1, 2 * SPAN, 128), lambda j, place: (j, place[0], 0, 0)),
                pl.BlockSpec((HEADS // 2, 2 * SPAN, 128), lambda j, place: (j, 0, 0)),
            ),
        ),
        compiler_params=pltpu.CompilerParams(vmem_limit_bytes=PROJECT_VMEM),
        name="project",
    )(place, tokens, upstream, weights)


def attend_kernel(
    core_ref, tiles_ref, own_ref, other_ref, out_ref, own_grad_ref, other_grad_ref,
    key_ref, grad_ref, score_ref, prob_grad_ref,
):
    core = core_ref[0]
    first = tiles_ref[0]
    second = first + tiles_ref[1]
    third = second + tiles_ref[2]
    grad_ref[...] = jnp.zeros_like(grad_ref)
    key_ref[TILES * SPAN :, :] = jnp.zeros((CHUNK, 128), jnp.bfloat16)

    def own_tile(rank):
        return jnp.where(rank % 2 == core, rank, TILES - 1 - rank)

    def tile_rows(tile):
        return pl.ds(pl.multiple_of(tile * SPAN, SPAN), SPAN)

    for rank in range(RANKS):
        tile = own_tile(rank)
        key_ref[tile_rows(tile), :] = own_ref[rank, SPAN:, :]
        key_ref[tile_rows(TILES - 1 - tile), :] = other_ref[rank]


    def tile_start(tile):
        return jnp.where(
            tile >= third, third, jnp.where(tile >= second, second, jnp.where(tile >= first, first, 0))
        )

    def holder(tile):
        return jnp.where(tile < RANKS, tile, TILES - 1 - tile)

    def two_tiles(tile, chunks):
        start, next_start = tile_start(tile), tile_start(tile + 2)
        base = pl.multiple_of(start * SPAN, SPAN)
        ranks = (holder(tile), holder(tile + 2))
        packed = jnp.concatenate([own_ref[rank, :SPAN, :] for rank in ranks], axis=0)
        low = low_lanes(2 * SPAN)
        query_only = jnp.where(low, packed, jnp.zeros_like(packed)) * jnp.bfloat16(HEAD ** -0.5)
        grad_only = jnp.where(low, jnp.zeros_like(packed), packed)
        left = jnp.concatenate([query_only, grad_only], axis=0)
        right = jnp.concatenate([grad_only, query_only], axis=0)
        row = lax.broadcasted_iota(jnp.int32, (2 * SPAN, CHUNK), 0)
        lane = lax.broadcasted_iota(jnp.int32, (2 * SPAN, CHUNK), 1)
        upper = row < SPAN
        last = row + (tile - start) * SPAN + jnp.where(upper, 0, SPAN) - lane
        earliest = jnp.where(upper, 0, (next_start - start) * SPAN) - lane

        def rows(j):
            return pl.ds(pl.multiple_of(base + CHUNK * j, 32), CHUNK)

        top = jnp.full((2 * SPAN, 1), NEGATIVE, jnp.float32)
        for j in range(chunks):
            both = lax.dot_general(
                left, key_ref[rows(j), :], (((1,), (1,)), ((), ())),
                preferred_element_type=jnp.float32,
            )
            allowed = earliest <= CHUNK * j
            if j >= chunks - 3:
                allowed = jnp.logical_and(allowed, last >= CHUNK * j)
            scores = jnp.where(allowed, both[: 2 * SPAN], NEGATIVE)
            place = slice(CHUNK * j, CHUNK * j + CHUNK)
            score_ref[:, place] = scores
            prob_grad_ref[:, place] = both[2 * SPAN :]
            top = jnp.maximum(top, jnp.max(scores, axis=1, keepdims=True))
        total = jnp.zeros((2 * SPAN, 1), jnp.float32)
        accum = jnp.zeros((2 * SPAN, 128), jnp.float32)
        for j in range(chunks):
            place = slice(CHUNK * j, CHUNK * j + CHUNK)
            expo = jnp.exp(score_ref[:, place] - top)
            score_ref[:, place] = expo
            total = total + jnp.sum(expo, axis=1, keepdims=True)
            accum = accum + jnp.dot(
                expo.astype(jnp.bfloat16), key_ref[rows(j), :], preferred_element_type=jnp.float32
            )
        inverse = 1.0 / total
        context = (accum / total).astype(jnp.bfloat16)
        delta = jnp.sum(
            grad_only.astype(jnp.float32) * context.astype(jnp.float32), axis=1, keepdims=True
        )
        query_grad = jnp.zeros((2 * SPAN, 128), jnp.float32)
        for j in range(chunks):
            place = slice(CHUNK * j, CHUNK * j + CHUNK)
            probs = score_ref[:, place] * inverse
            score_grad = (probs * (prob_grad_ref[:, place] - delta)).astype(jnp.bfloat16)
            query_grad = query_grad + jnp.dot(
                score_grad, key_ref[rows(j), :], preferred_element_type=jnp.float32
            )
            stacked = jnp.concatenate([probs.astype(jnp.bfloat16), score_grad], axis=0)
            grad_ref[rows(j), :] += lax.dot_general(
                stacked, right, (((0,), (0,)), ((), ())), preferred_element_type=jnp.float32
            )
        merged = jnp.where(low, query_grad * HEAD ** -0.5, context.astype(jnp.float32)).astype(jnp.bfloat16)
        out_ref[ranks[0]] = merged[:SPAN]
        out_ref[ranks[1]] = merged[SPAN:]

    def one_step(step, carry):
        tile = core + 4 * step
        chunks = ((tile + 3 - tile_start(tile)) * SPAN + CHUNK - 1) // CHUNK
        for count in range(2, 8):
            @pl.when(chunks == count)
            def _():
                two_tiles(tile, count)
        return carry

    lax.fori_loop(0, TILES // 4, one_step, 0)
    for rank in range(RANKS):
        tile = own_tile(rank)
        own_grad_ref[rank] = grad_ref[tile_rows(tile), :]
        other_grad_ref[rank] = grad_ref[tile_rows(TILES - 1 - tile), :].astype(jnp.bfloat16)


def attend(core, tiles, own, other_keys):
    smem = pl.BlockSpec(memory_space=pltpu.SMEM)
    vmem = pl.BlockSpec(memory_space=pltpu.VMEM)
    block = (RANKS, SPAN, 128)
    return pl.pallas_call(
        attend_kernel,
        out_shape=(
            jax.ShapeDtypeStruct(block, jnp.bfloat16),
            jax.ShapeDtypeStruct(block, jnp.float32),
            jax.ShapeDtypeStruct(block, jnp.bfloat16),
        ),
        in_specs=[smem, smem, vmem, vmem],
        out_specs=(vmem, vmem, vmem),
        scratch_shapes=[
            pltpu.VMEM((KEY_ROWS, 128), jnp.bfloat16),
            pltpu.VMEM((KEY_ROWS, 128), jnp.float32),
            pltpu.VMEM((2 * SPAN, 7 * CHUNK), jnp.float32),
            pltpu.VMEM((2 * SPAN, 7 * CHUNK), jnp.float32),
        ],
        compiler_params=pltpu.CompilerParams(vmem_limit_bytes=SMALL_VMEM),
        cost_estimate=pl.CostEstimate(
            flops=12_000_000_000, bytes_accessed=4 * 1024 * 1024, transcendentals=0
        ),
        name="attend",
    )(core, tiles, own, other_keys)


def repack_kernel(back_ref, out_ref):
    low = low_lanes(SPAN)
    for sequence in range(2):
        for half, (lower, upper) in enumerate(((0, 3), (1, 2))):
            place = slice(SPAN * half, SPAN * half + SPAN)
            for pair in range(HEADS // 2):
                columns = slice(128 * pair, 128 * pair + 128)
                one = back_ref[2 * pair, sequence, place, :].astype(jnp.float32)
                two = back_ref[2 * pair + 1, sequence, place, :].astype(jnp.float32)
                out_ref[lower, sequence, :, columns] = jnp.where(
                    low, one, pltpu.roll(two, HEAD, 1)
                ).astype(jnp.bfloat16)
                out_ref[upper, sequence, :, columns] = jnp.where(
                    low, pltpu.roll(one, HEAD, 1), two
                ).astype(jnp.bfloat16)


def repack(back):
    vmem = pl.BlockSpec(memory_space=pltpu.VMEM)
    return pl.pallas_call(
        repack_kernel,
        out_shape=jax.ShapeDtypeStruct((4, 2, SPAN, HQ), jnp.bfloat16),
        in_specs=[vmem],
        out_specs=vmem,
        compiler_params=pltpu.CompilerParams(vmem_limit_bytes=SMALL_VMEM),
        name="repack",
    )(back)


def weight_kernel(
    place_ref, grads_ref, own_ref, near_ref, far_ref, back_ref, keep_ref, give_ref, held_ref
):
    core, column = place_ref[0], place_ref[1]

    @pl.when(pl.program_id(0) == 0)
    def _():
        for shift in range(4):
            chip = jnp.bitwise_and(column + 4 - shift, 3)
            for part in range(2):
                first = (2 * shift + part) * SPAN
                held_ref[first : first + SPAN, :] = grads_ref[chip, jnp.bitwise_xor(core, part)]

    rows = jnp.concatenate(
        [
            ref[...].reshape(2 * SPAN, D // 4)
            for ref in (own_ref, near_ref, far_ref, back_ref)
        ],
        axis=0,
    )
    result = lax.dot_general(
        rows, held_ref[...], (((0,), (0,)), ((), ())), preferred_element_type=jnp.float32
    )
    zero, one = result[:, :256], result[:, 256:]
    keep_ref[...] = jnp.where(core == 0, zero, one).astype(jnp.bfloat16).reshape(4, 64, 256)
    give_ref[...] = jnp.where(core == 0, one, zero).astype(jnp.bfloat16).reshape(4, 64, 256)


def weight_terms(place, grads, lines):
    shape = jax.ShapeDtypeStruct((RANKS, 64, 256), jnp.bfloat16)
    line_spec = pl.BlockSpec((2, SPAN, D // 4), lambda j, place: (0, 0, j))
    out_spec = pl.BlockSpec((4, 64, 256), lambda j, place: (j, 0, 0))
    return pl.pallas_call(
        weight_kernel,
        out_shape=(shape, shape),
        grid_spec=pltpu.PrefetchScalarGridSpec(
            num_scalar_prefetch=1,
            grid=(4,),
            in_specs=[
                pl.BlockSpec((4, 2, SPAN, HQ), lambda j, place: (0, 0, 0, 0)),
                *[line_spec] * 4,
            ],
            out_specs=(out_spec, out_spec),
            scratch_shapes=[pltpu.VMEM((8 * SPAN, HQ), jnp.bfloat16)],
        ),
        compiler_params=pltpu.CompilerParams(vmem_limit_bytes=SMALL_VMEM),
        name="weight_terms",
    )(place, grads, *lines)


def spread_kernel(parts_ref, out_ref):
    factor = float(16 * RANKS * 2 * SPAN) ** -0.5
    for column in range(4):
        for core in range(2):
            total = parts_ref[column, 0, core].astype(jnp.float32) + parts_ref[
                column, 1, core
            ].astype(jnp.float32)
            out_ref[column, :, 256 * core : 256 * core + 256] = (total * factor).astype(
                jnp.bfloat16
            )


def spread(parts):
    return pl.pallas_call(
        spread_kernel,
        out_shape=jax.ShapeDtypeStruct((4, 64, HQ), jnp.bfloat16),
        name="spread",
    )(parts)


def output_kernel(place_ref, grads_ref, arrived_ref, weights_ref, out_ref, input_grad_ref, held_ref):
    core, odd = place_ref[0], place_ref[1]

    @pl.when(pl.program_id(0) == 0)
    def _():
        for block in range(2):
            mine = jnp.bitwise_xor(odd, block) == core
            for number in range(4):
                held_ref[number, SPAN * block : SPAN * block + SPAN, :] = jnp.where(
                    mine,
                    grads_ref[number, 0].astype(jnp.float32),
                    arrived_ref[number].astype(jnp.float32),
                ).astype(jnp.bfloat16)

    def product(number):
        return lax.dot_general(
            held_ref[number], weights_ref[number], (((1,), (1,)), ((), ())),
            preferred_element_type=jnp.float32,
        )

    out_ref[...] = product(3).astype(jnp.bfloat16).reshape(2, SPAN, D // 4)
    input_grad = product(0) + product(1) + product(2)
    input_grad_ref[...] = input_grad.astype(jnp.bfloat16).reshape(2, SPAN, D // 4)


def outputs(place, grads, arrived, weights):
    shape = jax.ShapeDtypeStruct((2, SPAN, D), jnp.bfloat16)
    out_spec = pl.BlockSpec((2, SPAN, D // 4), lambda j, place: (0, 0, j))
    return pl.pallas_call(
        output_kernel,
        out_shape=(shape, shape),
        grid_spec=pltpu.PrefetchScalarGridSpec(
            num_scalar_prefetch=1,
            grid=(4,),
            in_specs=[
                pl.BlockSpec((4, 1, SPAN, HQ), lambda j, place: (0, place[0], 0, 0)),
                pl.BlockSpec((4, SPAN, HQ), lambda j, place: (0, 0, 0)),
                pl.BlockSpec((4, D // 4, HQ), lambda j, place: (0, j, 0)),
            ],
            out_specs=(out_spec, out_spec),
            scratch_shapes=[pltpu.VMEM((4, 2 * SPAN, HQ), jnp.bfloat16)],
        ),
        compiler_params=pltpu.CompilerParams(vmem_limit_bytes=SMALL_VMEM),
        cost_estimate=pl.CostEstimate(
            flops=8 * 2 * SPAN * D * HQ, bytes_accessed=7 * 1024 * 1024, transcendentals=0
        ),
        name="outputs",
    )(place, grads, arrived, weights)


def per_device(tokens, sweep_tiles, weights, cotangent):
    core = lax.axis_index("dp") % 2
    column = lax.axis_index("dp") // 4
    rank = lax.axis_index("ctx")
    odd = rank % 2
    block = jnp.bitwise_xor(core, odd)

    rows = tokens.reshape(2, SPAN, D)
    upstream = cotangent.reshape(2, SPAN, D)
    other_tiles = lax.ppermute(sweep_tiles, "dp", CORE_SWAP)
    core_number = core.astype(jnp.int32).reshape(1)
    packed, give = project(
        jnp.stack([core, block]).astype(jnp.int32), rows, upstream, weights
    )
    given = lax.ppermute(give, "dp", CORE_SWAP)
    packed = lax.dynamic_update_index_in_dim(packed, given, 1 - core, 1)

    def chosen(x, number):
        return lax.dynamic_index_in_dim(x, number, 0, keepdims=False)

    arrived = lax.ppermute(
        jnp.stack([chosen(x, 1 - block) for x in (rows, upstream)]), "dp", CORE_SWAP
    )
    own_line = [
        jnp.stack([chosen(x, block), arrived[kind]]) for kind, x in enumerate((rows, upstream))
    ]
    packed, other_tiles = lax.optimization_barrier((packed, other_tiles))
    packed = packed.reshape(RANKS, 2 * SPAN, 128)
    line, *lines = (
        jnp.where((column + shift) % 4 == 3, own_line[1], own_line[0]) for shift in range(4)
    )
    near, far, back_near = (
        lax.ppermute(rows, "dp", shift) for rows, shift in zip(lines, X_SHIFTS)
    )
    own = lax.all_to_all(packed, "ctx", 0, 0)
    own, near, back_near = lax.optimization_barrier((own, near, back_near))
    other_keys = lax.ppermute(own[:, SPAN:], "dp", CORE_SWAP)
    tiles = jnp.where(odd == core, sweep_tiles, other_tiles).reshape(-1)
    query_part, own_grad, other_grad = attend(core_number, tiles, own, other_keys)
    arrived = lax.ppermute(other_grad, "dp", CORE_SWAP)
    key_part = (own_grad + arrived.astype(jnp.float32)).astype(jnp.bfloat16)
    back = lax.all_to_all(jnp.concatenate([query_part, key_part], axis=1), "ctx", 0, 0)
    grads = repack(back.reshape(HEADS, 2, 2 * SPAN, 128))
    grads, far = lax.optimization_barrier((grads, far))
    line_grads = lax.all_to_all(grads, "dp", 0, 0, axis_index_groups=CHIP_LINES)
    keep, give = weight_terms(
        jnp.stack([core, column]).astype(jnp.int32), line_grads, (line, near, far, back_near)
    )
    given = lax.ppermute(give, "dp", CORE_SWAP)
    terms = (keep.astype(jnp.float32) + given.astype(jnp.float32)).astype(jnp.bfloat16)
    terms, own_grads = lax.optimization_barrier((terms, grads))
    terms = lax.all_to_all(terms, "ctx", 0, 0)
    swapped = lax.ppermute(
        lax.dynamic_index_in_dim(grads, 1 - core, 1, keepdims=False), "dp", CORE_SWAP
    )
    place = jnp.stack([core, odd]).astype(jnp.int32)
    attn_out, input_grad = outputs(place, own_grads, swapped, weights)
    terms, attn_out, input_grad = lax.optimization_barrier((terms, attn_out, input_grad))
    rows = jnp.sum(terms.astype(jnp.float32), axis=0).astype(jnp.bfloat16)
    parts = lax.all_to_all(jnp.broadcast_to(rows, (16, 64, 256)), "dp", 0, 0)
    weight_grads = spread(parts.reshape(4, 2, 2, 64, 256))
    return (attn_out.reshape(tokens.shape), input_grad.reshape(tokens.shape), weight_grads)


def solution(mesh):
    placed = (
        P("dp", "ctx", None, None, None),
        P("dp", None),
        P(),
        P("dp", "ctx", None, None, None),
    )
    return jax.shard_map(
        per_device,
        mesh=mesh,
        in_specs=placed,
        out_specs=(
            P("dp", "ctx", None, None, None),
            P("dp", "ctx", None, None, None),
            P(None, "ctx", None),
        ),
        check_vma=False,
    )
```

```python
import jax
import jax.numpy as jnp
from jax import lax
from jax.experimental import pallas as pl
from jax.experimental.pallas import tpu as pltpu
from jax.sharding import PartitionSpec as P

D = 1024
HEADS = 8
HEAD = 64
HQ = HEADS * HEAD
SPAN = 96
RANKS = 16
TILES = 2 * RANKS
CHUNK = 256
KEY_ROWS = TILES * SPAN + CHUNK
NEGATIVE = -1e30
SMALL_VMEM = 24 * 1024 * 1024
PROJECT_VMEM = 60 * 1024 * 1024

CORE_SWAP = [(i, i ^ 1) for i in range(16)]
X_SHIFTS = [[(i, (i + 4 * shift) % 16) for i in range(16)] for shift in range(1, 4)]


def low_lanes(rows):
    return lax.broadcasted_iota(jnp.int32, (rows, 128), 1) < HEAD


def project_kernel(place_ref, tokens_ref, upstream_ref, weights_ref, keep_ref, give_ref):
    keep_first = place_ref[1] == 0
    inputs = tokens_ref[...].reshape(2 * SPAN, D)
    upstream = upstream_ref[...].reshape(2 * SPAN, D)

    def product(rows, number):
        return jnp.dot(rows, weights_ref[number], preferred_element_type=jnp.float32)

    queries, keys, values = (product(inputs, number) for number in range(3))
    grads = product(upstream, 3)
    low = low_lanes(2 * SPAN)
    for half, (first, second) in enumerate(((queries, grads), (keys, values))):
        place = slice(SPAN * half, SPAN * half + SPAN)
        for pair in range(2):
            one = first[:, 128 * pair : 128 * pair + 128]
            two = second[:, 128 * pair : 128 * pair + 128]
            even = jnp.where(low, one, pltpu.roll(two, HEAD, 1))
            odd = jnp.where(low, pltpu.roll(one, HEAD, 1), two)
            for head, rows in ((2 * pair, even), (2 * pair + 1, odd)):
                zero, other = rows[:SPAN], rows[SPAN:]
                keep_ref[head, 0, place, :] = jnp.where(keep_first, zero, other).astype(
                    jnp.bfloat16
                )
                give_ref[head, place, :] = jnp.where(keep_first, other, zero).astype(jnp.bfloat16)


def project(place, tokens, upstream, weights):
    rows_spec = pl.BlockSpec((2, SPAN, D), lambda j, place: (0, 0, 0))
    return pl.pallas_call(
        project_kernel,
        out_shape=(
            jax.ShapeDtypeStruct((HEADS, 2, 2 * SPAN, 128), jnp.bfloat16),
            jax.ShapeDtypeStruct((HEADS, 2 * SPAN, 128), jnp.bfloat16),
        ),
        grid_spec=pltpu.PrefetchScalarGridSpec(
            num_scalar_prefetch=1,
            grid=(2,),
            in_specs=[
                rows_spec,
                rows_spec,
                pl.BlockSpec((4, D, HQ // 2), lambda j, place: (0, 0, j)),
            ],
            out_specs=(
                pl.BlockSpec((HEADS // 2, 1, 2 * SPAN, 128), lambda j, place: (j, place[0], 0, 0)),
                pl.BlockSpec((HEADS // 2, 2 * SPAN, 128), lambda j, place: (j, 0, 0)),
            ),
        ),
        compiler_params=pltpu.CompilerParams(vmem_limit_bytes=PROJECT_VMEM),
        name="project",
    )(place, tokens, upstream, weights)


def attend_kernel(
    core_ref, tiles_ref, own_ref, other_ref, out_ref, own_grad_ref, other_grad_ref,
    key_ref, grad_ref, score_ref, prob_grad_ref,
):
    core = core_ref[0]
    first = tiles_ref[0]
    second = first + tiles_ref[1]
    third = second + tiles_ref[2]
    grad_ref[...] = jnp.zeros_like(grad_ref)
    key_ref[TILES * SPAN :, :] = jnp.zeros((CHUNK, 128), jnp.bfloat16)

    def own_tile(rank):
        return jnp.where(rank % 2 == core, rank, TILES - 1 - rank)

    def tile_rows(tile):
        return pl.ds(pl.multiple_of(tile * SPAN, SPAN), SPAN)

    for rank in range(RANKS):
        tile = own_tile(rank)
        key_ref[tile_rows(tile), :] = own_ref[rank, SPAN:, :]
        key_ref[tile_rows(TILES - 1 - tile), :] = other_ref[rank]


    def tile_start(tile):
        return jnp.where(
            tile >= third, third, jnp.where(tile >= second, second, jnp.where(tile >= first, first, 0))
        )

    def holder(tile):
        return jnp.where(tile < RANKS, tile, TILES - 1 - tile)

    def two_tiles(tile, chunks):
        start, next_start = tile_start(tile), tile_start(tile + 2)
        base = pl.multiple_of(start * SPAN, SPAN)
        ranks = (holder(tile), holder(tile + 2))
        packed = jnp.concatenate([own_ref[rank, :SPAN, :] for rank in ranks], axis=0)
        low = low_lanes(2 * SPAN)
        query_only = jnp.where(low, packed, jnp.zeros_like(packed)) * jnp.bfloat16(HEAD ** -0.5)
        grad_only = jnp.where(low, jnp.zeros_like(packed), packed)
        left = jnp.concatenate([query_only, grad_only], axis=0)
        right = jnp.concatenate([grad_only, query_only], axis=0)
        row = lax.broadcasted_iota(jnp.int32, (2 * SPAN, CHUNK), 0)
        lane = lax.broadcasted_iota(jnp.int32, (2 * SPAN, CHUNK), 1)
        upper = row < SPAN
        last = row + (tile - start) * SPAN + jnp.where(upper, 0, SPAN) - lane
        earliest = jnp.where(upper, 0, (next_start - start) * SPAN) - lane

        def rows(j):
            return pl.ds(pl.multiple_of(base + CHUNK * j, 32), CHUNK)

        top = jnp.full((2 * SPAN, 1), NEGATIVE, jnp.float32)
        for j in range(chunks):
            both = lax.dot_general(
                left, key_ref[rows(j), :], (((1,), (1,)), ((), ())),
                preferred_element_type=jnp.float32,
            )
            allowed = earliest <= CHUNK * j
            if j >= chunks - 3:
                allowed = jnp.logical_and(allowed, last >= CHUNK * j)
            scores = jnp.where(allowed, both[: 2 * SPAN], NEGATIVE)
            place = slice(CHUNK * j, CHUNK * j + CHUNK)
            score_ref[:, place] = scores
            prob_grad_ref[:, place] = both[2 * SPAN :]
            top = jnp.maximum(top, jnp.max(scores, axis=1, keepdims=True))
        total = jnp.zeros((2 * SPAN, 1), jnp.float32)
        accum = jnp.zeros((2 * SPAN, 128), jnp.float32)
        for j in range(chunks):
            place = slice(CHUNK * j, CHUNK * j + CHUNK)
            expo = jnp.exp(score_ref[:, place] - top)
            score_ref[:, place] = expo
            total = total + jnp.sum(expo, axis=1, keepdims=True)
            accum = accum + jnp.dot(
                expo.astype(jnp.bfloat16), key_ref[rows(j), :], preferred_element_type=jnp.float32
            )
        inverse = 1.0 / total
        context = (accum / total).astype(jnp.bfloat16)
        delta = jnp.sum(
            grad_only.astype(jnp.float32) * context.astype(jnp.float32), axis=1, keepdims=True
        )
        query_grad = jnp.zeros((2 * SPAN, 128), jnp.float32)
        for j in range(chunks):
            place = slice(CHUNK * j, CHUNK * j + CHUNK)
            probs = score_ref[:, place] * inverse
            score_grad = (probs * (prob_grad_ref[:, place] - delta)).astype(jnp.bfloat16)
            query_grad = query_grad + jnp.dot(
                score_grad, key_ref[rows(j), :], preferred_element_type=jnp.float32
            )
            stacked = jnp.concatenate([probs.astype(jnp.bfloat16), score_grad], axis=0)
            grad_ref[rows(j), :] += lax.dot_general(
                stacked, right, (((0,), (0,)), ((), ())), preferred_element_type=jnp.float32
            )
        merged = jnp.where(low, query_grad * HEAD ** -0.5, context.astype(jnp.float32)).astype(jnp.bfloat16)
        out_ref[ranks[0]] = merged[:SPAN]
        out_ref[ranks[1]] = merged[SPAN:]

    def one_step(step, carry):
        tile = core + 4 * step
        chunks = ((tile + 3 - tile_start(tile)) * SPAN + CHUNK - 1) // CHUNK
        for count in range(2, 8):
            @pl.when(chunks == count)
            def _():
                two_tiles(tile, count)
        return carry

    lax.fori_loop(0, TILES // 4, one_step, 0)
    for rank in range(RANKS):
        tile = own_tile(rank)
        own_grad_ref[rank] = grad_ref[tile_rows(tile), :]
        other_grad_ref[rank] = grad_ref[tile_rows(TILES - 1 - tile), :].astype(jnp.bfloat16)


def attend(core, tiles, own, other_keys):
    smem = pl.BlockSpec(memory_space=pltpu.SMEM)
    vmem = pl.BlockSpec(memory_space=pltpu.VMEM)
    block = (RANKS, SPAN, 128)
    return pl.pallas_call(
        attend_kernel,
        out_shape=(
            jax.ShapeDtypeStruct(block, jnp.bfloat16),
            jax.ShapeDtypeStruct(block, jnp.float32),
            jax.ShapeDtypeStruct(block, jnp.bfloat16),
        ),
        in_specs=[smem, smem, vmem, vmem],
        out_specs=(vmem, vmem, vmem),
        scratch_shapes=[
            pltpu.VMEM((KEY_ROWS, 128), jnp.bfloat16),
            pltpu.VMEM((KEY_ROWS, 128), jnp.float32),
            pltpu.VMEM((2 * SPAN, 7 * CHUNK), jnp.float32),
            pltpu.VMEM((2 * SPAN, 7 * CHUNK), jnp.float32),
        ],
        compiler_params=pltpu.CompilerParams(vmem_limit_bytes=SMALL_VMEM),
        cost_estimate=pl.CostEstimate(
            flops=12_000_000_000, bytes_accessed=4 * 1024 * 1024, transcendentals=0
        ),
        name="attend",
    )(core, tiles, own, other_keys)


def repack_kernel(column_ref, back_ref, out_ref, *shift_refs):
    low = low_lanes(SPAN)
    for sequence in range(2):
        for half, (lower, upper) in enumerate(((0, 3), (1, 2))):
            place = slice(SPAN * half, SPAN * half + SPAN)
            for pair in range(HEADS // 2):
                columns = slice(128 * pair, 128 * pair + 128)
                one = back_ref[2 * pair, sequence, place, :].astype(jnp.float32)
                two = back_ref[2 * pair + 1, sequence, place, :].astype(jnp.float32)
                out_ref[lower, sequence, :, columns] = jnp.where(
                    low, one, pltpu.roll(two, HEAD, 1)
                ).astype(jnp.bfloat16)
                out_ref[upper, sequence, :, columns] = jnp.where(
                    low, pltpu.roll(one, HEAD, 1), two
                ).astype(jnp.bfloat16)
    for shift, ref in enumerate(shift_refs):
        ref[...] = out_ref[jnp.bitwise_and(column_ref[0] + shift, 3)]


def repack(column, back):
    vmem = pl.BlockSpec(memory_space=pltpu.VMEM)
    return pl.pallas_call(
        repack_kernel,
        out_shape=(
            jax.ShapeDtypeStruct((4, 2, SPAN, HQ), jnp.bfloat16),
            *[jax.ShapeDtypeStruct((2, SPAN, HQ), jnp.bfloat16)] * 4,
        ),
        in_specs=[pl.BlockSpec(memory_space=pltpu.SMEM), vmem],
        out_specs=(vmem,) * 5,
        compiler_params=pltpu.CompilerParams(vmem_limit_bytes=SMALL_VMEM),
        name="repack",
    )(column, back)


def weight_kernel(core_ref, *refs):
    grad_refs, line_refs, (keep_ref, give_ref, held_ref) = refs[:4], refs[4:8], refs[8:]
    core = core_ref[0]

    @pl.when(pl.program_id(0) == 0)
    def _():
        for shift in range(4):
            for part in range(2):
                first = (2 * shift + part) * SPAN
                held_ref[first : first + SPAN, :] = grad_refs[shift][jnp.bitwise_xor(core, part)]

    rows = jnp.concatenate([ref[...].reshape(2 * SPAN, D // 4) for ref in line_refs], axis=0)
    result = lax.dot_general(
        rows, held_ref[...], (((0,), (0,)), ((), ())), preferred_element_type=jnp.float32
    )
    zero, one = result[:, :256], result[:, 256:]
    keep_ref[...] = jnp.where(core == 0, zero, one).astype(jnp.bfloat16).reshape(4, 64, 256)
    give_ref[...] = jnp.where(core == 0, one, zero).astype(jnp.bfloat16).reshape(4, 64, 256)


def weight_terms(core, grads, lines):
    shape = jax.ShapeDtypeStruct((RANKS, 64, 256), jnp.bfloat16)
    grad_spec = pl.BlockSpec((2, SPAN, HQ), lambda j, core: (0, 0, 0))
    line_spec = pl.BlockSpec((2, SPAN, D // 4), lambda j, core: (0, 0, j))
    out_spec = pl.BlockSpec((4, 64, 256), lambda j, core: (j, 0, 0))
    return pl.pallas_call(
        weight_kernel,
        out_shape=(shape, shape),
        grid_spec=pltpu.PrefetchScalarGridSpec(
            num_scalar_prefetch=1,
            grid=(4,),
            in_specs=[
                *[grad_spec] * 4,
                *[line_spec] * 4,
            ],
            out_specs=(out_spec, out_spec),
            scratch_shapes=[pltpu.VMEM((8 * SPAN, HQ), jnp.bfloat16)],
        ),
        compiler_params=pltpu.CompilerParams(vmem_limit_bytes=SMALL_VMEM),
        name="weight_terms",
    )(core, *grads, *lines)


def spread_kernel(parts_ref, out_ref):
    factor = float(16 * RANKS * 2 * SPAN) ** -0.5
    for column in range(4):
        for core in range(2):
            total = parts_ref[column, 0, core].astype(jnp.float32) + parts_ref[
                column, 1, core
            ].astype(jnp.float32)
            out_ref[column, :, 256 * core : 256 * core + 256] = (total * factor).astype(
                jnp.bfloat16
            )


def spread(parts):
    return pl.pallas_call(
        spread_kernel,
        out_shape=jax.ShapeDtypeStruct((4, 64, HQ), jnp.bfloat16),
        name="spread",
    )(parts)


def output_kernel(place_ref, grads_ref, arrived_ref, weights_ref, out_ref, input_grad_ref, held_ref):
    core, odd = place_ref[0], place_ref[1]

    @pl.when(pl.program_id(0) == 0)
    def _():
        for block in range(2):
            mine = jnp.bitwise_xor(odd, block) == core
            for number in range(4):
                held_ref[number, SPAN * block : SPAN * block + SPAN, :] = jnp.where(
                    mine,
                    grads_ref[number, 0].astype(jnp.float32),
                    arrived_ref[number].astype(jnp.float32),
                ).astype(jnp.bfloat16)

    def product(number):
        return lax.dot_general(
            held_ref[number], weights_ref[number], (((1,), (1,)), ((), ())),
            preferred_element_type=jnp.float32,
        )

    out_ref[...] = product(3).astype(jnp.bfloat16).reshape(2, SPAN, D // 4)
    input_grad = product(0) + product(1) + product(2)
    input_grad_ref[...] = input_grad.astype(jnp.bfloat16).reshape(2, SPAN, D // 4)


def outputs(place, grads, arrived, weights):
    shape = jax.ShapeDtypeStruct((2, SPAN, D), jnp.bfloat16)
    out_spec = pl.BlockSpec((2, SPAN, D // 4), lambda j, place: (0, 0, j))
    return pl.pallas_call(
        output_kernel,
        out_shape=(shape, shape),
        grid_spec=pltpu.PrefetchScalarGridSpec(
            num_scalar_prefetch=1,
            grid=(4,),
            in_specs=[
                pl.BlockSpec((4, 1, SPAN, HQ), lambda j, place: (0, place[0], 0, 0)),
                pl.BlockSpec((4, SPAN, HQ), lambda j, place: (0, 0, 0)),
                pl.BlockSpec((4, D // 4, HQ), lambda j, place: (0, j, 0)),
            ],
            out_specs=(out_spec, out_spec),
            scratch_shapes=[pltpu.VMEM((4, 2 * SPAN, HQ), jnp.bfloat16)],
        ),
        compiler_params=pltpu.CompilerParams(vmem_limit_bytes=SMALL_VMEM),
        cost_estimate=pl.CostEstimate(
            flops=8 * 2 * SPAN * D * HQ, bytes_accessed=7 * 1024 * 1024, transcendentals=0
        ),
        name="outputs",
    )(place, grads, arrived, weights)


def per_device(tokens, sweep_tiles, weights, cotangent):
    core = lax.axis_index("dp") % 2
    column = lax.axis_index("dp") // 4
    rank = lax.axis_index("ctx")
    odd = rank % 2
    block = jnp.bitwise_xor(core, odd)

    rows = tokens.reshape(2, SPAN, D)
    upstream = cotangent.reshape(2, SPAN, D)
    other_tiles = lax.ppermute(sweep_tiles, "dp", CORE_SWAP)
    core_number = core.astype(jnp.int32).reshape(1)
    packed, give = project(
        jnp.stack([core, block]).astype(jnp.int32), rows, upstream, weights
    )
    given = lax.ppermute(give, "dp", CORE_SWAP)
    packed = lax.dynamic_update_index_in_dim(packed, given, 1 - core, 1)

    def chosen(x, number):
        return lax.dynamic_index_in_dim(x, number, 0, keepdims=False)

    arrived = lax.ppermute(
        jnp.stack([chosen(x, 1 - block) for x in (rows, upstream)]), "dp", CORE_SWAP
    )
    own_line = [
        jnp.stack([chosen(x, block), arrived[kind]]) for kind, x in enumerate((rows, upstream))
    ]
    packed, other_tiles = lax.optimization_barrier((packed, other_tiles))
    packed = packed.reshape(RANKS, 2 * SPAN, 128)
    line, *lines = (
        jnp.where((column + shift) % 4 == 3, own_line[1], own_line[0]) for shift in range(4)
    )
    near, far, back_near = (
        lax.ppermute(rows, "dp", shift) for rows, shift in zip(lines, X_SHIFTS)
    )
    own = lax.all_to_all(packed, "ctx", 0, 0)
    own, near, back_near = lax.optimization_barrier((own, near, back_near))
    other_keys = lax.ppermute(own[:, SPAN:], "dp", CORE_SWAP)
    tiles = jnp.where(odd == core, sweep_tiles, other_tiles).reshape(-1)
    query_part, own_grad, other_grad = attend(core_number, tiles, own, other_keys)
    arrived = lax.ppermute(other_grad, "dp", CORE_SWAP)
    key_part = (own_grad + arrived.astype(jnp.float32)).astype(jnp.bfloat16)
    back = lax.all_to_all(jnp.concatenate([query_part, key_part], axis=1), "ctx", 0, 0)
    grads, *pieces = repack(
        column.astype(jnp.int32).reshape(1), back.reshape(HEADS, 2, 2 * SPAN, 128)
    )
    pieces, far = lax.optimization_barrier((pieces, far))
    pieces = [pieces[0]] + [lax.ppermute(x, "dp", y) for x, y in zip(pieces[1:], X_SHIFTS)]
    keep, give = weight_terms(core_number, pieces, (line, near, far, back_near))
    given = lax.ppermute(give, "dp", CORE_SWAP)
    terms = (keep.astype(jnp.float32) + given.astype(jnp.float32)).astype(jnp.bfloat16)
    terms, own_grads = lax.optimization_barrier((terms, grads))
    terms = lax.all_to_all(terms, "ctx", 0, 0)
    swapped = lax.ppermute(
        lax.dynamic_index_in_dim(grads, 1 - core, 1, keepdims=False), "dp", CORE_SWAP
    )
    place = jnp.stack([core, odd]).astype(jnp.int32)
    attn_out, input_grad = outputs(place, own_grads, swapped, weights)
    terms, attn_out, input_grad = lax.optimization_barrier((terms, attn_out, input_grad))
    rows = jnp.sum(terms.astype(jnp.float32), axis=0).astype(jnp.bfloat16)
    parts = lax.all_to_all(jnp.broadcast_to(rows, (16, 64, 256)), "dp", 0, 0)
    weight_grads = spread(parts.reshape(4, 2, 2, 64, 256))
    return (attn_out.reshape(tokens.shape), input_grad.reshape(tokens.shape), weight_grads)


def solution(mesh):
    placed = (
        P("dp", "ctx", None, None, None),
        P("dp", None),
        P(),
        P("dp", "ctx", None, None, None),
    )
    return jax.shard_map(
        per_device,
        mesh=mesh,
        in_specs=placed,
        out_specs=(
            P("dp", "ctx", None, None, None),
            P("dp", "ctx", None, None, None),
            P(None, "ctx", None),
        ),
        check_vma=False,
    )
```

```python
import jax
import jax.numpy as jnp
from jax import lax
from jax.experimental import pallas as pl
from jax.experimental.pallas import tpu as pltpu
from jax.sharding import PartitionSpec as P

D = 1024
HEADS = 8
HEAD = 64
HQ = HEADS * HEAD
SPAN = 96
RANKS = 16
TILES = 2 * RANKS
CHUNK = 256
KEY_ROWS = TILES * SPAN + CHUNK
NEGATIVE = -1e30
SMALL_VMEM = 24 * 1024 * 1024
PROJECT_VMEM = 60 * 1024 * 1024

CORE_SWAP = [(i, i ^ 1) for i in range(16)]
Z_SWAP = [(i, i ^ 2) for i in range(16)]
X_SHIFTS = [[(i, (i + 4 * shift) % 16) for i in range(16)] for shift in range(1, 4)]


def low_lanes(rows):
    return lax.broadcasted_iota(jnp.int32, (rows, 128), 1) < HEAD


def project_kernel(place_ref, tokens_ref, upstream_ref, weights_ref, keep_ref, give_ref):
    keep_first = place_ref[1] == 0
    inputs = tokens_ref[...].reshape(2 * SPAN, D)
    upstream = upstream_ref[...].reshape(2 * SPAN, D)

    def product(rows, number):
        return jnp.dot(rows, weights_ref[number], preferred_element_type=jnp.float32)

    queries, keys, values = (product(inputs, number) for number in range(3))
    grads = product(upstream, 3)
    low = low_lanes(2 * SPAN)
    for half, (first, second) in enumerate(((queries, grads), (keys, values))):
        place = slice(SPAN * half, SPAN * half + SPAN)
        for pair in range(2):
            one = first[:, 128 * pair : 128 * pair + 128]
            two = second[:, 128 * pair : 128 * pair + 128]
            even = jnp.where(low, one, pltpu.roll(two, HEAD, 1))
            odd = jnp.where(low, pltpu.roll(one, HEAD, 1), two)
            for head, rows in ((2 * pair, even), (2 * pair + 1, odd)):
                zero, other = rows[:SPAN], rows[SPAN:]
                keep_ref[head, 0, place, :] = jnp.where(keep_first, zero, other).astype(
                    jnp.bfloat16
                )
                give_ref[head, place, :] = jnp.where(keep_first, other, zero).astype(jnp.bfloat16)


def project(place, tokens, upstream, weights):
    rows_spec = pl.BlockSpec((2, SPAN, D), lambda j, place: (0, 0, 0))
    return pl.pallas_call(
        project_kernel,
        out_shape=(
            jax.ShapeDtypeStruct((HEADS, 2, 2 * SPAN, 128), jnp.bfloat16),
            jax.ShapeDtypeStruct((HEADS, 2 * SPAN, 128), jnp.bfloat16),
        ),
        grid_spec=pltpu.PrefetchScalarGridSpec(
            num_scalar_prefetch=1,
            grid=(2,),
            in_specs=[
                rows_spec,
                rows_spec,
                pl.BlockSpec((4, D, HQ // 2), lambda j, place: (0, 0, j)),
            ],
            out_specs=(
                pl.BlockSpec((HEADS // 2, 1, 2 * SPAN, 128), lambda j, place: (j, place[0], 0, 0)),
                pl.BlockSpec((HEADS // 2, 2 * SPAN, 128), lambda j, place: (j, 0, 0)),
            ),
        ),
        compiler_params=pltpu.CompilerParams(vmem_limit_bytes=PROJECT_VMEM),
        name="project",
    )(place, tokens, upstream, weights)


def attend_kernel(
    core_ref, tiles_ref, own_ref, other_ref, out_ref, own_grad_ref, other_grad_ref,
    key_ref, grad_ref, score_ref, prob_grad_ref,
):
    core = core_ref[0]
    first = tiles_ref[0]
    second = first + tiles_ref[1]
    third = second + tiles_ref[2]
    grad_ref[...] = jnp.zeros_like(grad_ref)
    key_ref[TILES * SPAN :, :] = jnp.zeros((CHUNK, 128), jnp.bfloat16)

    def own_tile(rank):
        return jnp.where(rank % 2 == core, rank, TILES - 1 - rank)

    def tile_rows(tile):
        return pl.ds(pl.multiple_of(tile * SPAN, SPAN), SPAN)

    for rank in range(RANKS):
        tile = own_tile(rank)
        key_ref[tile_rows(tile), :] = own_ref[rank, SPAN:, :]
        key_ref[tile_rows(TILES - 1 - tile), :] = other_ref[rank]


    def tile_start(tile):
        return jnp.where(
            tile >= third, third, jnp.where(tile >= second, second, jnp.where(tile >= first, first, 0))
        )

    def holder(tile):
        return jnp.where(tile < RANKS, tile, TILES - 1 - tile)

    def two_tiles(tile, chunks):
        start, next_start = tile_start(tile), tile_start(tile + 2)
        base = pl.multiple_of(start * SPAN, SPAN)
        ranks = (holder(tile), holder(tile + 2))
        packed = jnp.concatenate([own_ref[rank, :SPAN, :] for rank in ranks], axis=0)
        low = low_lanes(2 * SPAN)
        query_only = jnp.where(low, packed, jnp.zeros_like(packed)) * jnp.bfloat16(HEAD ** -0.5)
        grad_only = jnp.where(low, jnp.zeros_like(packed), packed)
        left = jnp.concatenate([query_only, grad_only], axis=0)
        right = jnp.concatenate([grad_only, query_only], axis=0)
        row = lax.broadcasted_iota(jnp.int32, (2 * SPAN, CHUNK), 0)
        lane = lax.broadcasted_iota(jnp.int32, (2 * SPAN, CHUNK), 1)
        upper = row < SPAN
        last = row + (tile - start) * SPAN + jnp.where(upper, 0, SPAN) - lane
        earliest = jnp.where(upper, 0, (next_start - start) * SPAN) - lane

        def rows(j):
            return pl.ds(pl.multiple_of(base + CHUNK * j, 32), CHUNK)

        top = jnp.full((2 * SPAN, 1), NEGATIVE, jnp.float32)
        for j in range(chunks):
            both = lax.dot_general(
                left, key_ref[rows(j), :], (((1,), (1,)), ((), ())),
                preferred_element_type=jnp.float32,
            )
            allowed = earliest <= CHUNK * j
            if j >= chunks - 3:
                allowed = jnp.logical_and(allowed, last >= CHUNK * j)
            scores = jnp.where(allowed, both[: 2 * SPAN], NEGATIVE)
            place = slice(CHUNK * j, CHUNK * j + CHUNK)
            score_ref[:, place] = scores
            prob_grad_ref[:, place] = both[2 * SPAN :]
            top = jnp.maximum(top, jnp.max(scores, axis=1, keepdims=True))
        total = jnp.zeros((2 * SPAN, 1), jnp.float32)
        accum = jnp.zeros((2 * SPAN, 128), jnp.float32)
        for j in range(chunks):
            place = slice(CHUNK * j, CHUNK * j + CHUNK)
            expo = jnp.exp(score_ref[:, place] - top)
            score_ref[:, place] = expo
            total = total + jnp.sum(expo, axis=1, keepdims=True)
            accum = accum + jnp.dot(
                expo.astype(jnp.bfloat16), key_ref[rows(j), :], preferred_element_type=jnp.float32
            )
        inverse = 1.0 / total
        context = (accum / total).astype(jnp.bfloat16)
        delta = jnp.sum(
            grad_only.astype(jnp.float32) * context.astype(jnp.float32), axis=1, keepdims=True
        )
        query_grad = jnp.zeros((2 * SPAN, 128), jnp.float32)
        for j in range(chunks):
            place = slice(CHUNK * j, CHUNK * j + CHUNK)
            probs = score_ref[:, place] * inverse
            score_grad = (probs * (prob_grad_ref[:, place] - delta)).astype(jnp.bfloat16)
            query_grad = query_grad + jnp.dot(
                score_grad, key_ref[rows(j), :], preferred_element_type=jnp.float32
            )
            stacked = jnp.concatenate([probs.astype(jnp.bfloat16), score_grad], axis=0)
            grad_ref[rows(j), :] += lax.dot_general(
                stacked, right, (((0,), (0,)), ((), ())), preferred_element_type=jnp.float32
            )
        merged = jnp.where(low, query_grad * HEAD ** -0.5, context.astype(jnp.float32)).astype(jnp.bfloat16)
        out_ref[ranks[0]] = merged[:SPAN]
        out_ref[ranks[1]] = merged[SPAN:]

    def one_step(step, carry):
        tile = core + 4 * step
        chunks = ((tile + 3 - tile_start(tile)) * SPAN + CHUNK - 1) // CHUNK
        for count in range(2, 8):
            @pl.when(chunks == count)
            def _():
                two_tiles(tile, count)
        return carry

    lax.fori_loop(0, TILES // 4, one_step, 0)
    for rank in range(RANKS):
        tile = own_tile(rank)
        own_grad_ref[rank] = grad_ref[tile_rows(tile), :]
        other_grad_ref[rank] = grad_ref[tile_rows(TILES - 1 - tile), :].astype(jnp.bfloat16)


def attend(core, tiles, own, other_keys):
    smem = pl.BlockSpec(memory_space=pltpu.SMEM)
    vmem = pl.BlockSpec(memory_space=pltpu.VMEM)
    block = (RANKS, SPAN, 128)
    return pl.pallas_call(
        attend_kernel,
        out_shape=(
            jax.ShapeDtypeStruct(block, jnp.bfloat16),
            jax.ShapeDtypeStruct(block, jnp.float32),
            jax.ShapeDtypeStruct(block, jnp.bfloat16),
        ),
        in_specs=[smem, smem, vmem, vmem],
        out_specs=(vmem, vmem, vmem),
        scratch_shapes=[
            pltpu.VMEM((KEY_ROWS, 128), jnp.bfloat16),
            pltpu.VMEM((KEY_ROWS, 128), jnp.float32),
            pltpu.VMEM((2 * SPAN, 7 * CHUNK), jnp.float32),
            pltpu.VMEM((2 * SPAN, 7 * CHUNK), jnp.float32),
        ],
        compiler_params=pltpu.CompilerParams(vmem_limit_bytes=SMALL_VMEM),
        cost_estimate=pl.CostEstimate(
            flops=12_000_000_000, bytes_accessed=4 * 1024 * 1024, transcendentals=0
        ),
        name="attend",
    )(core, tiles, own, other_keys)


def repack_kernel(column_ref, back_ref, out_ref, *shift_refs):
    low = low_lanes(SPAN)
    for sequence in range(2):
        for half, (lower, upper) in enumerate(((0, 3), (1, 2))):
            place = slice(SPAN * half, SPAN * half + SPAN)
            for pair in range(HEADS // 2):
                columns = slice(128 * pair, 128 * pair + 128)
                one = back_ref[2 * pair, sequence, place, :].astype(jnp.float32)
                two = back_ref[2 * pair + 1, sequence, place, :].astype(jnp.float32)
                out_ref[lower, sequence, :, columns] = jnp.where(
                    low, one, pltpu.roll(two, HEAD, 1)
                ).astype(jnp.bfloat16)
                out_ref[upper, sequence, :, columns] = jnp.where(
                    low, pltpu.roll(one, HEAD, 1), two
                ).astype(jnp.bfloat16)
    for shift, ref in enumerate(shift_refs):
        ref[...] = out_ref[jnp.bitwise_and(column_ref[0] + shift, 3)]


def repack(column, back):
    vmem = pl.BlockSpec(memory_space=pltpu.VMEM)
    return pl.pallas_call(
        repack_kernel,
        out_shape=(
            jax.ShapeDtypeStruct((4, 2, SPAN, HQ), jnp.bfloat16),
            *[jax.ShapeDtypeStruct((2, SPAN, HQ), jnp.bfloat16)] * 4,
        ),
        in_specs=[pl.BlockSpec(memory_space=pltpu.SMEM), vmem],
        out_specs=(vmem,) * 5,
        compiler_params=pltpu.CompilerParams(vmem_limit_bytes=SMALL_VMEM),
        name="repack",
    )(column, back)


def weight_kernel(core_ref, *refs):
    grad_refs, line_refs, (keep_ref, give_ref, held_ref) = refs[:4], refs[4:8], refs[8:]
    core = core_ref[0]

    @pl.when(pl.program_id(0) == 0)
    def _():
        for shift in range(4):
            for part in range(2):
                first = (2 * shift + part) * SPAN
                held_ref[first : first + SPAN, :] = grad_refs[shift][jnp.bitwise_xor(core, part)]

    rows = jnp.concatenate([ref[...].reshape(2 * SPAN, D // 4) for ref in line_refs], axis=0)
    result = lax.dot_general(
        rows, held_ref[...], (((0,), (0,)), ((), ())), preferred_element_type=jnp.float32
    )
    zero, one = result[:, :256], result[:, 256:]
    keep_ref[...] = jnp.where(core == 0, zero, one).astype(jnp.bfloat16).reshape(4, 64, 256)
    give_ref[...] = jnp.where(core == 0, one, zero).astype(jnp.bfloat16).reshape(4, 64, 256)


def weight_terms(core, grads, lines):
    shape = jax.ShapeDtypeStruct((RANKS, 64, 256), jnp.bfloat16)
    grad_spec = pl.BlockSpec((2, SPAN, HQ), lambda j, core: (0, 0, 0))
    line_spec = pl.BlockSpec((2, SPAN, D // 4), lambda j, core: (0, 0, j))
    out_spec = pl.BlockSpec((4, 64, 256), lambda j, core: (j, 0, 0))
    return pl.pallas_call(
        weight_kernel,
        out_shape=(shape, shape),
        grid_spec=pltpu.PrefetchScalarGridSpec(
            num_scalar_prefetch=1,
            grid=(4,),
            in_specs=[
                *[grad_spec] * 4,
                *[line_spec] * 4,
            ],
            out_specs=(out_spec, out_spec),
            scratch_shapes=[pltpu.VMEM((8 * SPAN, HQ), jnp.bfloat16)],
        ),
        compiler_params=pltpu.CompilerParams(vmem_limit_bytes=SMALL_VMEM),
        name="weight_terms",
    )(core, *grads, *lines)


def place_kernel(column_ref, *refs):
    out_ref = refs[4]
    for shift in range(4):
        out_ref[jnp.bitwise_and(column_ref[0] + 4 - shift, 3)] = refs[shift][...]


def place_weights(column, parts):
    vmem = pl.BlockSpec(memory_space=pltpu.VMEM)
    return pl.pallas_call(
        place_kernel,
        out_shape=jax.ShapeDtypeStruct((4, 64, HQ), jnp.bfloat16),
        in_specs=[pl.BlockSpec(memory_space=pltpu.SMEM), vmem, vmem, vmem, vmem],
        out_specs=vmem,
        compiler_params=pltpu.CompilerParams(vmem_limit_bytes=SMALL_VMEM),
        name="place_weights",
    )(column, *parts)


def output_kernel(place_ref, grads_ref, arrived_ref, weights_ref, out_ref, input_grad_ref, held_ref):
    core, odd = place_ref[0], place_ref[1]

    @pl.when(pl.program_id(0) == 0)
    def _():
        for block in range(2):
            mine = jnp.bitwise_xor(odd, block) == core
            for number in range(4):
                held_ref[number, SPAN * block : SPAN * block + SPAN, :] = jnp.where(
                    mine,
                    grads_ref[number, 0].astype(jnp.float32),
                    arrived_ref[number].astype(jnp.float32),
                ).astype(jnp.bfloat16)

    def product(number):
        return lax.dot_general(
            held_ref[number], weights_ref[number], (((1,), (1,)), ((), ())),
            preferred_element_type=jnp.float32,
        )

    out_ref[...] = product(3).astype(jnp.bfloat16).reshape(2, SPAN, D // 4)
    input_grad = product(0) + product(1) + product(2)
    input_grad_ref[...] = input_grad.astype(jnp.bfloat16).reshape(2, SPAN, D // 4)


def outputs(place, grads, arrived, weights):
    shape = jax.ShapeDtypeStruct((2, SPAN, D), jnp.bfloat16)
    out_spec = pl.BlockSpec((2, SPAN, D // 4), lambda j, place: (0, 0, j))
    return pl.pallas_call(
        output_kernel,
        out_shape=(shape, shape),
        grid_spec=pltpu.PrefetchScalarGridSpec(
            num_scalar_prefetch=1,
            grid=(4,),
            in_specs=[
                pl.BlockSpec((4, 1, SPAN, HQ), lambda j, place: (0, place[0], 0, 0)),
                pl.BlockSpec((4, SPAN, HQ), lambda j, place: (0, 0, 0)),
                pl.BlockSpec((4, D // 4, HQ), lambda j, place: (0, j, 0)),
            ],
            out_specs=(out_spec, out_spec),
            scratch_shapes=[pltpu.VMEM((4, 2 * SPAN, HQ), jnp.bfloat16)],
        ),
        compiler_params=pltpu.CompilerParams(vmem_limit_bytes=SMALL_VMEM),
        cost_estimate=pl.CostEstimate(
            flops=8 * 2 * SPAN * D * HQ, bytes_accessed=7 * 1024 * 1024, transcendentals=0
        ),
        name="outputs",
    )(place, grads, arrived, weights)


def per_device(tokens, sweep_tiles, weights, cotangent):
    core = lax.axis_index("dp") % 2
    column = lax.axis_index("dp") // 4
    rank = lax.axis_index("ctx")
    odd = rank % 2
    block = jnp.bitwise_xor(core, odd)

    rows = tokens.reshape(2, SPAN, D)
    upstream = cotangent.reshape(2, SPAN, D)
    other_tiles = lax.ppermute(sweep_tiles, "dp", CORE_SWAP)
    core_number = core.astype(jnp.int32).reshape(1)
    packed, give = project(
        jnp.stack([core, block]).astype(jnp.int32), rows, upstream, weights
    )
    given = lax.ppermute(give, "dp", CORE_SWAP)
    packed = lax.dynamic_update_index_in_dim(packed, given, 1 - core, 1)

    def chosen(x, number):
        return lax.dynamic_index_in_dim(x, number, 0, keepdims=False)

    arrived = lax.ppermute(
        jnp.stack([chosen(x, 1 - block) for x in (rows, upstream)]), "dp", CORE_SWAP
    )
    own_line = [
        jnp.stack([chosen(x, block), arrived[kind]]) for kind, x in enumerate((rows, upstream))
    ]
    packed, other_tiles = lax.optimization_barrier((packed, other_tiles))
    packed = packed.reshape(RANKS, 2 * SPAN, 128)
    line, *lines = (
        jnp.where((column + shift) % 4 == 3, own_line[1], own_line[0]) for shift in range(4)
    )
    near, far, back_near = (
        lax.ppermute(rows, "dp", shift) for rows, shift in zip(lines, X_SHIFTS)
    )
    own = lax.all_to_all(packed, "ctx", 0, 0)
    own, near, back_near = lax.optimization_barrier((own, near, back_near))
    other_keys = lax.ppermute(own[:, SPAN:], "dp", CORE_SWAP)
    tiles = jnp.where(odd == core, sweep_tiles, other_tiles).reshape(-1)
    query_part, own_grad, other_grad = attend(core_number, tiles, own, other_keys)
    arrived = lax.ppermute(other_grad, "dp", CORE_SWAP)
    key_part = (own_grad + arrived.astype(jnp.float32)).astype(jnp.bfloat16)
    back = lax.all_to_all(jnp.concatenate([query_part, key_part], axis=1), "ctx", 0, 0)
    grads, *pieces = repack(
        column.astype(jnp.int32).reshape(1), back.reshape(HEADS, 2, 2 * SPAN, 128)
    )
    pieces, far = lax.optimization_barrier((pieces, far))
    pieces = [pieces[0]] + [lax.ppermute(x, "dp", y) for x, y in zip(pieces[1:], X_SHIFTS)]
    keep, give = weight_terms(core_number, pieces, (line, near, far, back_near))
    given = lax.ppermute(give, "dp", CORE_SWAP)
    terms = (keep.astype(jnp.float32) + given.astype(jnp.float32)).astype(jnp.bfloat16)
    terms, own_grads = lax.optimization_barrier((terms, grads))
    terms = lax.all_to_all(terms, "ctx", 0, 0)
    swapped = lax.ppermute(
        lax.dynamic_index_in_dim(grads, 1 - core, 1, keepdims=False), "dp", CORE_SWAP
    )
    place = jnp.stack([core, odd]).astype(jnp.int32)
    attn_out, input_grad = outputs(place, own_grads, swapped, weights)
    terms, attn_out, input_grad = lax.optimization_barrier((terms, attn_out, input_grad))
    rows = lax.reduce_precision(jnp.sum(terms.astype(jnp.float32), axis=0), 8, 7)
    other_rows = lax.ppermute(rows.astype(jnp.bfloat16), "dp", Z_SWAP)
    factor = float(16 * RANKS * 2 * SPAN) ** -0.5
    total = ((rows + other_rows.astype(jnp.float32)) * factor).astype(jnp.bfloat16)
    other_total = lax.ppermute(total, "dp", CORE_SWAP)
    first = core == 0
    part = jnp.concatenate(
        [jnp.where(first, total, other_total), jnp.where(first, other_total, total)], axis=1
    )
    parts = [part] + [lax.ppermute(part, "dp", shift) for shift in X_SHIFTS]
    weight_grads = place_weights(column.astype(jnp.int32).reshape(1), parts)
    return (attn_out.reshape(tokens.shape), input_grad.reshape(tokens.shape), weight_grads)


def solution(mesh):
    placed = (
        P("dp", "ctx", None, None, None),
        P("dp", None),
        P(),
        P("dp", "ctx", None, None, None),
    )
    return jax.shard_map(
        per_device,
        mesh=mesh,
        in_specs=placed,
        out_specs=(
            P("dp", "ctx", None, None, None),
            P("dp", "ctx", None, None, None),
            P(None, "ctx", None),
        ),
        check_vma=False,
    )
```

```python
import jax
import jax.numpy as jnp
from jax import lax
from jax.experimental import pallas as pl
from jax.experimental.pallas import tpu as pltpu
from jax.sharding import PartitionSpec as P

D = 1024
HEADS = 8
HEAD = 64
HQ = HEADS * HEAD
SPAN = 96
RANKS = 16
TILES = 2 * RANKS
CHUNK = 256
KEY_ROWS = TILES * SPAN + CHUNK
NEGATIVE = -1e30
SMALL_VMEM = 24 * 1024 * 1024
PROJECT_VMEM = 60 * 1024 * 1024

CORE_SWAP = [(i, i ^ 1) for i in range(16)]
Z_SWAP = [(i, i ^ 2) for i in range(16)]
BOTH_SWAP = [(i, i ^ 3) for i in range(16)]
X_SHIFTS = [[(i, (i + 4 * shift) % 16) for i in range(16)] for shift in range(1, 4)]


def low_lanes(rows):
    return lax.broadcasted_iota(jnp.int32, (rows, 128), 1) < HEAD


def project_kernel(place_ref, tokens_ref, upstream_ref, weights_ref, keep_ref, give_ref):
    keep_first = place_ref[1] == 0
    inputs = tokens_ref[...].reshape(2 * SPAN, D)
    upstream = upstream_ref[...].reshape(2 * SPAN, D)

    def product(rows, number):
        return jnp.dot(rows, weights_ref[number], preferred_element_type=jnp.float32)

    queries, keys, values = (product(inputs, number) for number in range(3))
    grads = product(upstream, 3)
    low = low_lanes(2 * SPAN)
    for half, (first, second) in enumerate(((queries, grads), (keys, values))):
        place = slice(SPAN * half, SPAN * half + SPAN)
        for pair in range(2):
            one = first[:, 128 * pair : 128 * pair + 128]
            two = second[:, 128 * pair : 128 * pair + 128]
            even = jnp.where(low, one, pltpu.roll(two, HEAD, 1))
            odd = jnp.where(low, pltpu.roll(one, HEAD, 1), two)
            for head, rows in ((2 * pair, even), (2 * pair + 1, odd)):
                zero, other = rows[:SPAN], rows[SPAN:]
                keep_ref[head, 0, place, :] = jnp.where(keep_first, zero, other).astype(
                    jnp.bfloat16
                )
                give_ref[head, place, :] = jnp.where(keep_first, other, zero).astype(jnp.bfloat16)


def project(place, tokens, upstream, weights):
    rows_spec = pl.BlockSpec((2, SPAN, D), lambda j, place: (0, 0, 0))
    return pl.pallas_call(
        project_kernel,
        out_shape=(
            jax.ShapeDtypeStruct((HEADS, 2, 2 * SPAN, 128), jnp.bfloat16),
            jax.ShapeDtypeStruct((HEADS, 2 * SPAN, 128), jnp.bfloat16),
        ),
        grid_spec=pltpu.PrefetchScalarGridSpec(
            num_scalar_prefetch=1,
            grid=(2,),
            in_specs=[
                rows_spec,
                rows_spec,
                pl.BlockSpec((4, D, HQ // 2), lambda j, place: (0, 0, j)),
            ],
            out_specs=(
                pl.BlockSpec((HEADS // 2, 1, 2 * SPAN, 128), lambda j, place: (j, place[0], 0, 0)),
                pl.BlockSpec((HEADS // 2, 2 * SPAN, 128), lambda j, place: (j, 0, 0)),
            ),
        ),
        compiler_params=pltpu.CompilerParams(vmem_limit_bytes=PROJECT_VMEM),
        name="project",
    )(place, tokens, upstream, weights)


def attend_kernel(
    core_ref, tiles_ref, own_ref, other_ref, out_ref, own_grad_ref, other_grad_ref,
    key_ref, grad_ref, score_ref, prob_grad_ref,
):
    core = core_ref[0]
    first = tiles_ref[0]
    second = first + tiles_ref[1]
    third = second + tiles_ref[2]
    grad_ref[...] = jnp.zeros_like(grad_ref)
    key_ref[TILES * SPAN :, :] = jnp.zeros((CHUNK, 128), jnp.bfloat16)

    def own_tile(rank):
        return jnp.where(rank % 2 == core, rank, TILES - 1 - rank)

    def tile_rows(tile):
        return pl.ds(pl.multiple_of(tile * SPAN, SPAN), SPAN)

    for rank in range(RANKS):
        tile = own_tile(rank)
        key_ref[tile_rows(tile), :] = own_ref[rank, SPAN:, :]
        key_ref[tile_rows(TILES - 1 - tile), :] = other_ref[rank]


    def tile_start(tile):
        return jnp.where(
            tile >= third, third, jnp.where(tile >= second, second, jnp.where(tile >= first, first, 0))
        )

    def holder(tile):
        return jnp.where(tile < RANKS, tile, TILES - 1 - tile)

    def two_tiles(tile, chunks):
        start, next_start = tile_start(tile), tile_start(tile + 2)
        base = pl.multiple_of(start * SPAN, SPAN)
        ranks = (holder(tile), holder(tile + 2))
        packed = jnp.concatenate([own_ref[rank, :SPAN, :] for rank in ranks], axis=0)
        low = low_lanes(2 * SPAN)
        query_only = jnp.where(low, packed, jnp.zeros_like(packed)) * jnp.bfloat16(HEAD ** -0.5)
        grad_only = jnp.where(low, jnp.zeros_like(packed), packed)
        left = jnp.concatenate([query_only, grad_only], axis=0)
        right = jnp.concatenate([grad_only, query_only], axis=0)
        row = lax.broadcasted_iota(jnp.int32, (2 * SPAN, CHUNK), 0)
        lane = lax.broadcasted_iota(jnp.int32, (2 * SPAN, CHUNK), 1)
        upper = row < SPAN
        last = row + (tile - start) * SPAN + jnp.where(upper, 0, SPAN) - lane
        earliest = jnp.where(upper, 0, (next_start - start) * SPAN) - lane

        def rows(j):
            return pl.ds(pl.multiple_of(base + CHUNK * j, 32), CHUNK)

        top = jnp.full((2 * SPAN, 1), NEGATIVE, jnp.float32)
        for j in range(chunks):
            both = lax.dot_general(
                left, key_ref[rows(j), :], (((1,), (1,)), ((), ())),
                preferred_element_type=jnp.float32,
            )
            allowed = earliest <= CHUNK * j
            if j >= chunks - 3:
                allowed = jnp.logical_and(allowed, last >= CHUNK * j)
            scores = jnp.where(allowed, both[: 2 * SPAN], NEGATIVE)
            place = slice(CHUNK * j, CHUNK * j + CHUNK)
            score_ref[:, place] = scores
            prob_grad_ref[:, place] = both[2 * SPAN :]
            top = jnp.maximum(top, jnp.max(scores, axis=1, keepdims=True))
        total = jnp.zeros((2 * SPAN, 1), jnp.float32)
        accum = jnp.zeros((2 * SPAN, 128), jnp.float32)
        for j in range(chunks):
            place = slice(CHUNK * j, CHUNK * j + CHUNK)
            expo = jnp.exp(score_ref[:, place] - top)
            score_ref[:, place] = expo
            total = total + jnp.sum(expo, axis=1, keepdims=True)
            accum = accum + jnp.dot(
                expo.astype(jnp.bfloat16), key_ref[rows(j), :], preferred_element_type=jnp.float32
            )
        inverse = 1.0 / total
        context = (accum / total).astype(jnp.bfloat16)
        delta = jnp.sum(
            grad_only.astype(jnp.float32) * context.astype(jnp.float32), axis=1, keepdims=True
        )
        query_grad = jnp.zeros((2 * SPAN, 128), jnp.float32)
        for j in range(chunks):
            place = slice(CHUNK * j, CHUNK * j + CHUNK)
            probs = score_ref[:, place] * inverse
            score_grad = (probs * (prob_grad_ref[:, place] - delta)).astype(jnp.bfloat16)
            query_grad = query_grad + jnp.dot(
                score_grad, key_ref[rows(j), :], preferred_element_type=jnp.float32
            )
            stacked = jnp.concatenate([probs.astype(jnp.bfloat16), score_grad], axis=0)
            grad_ref[rows(j), :] += lax.dot_general(
                stacked, right, (((0,), (0,)), ((), ())), preferred_element_type=jnp.float32
            )
        merged = jnp.where(low, query_grad * HEAD ** -0.5, context.astype(jnp.float32)).astype(jnp.bfloat16)
        out_ref[ranks[0]] = merged[:SPAN]
        out_ref[ranks[1]] = merged[SPAN:]

    def one_step(step, carry):
        tile = core + 4 * step
        chunks = ((tile + 3 - tile_start(tile)) * SPAN + CHUNK - 1) // CHUNK
        for count in range(2, 8):
            @pl.when(chunks == count)
            def _():
                two_tiles(tile, count)
        return carry

    lax.fori_loop(0, TILES // 4, one_step, 0)
    for rank in range(RANKS):
        tile = own_tile(rank)
        own_grad_ref[rank] = grad_ref[tile_rows(tile), :]
        other_grad_ref[rank] = grad_ref[tile_rows(TILES - 1 - tile), :].astype(jnp.bfloat16)


def attend(core, tiles, own, other_keys):
    smem = pl.BlockSpec(memory_space=pltpu.SMEM)
    vmem = pl.BlockSpec(memory_space=pltpu.VMEM)
    block = (RANKS, SPAN, 128)
    return pl.pallas_call(
        attend_kernel,
        out_shape=(
            jax.ShapeDtypeStruct(block, jnp.bfloat16),
            jax.ShapeDtypeStruct(block, jnp.float32),
            jax.ShapeDtypeStruct(block, jnp.bfloat16),
        ),
        in_specs=[smem, smem, vmem, vmem],
        out_specs=(vmem, vmem, vmem),
        scratch_shapes=[
            pltpu.VMEM((KEY_ROWS, 128), jnp.bfloat16),
            pltpu.VMEM((KEY_ROWS, 128), jnp.float32),
            pltpu.VMEM((2 * SPAN, 7 * CHUNK), jnp.float32),
            pltpu.VMEM((2 * SPAN, 7 * CHUNK), jnp.float32),
        ],
        compiler_params=pltpu.CompilerParams(vmem_limit_bytes=SMALL_VMEM),
        cost_estimate=pl.CostEstimate(
            flops=12_000_000_000, bytes_accessed=4 * 1024 * 1024, transcendentals=0
        ),
        name="attend",
    )(core, tiles, own, other_keys)


def repack_kernel(column_ref, back_ref, out_ref, *shift_refs):
    low = low_lanes(SPAN)
    for sequence in range(2):
        for half, (lower, upper) in enumerate(((0, 3), (1, 2))):
            place = slice(SPAN * half, SPAN * half + SPAN)
            for pair in range(HEADS // 2):
                columns = slice(128 * pair, 128 * pair + 128)
                one = back_ref[2 * pair, sequence, place, :].astype(jnp.float32)
                two = back_ref[2 * pair + 1, sequence, place, :].astype(jnp.float32)
                out_ref[lower, sequence, :, columns] = jnp.where(
                    low, one, pltpu.roll(two, HEAD, 1)
                ).astype(jnp.bfloat16)
                out_ref[upper, sequence, :, columns] = jnp.where(
                    low, pltpu.roll(one, HEAD, 1), two
                ).astype(jnp.bfloat16)
    for shift, ref in enumerate(shift_refs):
        ref[...] = out_ref[jnp.bitwise_and(column_ref[0] + shift, 3)]


def repack(column, back):
    vmem = pl.BlockSpec(memory_space=pltpu.VMEM)
    return pl.pallas_call(
        repack_kernel,
        out_shape=(
            jax.ShapeDtypeStruct((4, 2, SPAN, HQ), jnp.bfloat16),
            *[jax.ShapeDtypeStruct((2, SPAN, HQ), jnp.bfloat16)] * 4,
        ),
        in_specs=[pl.BlockSpec(memory_space=pltpu.SMEM), vmem],
        out_specs=(vmem,) * 5,
        compiler_params=pltpu.CompilerParams(vmem_limit_bytes=SMALL_VMEM),
        name="repack",
    )(column, back)


def weight_kernel(core_ref, *refs):
    grad_refs, line_refs, (keep_ref, give_ref, held_ref) = refs[:4], refs[4:8], refs[8:]
    core = core_ref[0]

    @pl.when(pl.program_id(0) == 0)
    def _():
        for shift in range(4):
            for part in range(2):
                first = (2 * shift + part) * SPAN
                held_ref[first : first + SPAN, :] = grad_refs[shift][jnp.bitwise_xor(core, part)]

    rows = jnp.concatenate([ref[...].reshape(2 * SPAN, D // 4) for ref in line_refs], axis=0)
    result = lax.dot_general(
        rows, held_ref[...], (((0,), (0,)), ((), ())), preferred_element_type=jnp.float32
    )
    zero, one = result[:, :256], result[:, 256:]
    keep_ref[...] = jnp.where(core == 0, zero, one).astype(jnp.bfloat16).reshape(4, 64, 256)
    give_ref[...] = jnp.where(core == 0, one, zero).astype(jnp.bfloat16).reshape(4, 64, 256)


def weight_terms(core, grads, lines):
    shape = jax.ShapeDtypeStruct((RANKS, 64, 256), jnp.bfloat16)
    grad_spec = pl.BlockSpec((2, SPAN, HQ), lambda j, core: (0, 0, 0))
    line_spec = pl.BlockSpec((2, SPAN, D // 4), lambda j, core: (0, 0, j))
    out_spec = pl.BlockSpec((4, 64, 256), lambda j, core: (j, 0, 0))
    return pl.pallas_call(
        weight_kernel,
        out_shape=(shape, shape),
        grid_spec=pltpu.PrefetchScalarGridSpec(
            num_scalar_prefetch=1,
            grid=(4,),
            in_specs=[
                *[grad_spec] * 4,
                *[line_spec] * 4,
            ],
            out_specs=(out_spec, out_spec),
            scratch_shapes=[pltpu.VMEM((8 * SPAN, HQ), jnp.bfloat16)],
        ),
        compiler_params=pltpu.CompilerParams(vmem_limit_bytes=SMALL_VMEM),
        name="weight_terms",
    )(core, *grads, *lines)


def place_kernel(column_ref, *refs):
    out_ref = refs[4]
    for shift in range(4):
        out_ref[jnp.bitwise_and(column_ref[0] + 4 - shift, 3)] = refs[shift][...]


def place_weights(column, parts):
    vmem = pl.BlockSpec(memory_space=pltpu.VMEM)
    return pl.pallas_call(
        place_kernel,
        out_shape=jax.ShapeDtypeStruct((4, 64, HQ), jnp.bfloat16),
        in_specs=[pl.BlockSpec(memory_space=pltpu.SMEM), vmem, vmem, vmem, vmem],
        out_specs=vmem,
        compiler_params=pltpu.CompilerParams(vmem_limit_bytes=SMALL_VMEM),
        name="place_weights",
    )(column, *parts)


def output_kernel(place_ref, grads_ref, arrived_ref, weights_ref, out_ref, input_grad_ref, held_ref):
    core, odd = place_ref[0], place_ref[1]

    @pl.when(pl.program_id(0) == 0)
    def _():
        for block in range(2):
            mine = jnp.bitwise_xor(odd, block) == core
            for number in range(4):
                held_ref[number, SPAN * block : SPAN * block + SPAN, :] = jnp.where(
                    mine,
                    grads_ref[number, 0].astype(jnp.float32),
                    arrived_ref[number].astype(jnp.float32),
                ).astype(jnp.bfloat16)

    def product(number):
        return lax.dot_general(
            held_ref[number], weights_ref[number], (((1,), (1,)), ((), ())),
            preferred_element_type=jnp.float32,
        )

    out_ref[...] = product(3).astype(jnp.bfloat16).reshape(2, SPAN, D // 4)
    input_grad = product(0) + product(1) + product(2)
    input_grad_ref[...] = input_grad.astype(jnp.bfloat16).reshape(2, SPAN, D // 4)


def outputs(place, grads, arrived, weights):
    shape = jax.ShapeDtypeStruct((2, SPAN, D), jnp.bfloat16)
    out_spec = pl.BlockSpec((2, SPAN, D // 4), lambda j, place: (0, 0, j))
    return pl.pallas_call(
        output_kernel,
        out_shape=(shape, shape),
        grid_spec=pltpu.PrefetchScalarGridSpec(
            num_scalar_prefetch=1,
            grid=(4,),
            in_specs=[
                pl.BlockSpec((4, 1, SPAN, HQ), lambda j, place: (0, place[0], 0, 0)),
                pl.BlockSpec((4, SPAN, HQ), lambda j, place: (0, 0, 0)),
                pl.BlockSpec((4, D // 4, HQ), lambda j, place: (0, j, 0)),
            ],
            out_specs=(out_spec, out_spec),
            scratch_shapes=[pltpu.VMEM((4, 2 * SPAN, HQ), jnp.bfloat16)],
        ),
        compiler_params=pltpu.CompilerParams(vmem_limit_bytes=SMALL_VMEM),
        cost_estimate=pl.CostEstimate(
            flops=8 * 2 * SPAN * D * HQ, bytes_accessed=7 * 1024 * 1024, transcendentals=0
        ),
        name="outputs",
    )(place, grads, arrived, weights)


def per_device(tokens, sweep_tiles, weights, cotangent):
    core = lax.axis_index("dp") % 2
    column = lax.axis_index("dp") // 4
    rank = lax.axis_index("ctx")
    odd = rank % 2
    block = jnp.bitwise_xor(core, odd)

    rows = tokens.reshape(2, SPAN, D)
    upstream = cotangent.reshape(2, SPAN, D)
    other_tiles = lax.ppermute(sweep_tiles, "dp", CORE_SWAP)
    core_number = core.astype(jnp.int32).reshape(1)
    packed, give = project(
        jnp.stack([core, block]).astype(jnp.int32), rows, upstream, weights
    )
    given = lax.ppermute(give, "dp", CORE_SWAP)
    packed = lax.dynamic_update_index_in_dim(packed, given, 1 - core, 1)

    def chosen(x, number):
        return lax.dynamic_index_in_dim(x, number, 0, keepdims=False)

    arrived = lax.ppermute(
        jnp.stack([chosen(x, 1 - block) for x in (rows, upstream)]), "dp", CORE_SWAP
    )
    own_line = [
        jnp.stack([chosen(x, block), arrived[kind]]) for kind, x in enumerate((rows, upstream))
    ]
    packed, other_tiles = lax.optimization_barrier((packed, other_tiles))
    packed = packed.reshape(RANKS, 2 * SPAN, 128)
    line, *lines = (
        jnp.where((column + shift) % 4 == 3, own_line[1], own_line[0]) for shift in range(4)
    )
    near, far, back_near = (
        lax.ppermute(rows, "dp", shift) for rows, shift in zip(lines, X_SHIFTS)
    )
    own = lax.all_to_all(packed, "ctx", 0, 0)
    own, near, back_near = lax.optimization_barrier((own, near, back_near))
    other_keys = lax.ppermute(own[:, SPAN:], "dp", CORE_SWAP)
    tiles = jnp.where(odd == core, sweep_tiles, other_tiles).reshape(-1)
    query_part, own_grad, other_grad = attend(core_number, tiles, own, other_keys)
    arrived = lax.ppermute(other_grad, "dp", CORE_SWAP)
    key_part = (own_grad + arrived.astype(jnp.float32)).astype(jnp.bfloat16)
    back = lax.all_to_all(jnp.concatenate([query_part, key_part], axis=1), "ctx", 0, 0)
    grads, *pieces = repack(
        column.astype(jnp.int32).reshape(1), back.reshape(HEADS, 2, 2 * SPAN, 128)
    )
    pieces, far = lax.optimization_barrier((pieces, far))
    pieces = [pieces[0]] + [lax.ppermute(x, "dp", y) for x, y in zip(pieces[1:], X_SHIFTS)]
    keep, give = weight_terms(core_number, pieces, (line, near, far, back_near))
    given = lax.ppermute(give, "dp", CORE_SWAP)
    terms = (keep.astype(jnp.float32) + given.astype(jnp.float32)).astype(jnp.bfloat16)
    terms, own_grads = lax.optimization_barrier((terms, grads))
    terms = lax.all_to_all(terms, "ctx", 0, 0)
    swapped = lax.ppermute(
        lax.dynamic_index_in_dim(grads, 1 - core, 1, keepdims=False), "dp", CORE_SWAP
    )
    place = jnp.stack([core, odd]).astype(jnp.int32)
    attn_out, input_grad = outputs(place, own_grads, swapped, weights)
    terms, attn_out, input_grad = lax.optimization_barrier((terms, attn_out, input_grad))
    rows = lax.reduce_precision(jnp.sum(terms.astype(jnp.float32), axis=0), 8, 7)
    rows_low = rows.astype(jnp.bfloat16)
    other_rows, core_rows, far_rows = (
        lax.ppermute(rows_low, "dp", swap).astype(jnp.float32)
        for swap in (Z_SWAP, CORE_SWAP, BOTH_SWAP)
    )
    factor = float(16 * RANKS * 2 * SPAN) ** -0.5
    total = ((rows + other_rows) * factor).astype(jnp.bfloat16)
    other_total = ((core_rows + far_rows) * factor).astype(jnp.bfloat16)
    first = core == 0
    part = jnp.concatenate(
        [jnp.where(first, total, other_total), jnp.where(first, other_total, total)], axis=1
    )
    parts = [part] + [lax.ppermute(part, "dp", shift) for shift in X_SHIFTS]
    weight_grads = place_weights(column.astype(jnp.int32).reshape(1), parts)
    return (attn_out.reshape(tokens.shape), input_grad.reshape(tokens.shape), weight_grads)


def solution(mesh):
    placed = (
        P("dp", "ctx", None, None, None),
        P("dp", None),
        P(),
        P("dp", "ctx", None, None, None),
    )
    return jax.shard_map(
        per_device,
        mesh=mesh,
        in_specs=placed,
        out_specs=(
            P("dp", "ctx", None, None, None),
            P("dp", "ctx", None, None, None),
            P(None, "ctx", None),
        ),
        check_vma=False,
    )
```

```python
import jax
import jax.numpy as jnp
from jax import lax
from jax.experimental import pallas as pl
from jax.experimental.pallas import tpu as pltpu
from jax.sharding import PartitionSpec as P

D = 1024
HEADS = 8
HEAD = 64
HQ = HEADS * HEAD
SPAN = 96
RANKS = 16
TILES = 2 * RANKS
CHUNK = 256
KEY_ROWS = TILES * SPAN + CHUNK
NEGATIVE = -1e30
SMALL_VMEM = 24 * 1024 * 1024
PROJECT_VMEM = 60 * 1024 * 1024

CORE_SWAP = [(i, i ^ 1) for i in range(16)]
Z_SWAP = [(i, i ^ 2) for i in range(16)]
X_SHIFTS = [[(i, (i + 4 * shift) % 16) for i in range(16)] for shift in range(1, 4)]


def low_lanes(rows):
    return lax.broadcasted_iota(jnp.int32, (rows, 128), 1) < HEAD


def project_kernel(place_ref, tokens_ref, upstream_ref, weights_ref, keep_ref, give_ref):
    keep_first = place_ref[1] == 0
    inputs = tokens_ref[...].reshape(2 * SPAN, D)
    upstream = upstream_ref[...].reshape(2 * SPAN, D)

    def product(rows, number):
        return jnp.dot(rows, weights_ref[number], preferred_element_type=jnp.float32)

    queries, keys, values = (product(inputs, number) for number in range(3))
    grads = product(upstream, 3)
    low = low_lanes(2 * SPAN)
    for half, (first, second) in enumerate(((queries, grads), (keys, values))):
        place = slice(SPAN * half, SPAN * half + SPAN)
        for pair in range(2):
            one = first[:, 128 * pair : 128 * pair + 128]
            two = second[:, 128 * pair : 128 * pair + 128]
            even = jnp.where(low, one, pltpu.roll(two, HEAD, 1))
            odd = jnp.where(low, pltpu.roll(one, HEAD, 1), two)
            for head, rows in ((2 * pair, even), (2 * pair + 1, odd)):
                zero, other = rows[:SPAN], rows[SPAN:]
                keep_ref[head, 0, place, :] = jnp.where(keep_first, zero, other).astype(
                    jnp.bfloat16
                )
                give_ref[head, place, :] = jnp.where(keep_first, other, zero).astype(jnp.bfloat16)


def project(place, tokens, upstream, weights):
    rows_spec = pl.BlockSpec((2, SPAN, D), lambda j, place: (0, 0, 0))
    return pl.pallas_call(
        project_kernel,
        out_shape=(
            jax.ShapeDtypeStruct((HEADS, 2, 2 * SPAN, 128), jnp.bfloat16),
            jax.ShapeDtypeStruct((HEADS, 2 * SPAN, 128), jnp.bfloat16),
        ),
        grid_spec=pltpu.PrefetchScalarGridSpec(
            num_scalar_prefetch=1,
            grid=(2,),
            in_specs=[
                rows_spec,
                rows_spec,
                pl.BlockSpec((4, D, HQ // 2), lambda j, place: (0, 0, j)),
            ],
            out_specs=(
                pl.BlockSpec((HEADS // 2, 1, 2 * SPAN, 128), lambda j, place: (j, place[0], 0, 0)),
                pl.BlockSpec((HEADS // 2, 2 * SPAN, 128), lambda j, place: (j, 0, 0)),
            ),
        ),
        compiler_params=pltpu.CompilerParams(vmem_limit_bytes=PROJECT_VMEM),
        name="project",
    )(place, tokens, upstream, weights)


def attend_kernel(
    core_ref, tiles_ref, own_ref, other_ref, out_ref, own_grad_ref, other_grad_ref,
    key_ref, grad_ref, score_ref, prob_grad_ref,
):
    core = core_ref[0]
    first = tiles_ref[0]
    second = first + tiles_ref[1]
    third = second + tiles_ref[2]
    grad_ref[...] = jnp.zeros_like(grad_ref)
    key_ref[TILES * SPAN :, :] = jnp.zeros((CHUNK, 128), jnp.bfloat16)

    def own_tile(rank):
        return jnp.where(rank % 2 == core, rank, TILES - 1 - rank)

    def tile_rows(tile):
        return pl.ds(pl.multiple_of(tile * SPAN, SPAN), SPAN)

    for rank in range(RANKS):
        tile = own_tile(rank)
        key_ref[tile_rows(tile), :] = own_ref[rank, SPAN:, :]
        key_ref[tile_rows(TILES - 1 - tile), :] = other_ref[rank]


    def tile_start(tile):
        return jnp.where(
            tile >= third, third, jnp.where(tile >= second, second, jnp.where(tile >= first, first, 0))
        )

    def holder(tile):
        return jnp.where(tile < RANKS, tile, TILES - 1 - tile)

    def two_tiles(tile, chunks):
        start, next_start = tile_start(tile), tile_start(tile + 2)
        base = pl.multiple_of(start * SPAN, SPAN)
        ranks = (holder(tile), holder(tile + 2))
        packed = jnp.concatenate([own_ref[rank, :SPAN, :] for rank in ranks], axis=0)
        low = low_lanes(2 * SPAN)
        query_only = jnp.where(low, packed, jnp.zeros_like(packed)) * jnp.bfloat16(HEAD ** -0.5)
        grad_only = jnp.where(low, jnp.zeros_like(packed), packed)
        left = jnp.concatenate([query_only, grad_only], axis=0)
        right = jnp.concatenate([grad_only, query_only], axis=0)
        row = lax.broadcasted_iota(jnp.int32, (2 * SPAN, CHUNK), 0)
        lane = lax.broadcasted_iota(jnp.int32, (2 * SPAN, CHUNK), 1)
        upper = row < SPAN
        last = row + (tile - start) * SPAN + jnp.where(upper, 0, SPAN) - lane
        earliest = jnp.where(upper, 0, (next_start - start) * SPAN) - lane

        def rows(j):
            return pl.ds(pl.multiple_of(base + CHUNK * j, 32), CHUNK)

        top = jnp.full((2 * SPAN, 1), NEGATIVE, jnp.float32)
        for j in range(chunks):
            both = lax.dot_general(
                left, key_ref[rows(j), :], (((1,), (1,)), ((), ())),
                preferred_element_type=jnp.float32,
            )
            allowed = earliest <= CHUNK * j
            if j >= chunks - 3:
                allowed = jnp.logical_and(allowed, last >= CHUNK * j)
            scores = jnp.where(allowed, both[: 2 * SPAN], NEGATIVE)
            place = slice(CHUNK * j, CHUNK * j + CHUNK)
            score_ref[:, place] = scores
            prob_grad_ref[:, place] = both[2 * SPAN :]
            top = jnp.maximum(top, jnp.max(scores, axis=1, keepdims=True))
        total = jnp.zeros((2 * SPAN, 1), jnp.float32)
        accum = jnp.zeros((2 * SPAN, 128), jnp.float32)
        for j in range(chunks):
            place = slice(CHUNK * j, CHUNK * j + CHUNK)
            expo = jnp.exp(score_ref[:, place] - top)
            score_ref[:, place] = expo
            total = total + jnp.sum(expo, axis=1, keepdims=True)
            accum = accum + jnp.dot(
                expo.astype(jnp.bfloat16), key_ref[rows(j), :], preferred_element_type=jnp.float32
            )
        inverse = 1.0 / total
        context = (accum / total).astype(jnp.bfloat16)
        delta = jnp.sum(
            grad_only.astype(jnp.float32) * context.astype(jnp.float32), axis=1, keepdims=True
        )
        query_grad = jnp.zeros((2 * SPAN, 128), jnp.float32)
        for j in range(chunks):
            place = slice(CHUNK * j, CHUNK * j + CHUNK)
            probs = score_ref[:, place] * inverse
            score_grad = (probs * (prob_grad_ref[:, place] - delta)).astype(jnp.bfloat16)
            query_grad = query_grad + jnp.dot(
                score_grad, key_ref[rows(j), :], preferred_element_type=jnp.float32
            )
            stacked = jnp.concatenate([probs.astype(jnp.bfloat16), score_grad], axis=0)
            grad_ref[rows(j), :] += lax.dot_general(
                stacked, right, (((0,), (0,)), ((), ())), preferred_element_type=jnp.float32
            )
        merged = jnp.where(low, query_grad * HEAD ** -0.5, context.astype(jnp.float32)).astype(jnp.bfloat16)
        out_ref[ranks[0]] = merged[:SPAN]
        out_ref[ranks[1]] = merged[SPAN:]

    def one_step(step, carry):
        tile = core + 4 * step
        chunks = ((tile + 3 - tile_start(tile)) * SPAN + CHUNK - 1) // CHUNK
        for count in range(2, 8):
            @pl.when(chunks == count)
            def _():
                two_tiles(tile, count)
        return carry

    lax.fori_loop(0, TILES // 4, one_step, 0)
    for rank in range(RANKS):
        tile = own_tile(rank)
        own_grad_ref[rank] = grad_ref[tile_rows(tile), :]
        other_grad_ref[rank] = grad_ref[tile_rows(TILES - 1 - tile), :].astype(jnp.bfloat16)


def attend(core, tiles, own, other_keys):
    smem = pl.BlockSpec(memory_space=pltpu.SMEM)
    vmem = pl.BlockSpec(memory_space=pltpu.VMEM)
    block = (RANKS, SPAN, 128)
    return pl.pallas_call(
        attend_kernel,
        out_shape=(
            jax.ShapeDtypeStruct(block, jnp.bfloat16),
            jax.ShapeDtypeStruct(block, jnp.float32),
            jax.ShapeDtypeStruct(block, jnp.bfloat16),
        ),
        in_specs=[smem, smem, vmem, vmem],
        out_specs=(vmem, vmem, vmem),
        scratch_shapes=[
            pltpu.VMEM((KEY_ROWS, 128), jnp.bfloat16),
            pltpu.VMEM((KEY_ROWS, 128), jnp.float32),
            pltpu.VMEM((2 * SPAN, 7 * CHUNK), jnp.float32),
            pltpu.VMEM((2 * SPAN, 7 * CHUNK), jnp.float32),
        ],
        compiler_params=pltpu.CompilerParams(vmem_limit_bytes=SMALL_VMEM),
        cost_estimate=pl.CostEstimate(
            flops=12_000_000_000, bytes_accessed=4 * 1024 * 1024, transcendentals=0
        ),
        name="attend",
    )(core, tiles, own, other_keys)


def repack_kernel(column_ref, back_ref, out_ref, *shift_refs):
    low = low_lanes(SPAN)
    for sequence in range(2):
        for half, (lower, upper) in enumerate(((0, 3), (1, 2))):
            place = slice(SPAN * half, SPAN * half + SPAN)
            for pair in range(HEADS // 2):
                columns = slice(128 * pair, 128 * pair + 128)
                one = back_ref[2 * pair, sequence, place, :].astype(jnp.float32)
                two = back_ref[2 * pair + 1, sequence, place, :].astype(jnp.float32)
                out_ref[lower, sequence, :, columns] = jnp.where(
                    low, one, pltpu.roll(two, HEAD, 1)
                ).astype(jnp.bfloat16)
                out_ref[upper, sequence, :, columns] = jnp.where(
                    low, pltpu.roll(one, HEAD, 1), two
                ).astype(jnp.bfloat16)
    for shift, ref in enumerate(shift_refs):
        ref[...] = out_ref[jnp.bitwise_and(column_ref[0] + shift, 3)]


def repack(column, back):
    vmem = pl.BlockSpec(memory_space=pltpu.VMEM)
    return pl.pallas_call(
        repack_kernel,
        out_shape=(
            jax.ShapeDtypeStruct((4, 2, SPAN, HQ), jnp.bfloat16),
            *[jax.ShapeDtypeStruct((2, SPAN, HQ), jnp.bfloat16)] * 4,
        ),
        in_specs=[pl.BlockSpec(memory_space=pltpu.SMEM), vmem],
        out_specs=(vmem,) * 5,
        compiler_params=pltpu.CompilerParams(vmem_limit_bytes=SMALL_VMEM),
        name="repack",
    )(column, back)


def weight_kernel(core_ref, *refs):
    grad_refs, line_refs, (out_ref, held_ref) = refs[:4], refs[4:8], refs[8:]
    core = core_ref[0]
    columns = pl.ds(pl.multiple_of(256 * core_ref[1], 256), 256)

    @pl.when(pl.program_id(0) == 0)
    def _():
        for shift in range(4):
            for part in range(2):
                first = (2 * shift + part) * SPAN
                held_ref[first : first + SPAN, :] = grad_refs[shift][
                    jnp.bitwise_xor(core, part), :, columns
                ]

    rows = jnp.concatenate([ref[...].reshape(2 * SPAN, D // 4) for ref in line_refs], axis=0)
    result = lax.dot_general(
        rows, held_ref[...], (((0,), (0,)), ((), ())), preferred_element_type=jnp.float32
    )
    out_ref[...] = result.astype(jnp.bfloat16).reshape(4, 64, 256)


def weight_terms(core, grads, lines):
    shape = jax.ShapeDtypeStruct((RANKS, 64, 256), jnp.bfloat16)
    grad_spec = pl.BlockSpec((2, SPAN, HQ), lambda j, core: (0, 0, 0))
    line_spec = pl.BlockSpec((2, SPAN, D // 4), lambda j, core: (0, 0, j))
    out_spec = pl.BlockSpec((4, 64, 256), lambda j, core: (j, 0, 0))
    return pl.pallas_call(
        weight_kernel,
        out_shape=shape,
        grid_spec=pltpu.PrefetchScalarGridSpec(
            num_scalar_prefetch=1,
            grid=(4,),
            in_specs=[
                *[grad_spec] * 4,
                *[line_spec] * 4,
            ],
            out_specs=out_spec,
            scratch_shapes=[pltpu.VMEM((8 * SPAN, 256), jnp.bfloat16)],
        ),
        compiler_params=pltpu.CompilerParams(vmem_limit_bytes=SMALL_VMEM),
        cost_estimate=pl.CostEstimate(
            flops=2_000_000_000, bytes_accessed=3 * 1024 * 1024, transcendentals=0
        ),
        name="weight_terms",
    )(core, *grads, *lines)


def place_kernel(column_ref, *refs):
    out_ref = refs[4]
    for shift in range(4):
        out_ref[jnp.bitwise_and(column_ref[0] + 4 - shift, 3)] = refs[shift][...]


def place_weights(column, parts):
    vmem = pl.BlockSpec(memory_space=pltpu.VMEM)
    return pl.pallas_call(
        place_kernel,
        out_shape=jax.ShapeDtypeStruct((4, 64, HQ), jnp.bfloat16),
        in_specs=[pl.BlockSpec(memory_space=pltpu.SMEM), vmem, vmem, vmem, vmem],
        out_specs=vmem,
        compiler_params=pltpu.CompilerParams(vmem_limit_bytes=SMALL_VMEM),
        name="place_weights",
    )(column, *parts)


def output_kernel(place_ref, grads_ref, arrived_ref, weights_ref, out_ref, input_grad_ref, held_ref):
    core, odd = place_ref[0], place_ref[1]

    @pl.when(pl.program_id(0) == 0)
    def _():
        for block in range(2):
            mine = jnp.bitwise_xor(odd, block) == core
            for number in range(4):
                held_ref[number, SPAN * block : SPAN * block + SPAN, :] = jnp.where(
                    mine,
                    grads_ref[number, 0].astype(jnp.float32),
                    arrived_ref[number].astype(jnp.float32),
                ).astype(jnp.bfloat16)

    def product(number):
        return lax.dot_general(
            held_ref[number], weights_ref[number], (((1,), (1,)), ((), ())),
            preferred_element_type=jnp.float32,
        )

    out_ref[...] = product(3).astype(jnp.bfloat16).reshape(2, SPAN, D // 4)
    input_grad = product(0) + product(1) + product(2)
    input_grad_ref[...] = input_grad.astype(jnp.bfloat16).reshape(2, SPAN, D // 4)


def outputs(place, grads, arrived, weights):
    shape = jax.ShapeDtypeStruct((2, SPAN, D), jnp.bfloat16)
    out_spec = pl.BlockSpec((2, SPAN, D // 4), lambda j, place: (0, 0, j))
    return pl.pallas_call(
        output_kernel,
        out_shape=(shape, shape),
        grid_spec=pltpu.PrefetchScalarGridSpec(
            num_scalar_prefetch=1,
            grid=(4,),
            in_specs=[
                pl.BlockSpec((4, 1, SPAN, HQ), lambda j, place: (0, place[0], 0, 0)),
                pl.BlockSpec((4, SPAN, HQ), lambda j, place: (0, 0, 0)),
                pl.BlockSpec((4, D // 4, HQ), lambda j, place: (0, j, 0)),
            ],
            out_specs=(out_spec, out_spec),
            scratch_shapes=[pltpu.VMEM((4, 2 * SPAN, HQ), jnp.bfloat16)],
        ),
        compiler_params=pltpu.CompilerParams(vmem_limit_bytes=SMALL_VMEM),
        cost_estimate=pl.CostEstimate(
            flops=8 * 2 * SPAN * D * HQ, bytes_accessed=7 * 1024 * 1024, transcendentals=0
        ),
        name="outputs",
    )(place, grads, arrived, weights)


def per_device(tokens, sweep_tiles, weights, cotangent):
    core = lax.axis_index("dp") % 2
    column = lax.axis_index("dp") // 4
    rank = lax.axis_index("ctx")
    odd = rank % 2
    block = jnp.bitwise_xor(core, odd)

    rows = tokens.reshape(2, SPAN, D)
    upstream = cotangent.reshape(2, SPAN, D)
    other_tiles = lax.ppermute(sweep_tiles, "dp", CORE_SWAP)
    core_number = core.astype(jnp.int32).reshape(1)
    packed, give = project(
        jnp.stack([core, block]).astype(jnp.int32), rows, upstream, weights
    )
    given = lax.ppermute(give, "dp", CORE_SWAP)
    packed = lax.dynamic_update_index_in_dim(packed, given, 1 - core, 1)

    def chosen(x, number):
        return lax.dynamic_index_in_dim(x, number, 0, keepdims=False)

    arrived = lax.ppermute(
        jnp.stack([chosen(x, 1 - block) for x in (rows, upstream)]), "dp", CORE_SWAP
    )
    own_line = [
        jnp.stack([chosen(x, block), arrived[kind]]) for kind, x in enumerate((rows, upstream))
    ]
    packed, other_tiles = lax.optimization_barrier((packed, other_tiles))
    packed = packed.reshape(RANKS, 2 * SPAN, 128)
    line, *lines = (
        jnp.where((column + shift) % 4 == 3, own_line[1], own_line[0]) for shift in range(4)
    )
    near, far, back_near = (
        lax.ppermute(rows, "dp", shift) for rows, shift in zip(lines, X_SHIFTS)
    )
    own = lax.all_to_all(packed, "ctx", 0, 0)
    own, near, back_near = lax.optimization_barrier((own, near, back_near))
    other_keys = lax.ppermute(own[:, SPAN:], "dp", CORE_SWAP)
    tiles = jnp.where(odd == core, sweep_tiles, other_tiles).reshape(-1)
    query_part, own_grad, other_grad = attend(core_number, tiles, own, other_keys)
    arrived = lax.ppermute(other_grad, "dp", CORE_SWAP)
    key_part = (own_grad + arrived.astype(jnp.float32)).astype(jnp.bfloat16)
    back = lax.all_to_all(jnp.concatenate([query_part, key_part], axis=1), "ctx", 0, 0)
    grads, *pieces = repack(
        column.astype(jnp.int32).reshape(1), back.reshape(HEADS, 2, 2 * SPAN, 128)
    )
    pieces, far = lax.optimization_barrier((pieces, far))
    pieces = [pieces[0]] + [lax.ppermute(x, "dp", y) for x, y in zip(pieces[1:], X_SHIFTS)]
    lines = (line, near, far, back_near)
    give, keep = (
        weight_terms(jnp.stack([core, half]).astype(jnp.int32), pieces, lines)
        for half in (1 - core, core)
    )
    given = lax.ppermute(give, "dp", CORE_SWAP)
    terms = (keep.astype(jnp.float32) + given.astype(jnp.float32)).astype(jnp.bfloat16)
    terms, own_grads = lax.optimization_barrier((terms, grads))
    terms = lax.all_to_all(terms, "ctx", 0, 0)
    swapped = lax.ppermute(
        lax.dynamic_index_in_dim(grads, 1 - core, 1, keepdims=False), "dp", CORE_SWAP
    )
    place = jnp.stack([core, odd]).astype(jnp.int32)
    attn_out, input_grad = outputs(place, own_grads, swapped, weights)
    terms, attn_out, input_grad = lax.optimization_barrier((terms, attn_out, input_grad))
    rows = lax.reduce_precision(jnp.sum(terms.astype(jnp.float32), axis=0), 8, 7)
    other_rows = lax.ppermute(rows.astype(jnp.bfloat16), "dp", Z_SWAP)
    factor = float(16 * RANKS * 2 * SPAN) ** -0.5
    total = ((rows + other_rows.astype(jnp.float32)) * factor).astype(jnp.bfloat16)
    other_total = lax.ppermute(total, "dp", CORE_SWAP)
    first = core == 0
    part = jnp.concatenate(
        [jnp.where(first, total, other_total), jnp.where(first, other_total, total)], axis=1
    )
    parts = [part] + [lax.ppermute(part, "dp", shift) for shift in X_SHIFTS]
    weight_grads = place_weights(column.astype(jnp.int32).reshape(1), parts)
    return (attn_out.reshape(tokens.shape), input_grad.reshape(tokens.shape), weight_grads)


def solution(mesh):
    placed = (
        P("dp", "ctx", None, None, None),
        P("dp", None),
        P(),
        P("dp", "ctx", None, None, None),
    )
    return jax.shard_map(
        per_device,
        mesh=mesh,
        in_specs=placed,
        out_specs=(
            P("dp", "ctx", None, None, None),
            P("dp", "ctx", None, None, None),
            P(None, "ctx", None),
        ),
        check_vma=False,
    )
```
